32 devices in a mesh: lat: 2 (over core), lon: 16 (over z, y, x).
Axes of the slice: x: 2, y: 2, z: 4, core: 2. Of those that a mesh axis runs over, the one named last changes fastest.
Arguments:
- forcing: bfloat16 [16, 32, 2048], P(None, 'lat', 'lon'), may hold values from -6 to 6
- hidden: bfloat16 [64, 32, 2048], P(None, 'lat', 'lon'), may hold values from -3 to 3
- cell: bfloat16 [64, 32, 2048], P(None, 'lat', 'lon'), may hold values from -6 to 6
- grad_hidden: bfloat16 [64, 32, 2048], P(None, 'lat', 'lon'), may hold values from -6 to 6
- grad_cell: bfloat16 [64, 32, 2048], P(None, 'lat', 'lon'), may hold values from -6 to 6
- wet_mask: int32 [2, 128], P('lat'), may hold values from 0 to 1
- tile_owner: int32 [2, 128], P('lat'), may hold values from 0 to 15, as said below
- w_gates: bfloat16 [256, 720], replicated, may hold values from -0.21875 to 0.21875
- b_gates: float32 [256], replicated, may hold values from -3 to 3
Outputs:
- hidden_next: bfloat16 [64, 32, 2048], P(None, 'lat', 'lon')
- cell_next: float32 [128, 64, 256], P(('lat', 'lon'))
- hidden_grad: float32 [64, 32, 2048], P(None, 'lat', 'lon')
- cell_grad: float32 [64, 32, 2048], P(None, 'lat', 'lon')
- weight_grad: float32 [256, 720], replicated
- bias_grad: float32 [256], replicated
The draws below stay inside these ranges and needn't reach their ends.
Inputs may be any that keep to these rules, and one draw needn't show every extreme that they name: Within each group of 1 tile rows, tile_owner gives every longitude index exactly 4 wet tiles, and gives the wet tiles of one longitude block of 8 tile columns at most 1 to any one index; both bounds are reached in every draw, and some block is wet throughout. Dry tiles carry an owner too.
All inputs are finite; a program needn't handle non-finite values.
Results may differ from the reference program's by a relative error of at most 0.0033.
Values may be sent and summed in bfloat16 or wider, within the bound.
No kernel may reach another device: no remote copies, remote signals or barrier semaphores. Data moves between devices by JAX's collectives and lax.ppermute only.
A program may use at most 64 MiB of HBM per device.

```python
import jax
import jax.numpy as jnp
from jax import lax

TILE = 16
INP = 16
HID = 64
TLAT_DEV = 1
TLON_DEV = 8
GATES = 256
CH = 80
TD = 8
CAP = 4
NTLAT = 2
NTLON = 128
NLAT = 32
NLON = 2048
WORK = 128
N_LAT = 2
N_LON = 16


def tile_layout(key):
    groups = NTLAT // TLAT_DEV
    device_total = NTLON // TLON_DEV
    per_dev = TLAT_DEV * TLON_DEV
    length_count = device_total * per_dev
    wet_total = CAP * device_total

    def one_group(cluster_key):
        boost_key, jitter_key, shuffle_key, offset_key, landmask_key = jax.random.split(cluster_key, 5)
        device_boost = jax.random.randint(boost_key, (device_total,), 0, 4 * length_count)
        unique_owners = device_boost * device_total + jnp.arange(device_total, dtype=jnp.int32)
        best_device = lax.top_k(unique_owners, 1)[1][0]
        device_boost = device_boost + jnp.where(jnp.arange(device_total, dtype=jnp.int32) == best_device, 100 * length_count, 0)
        tile_jitter = jax.random.randint(jitter_key, (device_total, per_dev), 0, 2 * length_count)
        tile_rating = ((tile_jitter + device_boost[:, None]) * length_count).reshape(length_count) + jnp.arange(length_count, dtype=jnp.int32)
        chosen = lax.top_k(tile_rating, wet_total)[1]
        wet_flag = jnp.zeros((length_count,), jnp.int32).at[chosen].set(1)
        wet_rank = jnp.cumsum(wet_flag) - 1
        labels = jax.random.permutation(shuffle_key, device_total).astype(jnp.int32)
        label_shift = jax.random.randint(offset_key, (), 0, device_total)
        wet_owner = labels[(wet_rank + label_shift) % device_total]
        dry_owner = jax.random.randint(landmask_key, (length_count,), 0, device_total)
        owner_flag = jnp.where(wet_flag > 0, wet_owner, dry_owner).astype(jnp.int32)
        return (wet_flag, owner_flag)
    group_keys = jax.random.split(jax.random.fold_in(key, 11), groups)
    wet_flag, owner_flag = jax.vmap(one_group)(group_keys)

    def to_grid(values):
        return values.reshape(groups, device_total, TLAT_DEV, TLON_DEV).transpose(0, 2, 1, 3).reshape(NTLAT, NTLON)
    return (to_grid(wet_flag), to_grid(owner_flag))


def draw_wet_mask(key, part):
    return tile_layout(key)[0]


def draw_tile_owner(key, part):
    return tile_layout(key)[1]


def block_scale(stream_key, extent, cuts, low, top_value):
    factor_of, own = 1.0, jax.random.fold_in(stream_key, 6)
    for dim, parts in cuts:
        steps = jnp.exp(jax.random.uniform(jax.random.fold_in(own, dim), (parts,), jnp.float32, low / len(cuts), top_value / len(cuts)))
        factor_of = factor_of * jnp.repeat(steps, extent[dim] // parts).reshape([-1 if axis == dim else 1 for axis in range(len(extent))])
    return factor_of


def bell_draw(rng, shape, scale, most, cuts=(), kind=jnp.bfloat16):
    gain = block_scale(rng, shape, cuts, -0.22, 0.18) if cuts else 1.0
    entries = jax.random.normal(rng, shape, jnp.float32) * scale * gain
    return jnp.minimum(jnp.maximum(entries, -most), most).astype(kind)


def setup_inputs(seed: int = 0) -> dict:
    key_of = jax.random.split(jax.random.key(seed), 10)
    return {
        "forcing": bell_draw(key_of[0], (INP, NLAT, NLON), 1.0, 6.0, ((1, 2), (2, 16))),
        "hidden": bell_draw(key_of[1], (HID, NLAT, NLON), 0.5, 3.0, ((1, 2), (2, 16))),
        "cell": bell_draw(key_of[2], (HID, NLAT, NLON), 1.0, 6.0, ((1, 2), (2, 16))),
        "grad_hidden": bell_draw(key_of[3], (HID, NLAT, NLON), 1.0, 6.0, ((1, 2), (2, 16))),
        "grad_cell": bell_draw(key_of[4], (HID, NLAT, NLON), 1.0, 6.0, ((1, 2), (2, 16))),
        "wet_mask": draw_wet_mask(jax.random.fold_in(key_of[9], 71), 0),
        "tile_owner": draw_tile_owner(jax.random.fold_in(key_of[9], 71), 0),
        "w_gates": bell_draw(key_of[7], (GATES, 9 * CH), (9 * CH) ** -0.5, 0.21875),
        "b_gates": bell_draw(key_of[8], (GATES,), 0.5, 3.0, (), jnp.float32),
    }


def last_pad(values_in, pad_front, pad_back):
    widths = [(0, 0)] * (values_in.ndim - 1) + [(pad_front, pad_back)]
    return jnp.pad(values_in, widths)

def fold_edges(values_in):
    tile_count = values_in.shape[-2]
    inner_size = values_in.shape[-1] - 2
    leading = values_in.shape[:-2]
    flat_shape = leading + (tile_count * inner_size,)
    middle = values_in[..., 1:inner_size + 1].reshape(flat_shape)
    zeros_left = jnp.zeros(leading + (tile_count, inner_size - 1), values_in.dtype)
    left_edge = jnp.concatenate([values_in[..., 0:1], zeros_left], -1).reshape(flat_shape)
    zeros_one = jnp.zeros(leading + (tile_count, 1), values_in.dtype)
    zeros_rest = jnp.zeros(leading + (tile_count, inner_size - 2), values_in.dtype)
    right_edge = jnp.concatenate([zeros_one, values_in[..., inner_size + 1:inner_size + 2], zeros_rest], -1).reshape(flat_shape)
    full_size = tile_count * inner_size + 2
    return last_pad(middle, 1, 1) + last_pad(left_edge, 0, 2) + last_pad(right_edge, inner_size, 0)[..., :full_size]

def lstm_terms(pre_in, pre_forget, pre_out, pre_cand, cell_in, hidden_cot, cell_cot, live_cells):
    gate_in = jax.nn.sigmoid(pre_in)
    gate_forget = jax.nn.sigmoid(pre_forget)
    gate_out = jax.nn.sigmoid(pre_out)
    candidate = jnp.tanh(pre_cand)
    cell_new = gate_forget * cell_in + gate_in * candidate
    squash = jnp.tanh(cell_new)
    hidden_new = (live_cells * gate_out * squash).astype(jnp.bfloat16)
    back_h = live_cells * hidden_cot.astype(jnp.float32)
    back_c = live_cells * cell_cot.astype(jnp.float32) + back_h * gate_out * (1.0 - squash * squash)
    cell_back = back_c * gate_forget
    delta_parts = (back_c * candidate * gate_in * (1.0 - gate_in), back_c * cell_in * gate_forget * (1.0 - gate_forget), back_h * squash * gate_out * (1.0 - gate_out), back_c * gate_in * (1.0 - candidate * candidate))
    return (hidden_new, cell_new, cell_back, delta_parts)

def gate_block(slab_in, cell_blk, hidden_cot, cell_cot, live_row, w_gates, b_gates):
    channels = slab_in.shape[0]
    hid_count = cell_blk.shape[0]
    row_count = cell_blk.shape[1]
    lon_count = cell_blk.shape[2]
    cells = row_count * lon_count
    tap_list = []
    for row_off in range(3):
        for col_off in range(3):
            tap_list.append(slab_in[:, row_off:row_off + row_count, col_off:col_off + lon_count].reshape(channels, cells))
    patches = jnp.concatenate(tap_list, 0).astype(jnp.float32)
    weights = w_gates.astype(jnp.float32)
    pre_gates = jnp.dot(weights, patches, preferred_element_type=jnp.float32, precision=lax.Precision.HIGHEST) + b_gates[:, None]
    live_cells = jnp.tile(live_row, row_count)[None, :]
    hidden_new, cell_new, cell_back, delta_parts = lstm_terms(pre_gates[:hid_count], pre_gates[hid_count:2 * hid_count], pre_gates[2 * hid_count:3 * hid_count], pre_gates[3 * hid_count:], cell_blk.reshape(hid_count, cells).astype(jnp.float32), hidden_cot.reshape(hid_count, cells), cell_cot.reshape(hid_count, cells), live_cells)
    gate_delta = lax.optimization_barrier(jnp.concatenate(delta_parts, 0).astype(jnp.bfloat16)).astype(jnp.float32)
    weight_part = jnp.dot(gate_delta, patches.T, preferred_element_type=jnp.float32, precision=lax.Precision.HIGHEST)
    bias_part = lax.optimization_barrier(jnp.sum(gate_delta, 1))
    hid_weights = weights.reshape(weights.shape[0], 9, channels)[:, :, channels - hid_count:]
    spread = jnp.einsum('gth,gc->thc', hid_weights, gate_delta, precision=lax.Precision.HIGHEST)
    grad_pad = jnp.zeros((hid_count, row_count + 2, lon_count + 2), jnp.float32)
    for row_off in range(3):
        for col_off in range(3):
            placed = spread[row_off * 3 + col_off].reshape(hid_count, row_count, lon_count)
            grad_pad = grad_pad + jnp.pad(placed, ((0, 0), (row_off, 2 - row_off), (col_off, 2 - col_off)))
    shape_out = (hid_count, row_count, lon_count)
    return (hidden_new.reshape(shape_out), cell_new.reshape(shape_out), cell_back.reshape(shape_out), grad_pad, weight_part, bias_part)

def reference(forcing, hidden, cell, grad_hidden, grad_cell, wet_mask, tile_owner, w_gates, b_gates):
    fields = jnp.concatenate([forcing, hidden], 0)
    wrapped = jnp.concatenate([fields[:, :, -1:], fields, fields[:, :, :1]], 2)
    padded = jnp.pad(wrapped, ((0, 0), (1, 1), (0, 0)))
    live_rows = jnp.repeat(wet_mask.astype(jnp.float32), TILE, axis=1)

    def scan_step(carry, block_row):
        top_row = (block_row * TILE).astype(jnp.int32)
        slab_in = lax.dynamic_slice_in_dim(padded, top_row, TILE + 2, 1)
        cell_blk = lax.dynamic_slice_in_dim(cell, top_row, TILE, 1)
        hidden_cot = lax.dynamic_slice_in_dim(grad_hidden, top_row, TILE, 1)
        cell_cot = lax.dynamic_slice_in_dim(grad_cell, top_row, TILE, 1)
        live_row = live_rows[block_row]
        results = gate_block(slab_in, cell_blk, hidden_cot, cell_cot, live_row, w_gates, b_gates)
        return ((carry[0] + results[4], carry[1] + results[5]), results[:4])
    start_sums = (jnp.zeros((GATES, 9 * CH), jnp.float32), jnp.zeros((GATES,), jnp.float32))
    totals, stacked = lax.scan(scan_step, start_sums, jnp.arange(NTLAT, dtype=jnp.int32))
    hid_blocks, cell_blocks, back_blocks, pad_blocks = stacked

    def merge_rows(blocks):
        return jnp.moveaxis(blocks, 0, 1).reshape(HID, NLAT, NLON)
    hidden_next = merge_rows(hid_blocks)
    cell_grad = merge_rows(back_blocks)
    lon_fold = pad_blocks[..., 1:NLON + 1]
    lon_fold = lon_fold.at[..., NLON - 1].add(pad_blocks[..., 0])
    lon_fold = lon_fold.at[..., 0].add(pad_blocks[..., NLON + 1])
    lat_major = jnp.transpose(lon_fold, (1, 3, 0, 2))
    hidden_grad = jnp.transpose(fold_edges(lat_major)[..., 1:NLAT + 1], (0, 2, 1))
    scaling = 1.0 / jnp.sqrt(jnp.float32(WORK * TILE * TILE))
    weight_grad = totals[0] * scaling
    bias_grad = totals[1] * scaling
    cell_grid = merge_rows(cell_blocks)
    cell_tiles = cell_grid.reshape(HID, NTLAT, TILE, NTLON, TILE).transpose(1, 3, 0, 2, 4).reshape(NTLAT * NTLON, HID, TILE * TILE)
    wet_order = wet_mask.reshape(N_LAT, TLAT_DEV, N_LON, TLON_DEV).transpose(0, 2, 1, 3).reshape(N_LAT, N_LON * TD)
    owner_order = tile_owner.reshape(N_LAT, TLAT_DEV, N_LON, TLON_DEV).transpose(0, 2, 1, 3).reshape(N_LAT, N_LON * TD)
    owner_hits = ((wet_order[..., None] > 0) & (owner_order[..., None] == jnp.arange(N_LON, dtype=jnp.int32)[None, None, :])).astype(jnp.int32)
    before = jnp.cumsum(owner_hits, 1) - owner_hits
    owner_rank = lax.optimization_barrier(jnp.sum(before * owner_hits, -1))
    group_index = jnp.arange(N_LAT, dtype=jnp.int32)[:, None]
    target = jnp.where(wet_order > 0, (group_index * N_LON + owner_order) * CAP + owner_rank, WORK).astype(jnp.int32)
    target = target.reshape(N_LAT, N_LON, TLAT_DEV, TLON_DEV).transpose(0, 2, 1, 3).reshape(NTLAT * NTLON)
    cell_next = jnp.zeros((WORK + 1, HID, TILE * TILE), jnp.float32).at[target].set(cell_tiles)[:WORK]
    return (hidden_next, cell_next, hidden_grad, cell_grad, weight_grad, bias_grad)
```

```python
import math

import jax
import jax.numpy as jnp
from jax import lax
from jax.experimental import pallas as pl
from jax.experimental.pallas import tpu as pltpu
from jax.sharding import PartitionSpec as P

TILE = 16
F32 = jnp.float32
BF16 = jnp.bfloat16
LIMIT = 48 * 1024 * 1024
SMEM = pl.BlockSpec(memory_space=pltpu.SMEM)
VMEM = pl.BlockSpec(memory_space=pltpu.VMEM)


def call(kernel, outs, operands, scalars=0, scratch=(), flops=0, moved=0):
    return pl.pallas_call(
        kernel,
        out_shape=outs,
        in_specs=[SMEM] * scalars + [VMEM] * (len(operands) - scalars),
        out_specs=jax.tree.map(lambda _: VMEM, outs),
        scratch_shapes=list(scratch),
        compiler_params=pltpu.CompilerParams(vmem_limit_bytes=LIMIT),
        cost_estimate=pl.CostEstimate(flops=flops, bytes_accessed=moved, transcendentals=0),
    )(*operands)


def lane_index(shape):
    return lax.broadcasted_iota(jnp.int32, shape, 1)


def sigmoid(values):
    return 0.5 * jnp.tanh(0.5 * values) + 0.5


def edges_kernel(place_ref, forcing_ref, hidden_ref, flat_ref, *rest):
    row_refs, (left_ref, right_ref, wide_ref) = rest[:-3], rest[-3:]
    inp, rows, width = forcing_ref.shape
    channels = inp + hidden_ref.shape[0]
    wide_ref[: inp * rows] = forcing_ref[...].astype(F32).reshape(inp * rows, width)
    wide_ref[inp * rows :] = hidden_ref[...].astype(F32).reshape((channels - inp) * rows, width)
    lane = lane_index((channels, width))
    left = jnp.zeros((channels, width), F32)
    right = jnp.zeros((channels, width), F32)
    ends = []
    for row in range(rows):
        slab = wide_ref[pl.ds(row, channels, stride=rows), :]
        flat_ref[:, row * width : (row + 1) * width] = slab.astype(BF16)
        left = jnp.where(lane == row, slab[:, :1], left)
        right = jnp.where(lane == row, slab[:, width - 1 :], right)
        if row in (0, rows - 1):
            ends.append(slab)
    left_ref[...] = left.astype(BF16)
    right_ref[...] = right.astype(BF16)
    if len(row_refs) == 1:
        row_refs[0][...] = jnp.where(place_ref[0] == 0, ends[-1], ends[0]).astype(BF16)
    else:
        row_refs[0][...] = ends[0].astype(BF16)
        row_refs[1][...] = ends[-1].astype(BF16)


def flatten_kernel(cell_ref, hcot_ref, ccot_ref, w_ref, cell_out, hcot_out, ccot_out, wt_ref, wide_ref):
    hid, rows, width = cell_ref.shape
    for source, target in ((cell_ref, cell_out), (hcot_ref, hcot_out), (ccot_ref, ccot_out)):
        wide_ref[...] = source[...].astype(F32).reshape(hid * rows, width)
        for row in range(rows):
            target[:, row * width : (row + 1) * width] = wide_ref[
                pl.ds(row, hid, stride=rows), :
            ].astype(BF16)
    wt_ref[...] = w_ref[...].astype(F32).T.astype(BF16)


def step_kernel(
    place_ref,
    wet_ref,
    owner_ref,
    flat_ref,
    up_ref,
    down_ref,
    up_left_ref,
    up_right_ref,
    down_left_ref,
    down_right_ref,
    left_ref,
    right_ref,
    cell_ref,
    hcot_ref,
    ccot_ref,
    w_ref,
    b_ref,
    hidden_next_ref,
    cell_grad_ref,
    send_ref,
    weight_ref,
    delta_ref,
    taps_ref,
    wide_ref,
    tiles_ref,
):
    channels = flat_ref.shape[0]
    hid = cell_ref.shape[0]
    gates = w_ref.shape[0]
    width = up_ref.shape[1]
    rows = flat_ref.shape[1] // width
    tile_cols = width // TILE
    span = 3 * channels
    first_tile = place_ref[1] * tile_cols
    lane = lane_index((channels, width))

    def put(row, slab, before, after):
        lanes = slice(row * width, (row + 1) * width)
        shifted = jnp.where(lane == 0, before, pltpu.roll(slab, 1, 1))
        taps_ref[0:channels, lanes] = shifted.astype(BF16)
        taps_ref[channels : 2 * channels, lanes] = slab.astype(BF16)
        shifted = jnp.where(lane == width - 1, after, pltpu.roll(slab, width - 1, 1))
        taps_ref[2 * channels : span, lanes] = shifted.astype(BF16)

    for row, flag, refs in (
        (0, place_ref[2], (up_ref, up_left_ref, up_right_ref)),
        (rows + 1, place_ref[3], (down_ref, down_left_ref, down_right_ref)),
    ):
        slab, before, after = [
            jnp.where(flag == 1, ref[...].astype(F32), 0.0) for ref in refs
        ]
        put(row, slab, before[:, width - 1 :], after[:, :1])
    left = left_ref[...].astype(F32)
    right = right_ref[...].astype(F32)
    for row in range(rows):
        slab = flat_ref[:, row * width : (row + 1) * width].astype(F32)
        put(row + 1, slab, left[:, row : row + 1], right[:, row : row + 1])
    extra = taps_ref.shape[0] - span
    ones = lax.broadcasted_iota(jnp.int32, (extra, taps_ref.shape[1]), 0) == 0
    taps_ref[span:] = jnp.where(ones, 1.0, 0.0).astype(BF16)

    live = jnp.zeros((1, width), F32)
    live_lane = lane_index((1, width)) // TILE
    for tile in range(tile_cols):
        wet = (wet_ref[0, first_tile + tile] > 0).astype(F32)
        live = jnp.where(live_lane == tile, wet, live)
    step = 2 if rows % 2 == 0 else 1
    chunk = step * width
    live = jnp.concatenate([live] * step, 1)
    blank = jnp.zeros((gates, 2 * width), BF16)
    delta_ref[:, : 2 * width] = blank
    delta_ref[:, (rows + 2) * width :] = blank
    bias = b_ref[...]
    group = 128 // TILE
    states = []
    for start in range(0, rows, step):
        pre = bias
        for row_off in range(3):
            low = (start + row_off) * width
            pre = pre + jnp.dot(
                w_ref[:, row_off * span : (row_off + 1) * span],
                taps_ref[:span, low : low + chunk],
                preferred_element_type=F32,
            )
        gate_in = sigmoid(pre[:hid])
        gate_forget = sigmoid(pre[hid : 2 * hid])
        gate_out = sigmoid(pre[2 * hid : 3 * hid])
        candidate = jnp.tanh(pre[3 * hid :])
        lanes = slice(start * width, start * width + chunk)
        cell_in = cell_ref[:, lanes].astype(F32)
        cell_new = gate_forget * cell_in + gate_in * candidate
        squash = jnp.tanh(cell_new)
        hidden_new = live * gate_out * squash
        back_h = live * hcot_ref[:, lanes].astype(F32)
        back_c = live * ccot_ref[:, lanes].astype(F32) + back_h * gate_out * (1.0 - squash * squash)
        cell_back = back_c * gate_forget
        carried = back_c * gate_in
        terms = (
            carried * candidate * (1.0 - gate_in),
            cell_back * cell_in * (1.0 - gate_forget),
            back_h * squash * gate_out * (1.0 - gate_out),
            carried * (1.0 - candidate * candidate),
        )
        low = (start + 2) * width
        for index, term in enumerate(terms):
            delta_ref[index * hid : (index + 1) * hid, low : low + chunk] = term.astype(BF16)
        for part in range(step):
            piece = slice(part * width, (part + 1) * width)
            wide_ref[pl.ds(start + part, hid, stride=rows), :] = hidden_new[:, piece]
            cell_grad_ref[pl.ds(start + part, hid, stride=rows), :] = cell_back[:, piece]
            states.append(cell_new[:, piece])
        if len(states) == group:
            block_of = lane_index((hid, width)) // TILE
            half = (start + step) // group - 1
            stride = group // 2
            while stride:
                upper = (block_of & stride) != 0
                mixed = list(states)
                for low_index in range(group):
                    if low_index & stride == 0:
                        first, second = states[low_index], states[low_index + stride]
                        mixed[low_index] = jnp.where(
                            upper, pltpu.roll(second, stride * TILE, 1), first
                        )
                        mixed[low_index + stride] = jnp.where(
                            upper, second, pltpu.roll(first, width - stride * TILE, 1)
                        )
                states = mixed
                stride //= 2
            for tile in range(tile_cols):
                tiles_ref[tile, :, half * 128 : (half + 1) * 128] = states[tile].astype(BF16)
            states = []
    hidden_next_ref[...] = wide_ref[...].reshape(hid, rows, width).astype(BF16)
    send_ref[...] = jnp.zeros(send_ref.shape, BF16)
    for tile in range(tile_cols):

        @pl.when(wet_ref[0, first_tile + tile] > 0)
        def _():
            send_ref[owner_ref[0, first_tile + tile]] = tiles_ref[tile]

    delta = delta_ref[:, 2 * width : (rows + 2) * width]
    lane_out = lane_index((gates, taps_ref.shape[0]))
    for row_off in range(3):
        part = lax.dot_general(
            delta,
            taps_ref[:, row_off * width : (row_off + rows) * width],
            (((1,), (1,)), ((), ())),
            preferred_element_type=F32,
        )
        if row_off == 1:
            rest = part - part.astype(BF16).astype(F32)
            part = jnp.where(lane_out == span, rest, part)
        base = row_off * taps_ref.shape[0]
        weight_ref[:, base : base + taps_ref.shape[0]] = part.astype(BF16)


def spread_kernel(place_ref, delta_ref, wt_ref, grad_ref, *rest):
    row_refs, (left_ref, right_ref, side_ref) = rest[:-3], rest[-3:]
    hid = grad_ref.shape[0]
    width = left_ref.shape[1]
    rows = grad_ref.shape[1] // width
    channels = wt_ref.shape[0] // 9
    total = [None] * 3
    for col_off in range(3):
        for row_off in range(3):
            first = (row_off * 3 + col_off + 1) * channels - hid
            low = (2 - row_off) * width
            term = jnp.dot(
                wt_ref[first : first + hid],
                delta_ref[:, low : low + (rows + 2) * width],
                preferred_element_type=F32,
            )
            total[col_off] = term if row_off == 0 else total[col_off] + term
        side_ref[col_off] = total[col_off]
    lane = lane_index((hid, width))
    left = jnp.zeros((hid, width), F32)
    right = jnp.zeros((hid, width), F32)
    ends = []
    for row in range(rows + 2):
        lanes = slice(row * width, (row + 1) * width)
        before = side_ref[0, :, lanes]
        after = side_ref[2, :, lanes]
        slab = (
            side_ref[1, :, lanes]
            + jnp.where(lane == width - 1, 0.0, pltpu.roll(before, width - 1, 1))
            + jnp.where(lane == 0, 0.0, pltpu.roll(after, 1, 1))
        )
        if row in (0, rows + 1):
            corners = jnp.where(lane == 0, before[:, :1], 0.0)
            corners = jnp.where(lane == width - 1, after[:, width - 1 :], corners)
            ends.append((slab, corners))
        else:
            grad_ref[:, (row - 1) * width : row * width] = slab
            left = jnp.where(lane == row - 1, before[:, :1], left)
            right = jnp.where(lane == row - 1, after[:, width - 1 :], right)
    left_ref[...] = left.astype(BF16)
    right_ref[...] = right.astype(BF16)
    if len(row_refs) == 2:
        for index in range(2):
            row_refs[index][...] = jnp.where(
                place_ref[0] == 0, ends[1][index], ends[0][index]
            ).astype(BF16)
    else:
        for end in range(2):
            for index in range(2):
                row_refs[2 * end + index][...] = ends[end][index].astype(BF16)


def fold_kernel(
    place_ref,
    grad_ref,
    up_ref,
    down_ref,
    up_left_ref,
    up_right_ref,
    down_left_ref,
    down_right_ref,
    left_ref,
    right_ref,
    out_ref,
):
    hid = grad_ref.shape[0]
    width = up_ref.shape[1]
    rows = grad_ref.shape[1] // width
    lane = lane_index((hid, width))
    left = left_ref[...].astype(F32)
    right = right_ref[...].astype(F32)
    ends = {}
    for row, flag, refs in (
        (0, place_ref[2], (up_ref, up_left_ref, up_right_ref)),
        (rows - 1, place_ref[3], (down_ref, down_left_ref, down_right_ref)),
    ):
        slab, before, after = [ref[...].astype(F32) for ref in refs]
        slab = slab + jnp.where(lane == 0, before[:, width - 1 :], 0.0)
        slab = slab + jnp.where(lane == width - 1, after[:, :1], 0.0)
        ends[row] = jnp.where(flag == 1, slab, 0.0)
    for row in range(rows):
        slab = grad_ref[:, row * width : (row + 1) * width]
        slab = slab + jnp.where(lane == 0, left[:, row : row + 1], 0.0)
        slab = slab + jnp.where(lane == width - 1, right[:, row : row + 1], 0.0)
        if row in ends:
            slab = slab + ends[row]
        out_ref[pl.ds(row, hid, stride=rows), :] = slab


def sum_kernel(parts_ref, out_ref):
    total = parts_ref[0].astype(F32)
    for index in range(1, parts_ref.shape[0]):
        total = total + parts_ref[index].astype(F32)
    out_ref[...] = total


def share_kernel(scaling, span, *refs):
    total = refs[0][...]
    for ref in refs[1:-1]:
        total = total + ref[...]
    total = total * scaling
    out_ref = refs[-1]
    third = total.shape[1] // 3
    lane = lane_index(total.shape)
    whole = total + pltpu.roll(total, 2 * third, 1)
    total = jnp.where(lane == span, whole, total)
    rest = whole - whole.astype(BF16).astype(F32)
    total = jnp.where(lane == third + span, pltpu.roll(rest, third, 1), total)
    for index in range(out_ref.shape[0]):
        out_ref[index] = total.astype(BF16)


def weights_kernel(span, parts_ref, weight_ref, bias_ref):
    third = parts_ref.shape[1] // 3
    for index in range(3):
        weight_ref[:, index * span : (index + 1) * span] = parts_ref[
            :, index * third : index * third + span
        ].astype(F32)
    first = span // 128 * 128
    both = parts_ref[:, first : first + 128].astype(F32)
    both = both + parts_ref[:, third + first : third + first + 128].astype(F32)
    bias_ref[...] = both.T[span - first : span - first + 1, :]


def tiles_kernel(work_ref, arrived_ref, out_ref):
    for index in range(out_ref.shape[0]):
        out_ref[index] = arrived_ref[work_ref[index]].astype(F32)


def moved(values, lat_step, lon_step, lat_devices, lon_devices):
    pairs = []
    for lat in range(lat_devices):
        for lon in range(lon_devices):
            to_lat = lat + lat_step
            if lat_step and lat_devices == 2:
                to_lat = 1 - lat
            if 0 <= to_lat < lat_devices:
                to = to_lat * lon_devices + (lon + lon_step) % lon_devices
                pairs.append((lat * lon_devices + lon, to))
    return lax.ppermute(values, ("lat", "lon"), pairs)


def exchange(ends, corners, left, right, lat_devices, lon_devices):
    def go(values, lat_step, lon_step):
        return moved(values, lat_step, lon_step, lat_devices, lon_devices)

    from_left, from_right = go(right, 0, 1), go(left, 0, -1)
    if lat_devices == 2:
        row = go(ends[0], 1, 0)
        row_left, row_right = go(corners[0], 1, 1), go(corners[0], 1, -1)
        return (row, row, row_left, row_right, row_left, row_right, from_left, from_right)
    return (
        go(ends[1], 1, 0),
        go(ends[0], -1, 0),
        go(corners[1], 1, 1),
        go(corners[1], 1, -1),
        go(corners[0], -1, 1),
        go(corners[0], -1, -1),
        from_left,
        from_right,
    )


def body(forcing, hidden, cell, grad_hidden, grad_cell, wet_mask, tile_owner, w_gates, b_gates):
    lat_index = lax.axis_index("lat")
    lon_index = lax.axis_index("lon")
    lat_devices = lax.axis_size("lat")
    lon_devices = lax.axis_size("lon")
    inp, rows, width = forcing.shape
    hid = hidden.shape[0]
    channels = inp + hid
    gates = w_gates.shape[0]
    span = 3 * channels
    third = (span + 128) // 128 * 128
    cells = rows * width
    tile_cols = width // TILE
    capacity = tile_cols // 2
    place = jnp.stack(
        [
            lat_index,
            lon_index,
            (lat_index > 0).astype(jnp.int32),
            (lat_index < lat_devices - 1).astype(jnp.int32),
        ]
    ).astype(jnp.int32)

    def shaped(*shape, dtype=BF16):
        return jax.ShapeDtypeStruct(shape, dtype)

    end_count = 1 if lat_devices == 2 else 2
    edges = call(
        edges_kernel,
        (shaped(channels, cells),) + (shaped(channels, width),) * (end_count + 2),
        (place, forcing, hidden),
        scalars=1,
        scratch=[pltpu.VMEM((channels * rows, width), F32)],
        moved=4 * channels * cells,
    )
    flat, ends, (left, right) = edges[0], edges[1:-2], edges[-2:]
    halo = exchange(ends, ends, left, right, lat_devices, lon_devices)
    cell_flat, hcot_flat, ccot_flat, w_turned = call(
        flatten_kernel,
        (shaped(hid, cells),) * 3 + (shaped(w_gates.shape[1], gates),),
        (cell, grad_hidden, grad_cell, w_gates),
        scratch=[pltpu.VMEM((hid * rows, width), F32)],
        moved=12 * hid * cells,
    )
    hidden_next, cell_grad, outgoing, weight_part, delta = call(
        step_kernel,
        (
            shaped(hid, rows, width),
            shaped(hid * rows, width, dtype=F32),
            shaped(lon_devices, hid, TILE * TILE),
            shaped(gates, 3 * third),
            shaped(gates, (rows + 4) * width),
        ),
        (place, wet_mask, tile_owner, flat, *halo)
        + (cell_flat, hcot_flat, ccot_flat, w_gates, b_gates.reshape(gates, 1)),
        scalars=3,
        scratch=[
            pltpu.VMEM((third, (rows + 2) * width), BF16),
            pltpu.VMEM((hid * rows, width), F32),
            pltpu.VMEM((tile_cols, hid, TILE * TILE), BF16),
        ],
        flops=4 * gates * 3 * span * cells,
        moved=16 * hid * cells,
    )
    share = gates // lon_devices
    parts = lax.all_to_all(
        weight_part.reshape(lon_devices, share, 3 * third), "lon", 0, 0, tiled=True
    )
    incoming = lax.all_to_all(outgoing, "lon", 0, 0, tiled=True)
    grad_parts = call(
        spread_kernel,
        (shaped(hid, cells, dtype=F32),) + (shaped(hid, width),) * (2 * end_count + 2),
        (place, delta, w_turned),
        scalars=1,
        scratch=[pltpu.VMEM((3, hid, (rows + 2) * width), F32)],
        flops=2 * gates * 9 * hid * cells,
        moved=8 * gates * cells,
    )
    grad_flat, grad_ends, grad_sides = grad_parts[0], grad_parts[1:-2], grad_parts[-2:]
    grad_halo = exchange(
        grad_ends[0::2], grad_ends[1::2], *grad_sides, lat_devices, lon_devices
    )
    hidden_grad = call(
        fold_kernel,
        shaped(hid * rows, width, dtype=F32),
        (place, grad_flat, *grad_halo),
        scalars=1,
        moved=8 * hid * cells,
    )
    summed = call(
        sum_kernel,
        shaped(share, 3 * third, dtype=F32),
        (parts,),
        moved=2 * gates * 3 * third,
    )
    scaling = 1.0 / math.sqrt(float(lat_devices * lon_devices * capacity * TILE * TILE))
    around = [summed]
    for _ in range(lat_devices - 1):
        pairs = [(i, (i + 1) % lat_devices) for i in range(lat_devices)]
        around.append(lax.ppermute(around[-1], "lat", pairs))
    shares = call(
        lambda *refs: share_kernel(scaling, span, *refs),
        shaped(lon_devices, share, 3 * third),
        tuple(around),
        moved=2 * gates * 3 * third,
    )
    gathered = lax.all_to_all(shares, "lon", 0, 0, tiled=True)
    weight_grad, bias_grad = call(
        lambda *refs: weights_kernel(span, *refs),
        (shaped(gates, 3 * span, dtype=F32), shaped(1, gates, dtype=F32)),
        (gathered.reshape(gates, 3 * third),),
        moved=6 * gates * 3 * third,
    )
    owned = (wet_mask > 0) & (tile_owner == lon_index)
    arrived = jnp.any(owned.reshape(lon_devices, tile_cols), 1)
    order = jnp.arange(lon_devices, dtype=jnp.int32)
    rank = jnp.sum((arrived[:, None] & (order[:, None] < order[None, :])).astype(jnp.int32), 0)
    placed = arrived[None, :] & (rank[None, :] == jnp.arange(capacity, dtype=jnp.int32)[:, None])
    work = jnp.sum(jnp.where(placed, order[None, :], 0), 1)
    cell_next = call(
        tiles_kernel,
        shaped(capacity, hid, TILE * TILE, dtype=F32),
        (work, incoming),
        scalars=1,
        moved=2 * lon_devices * hid * TILE * TILE,
    )
    return (
        hidden_next,
        cell_next,
        hidden_grad.reshape(hid, rows, width),
        cell_grad.reshape(hid, rows, width),
        weight_grad,
        bias_grad.reshape(gates),
    )


def solution(mesh):
    return jax.shard_map(
        body,
        mesh=mesh,
        in_specs=(
            P(None, "lat", "lon"),
            P(None, "lat", "lon"),
            P(None, "lat", "lon"),
            P(None, "lat", "lon"),
            P(None, "lat", "lon"),
            P("lat", None),
            P("lat", None),
            P(),
            P(),
        ),
        out_specs=(
            P(None, "lat", "lon"),
            P(("lat", "lon"), None, None),
            P(None, "lat", "lon"),
            P(None, "lat", "lon"),
            P(),
            P(),
        ),
        check_vma=False,
    )
```

```python
import math

import jax
import jax.numpy as jnp
from jax import lax
from jax.experimental import pallas as pl
from jax.experimental.pallas import tpu as pltpu
from jax.sharding import PartitionSpec as P

TILE = 16
F32 = jnp.float32
BF16 = jnp.bfloat16
LIMIT = 48 * 1024 * 1024
SMEM = pl.BlockSpec(memory_space=pltpu.SMEM)
VMEM = pl.BlockSpec(memory_space=pltpu.VMEM)


def call(kernel, outs, operands, scalars=0, scratch=(), flops=0, moved=0, after=()):
    count = len(operands)

    def run(*refs):
        kernel(*refs[:count], *refs[count + len(after) :])

    return pl.pallas_call(
        run,
        out_shape=outs,
        in_specs=[SMEM] * scalars
        + [VMEM] * (count - scalars)
        + [pl.BlockSpec(memory_space=pl.ANY)] * len(after),
        out_specs=jax.tree.map(lambda _: VMEM, outs),
        scratch_shapes=list(scratch),
        compiler_params=pltpu.CompilerParams(vmem_limit_bytes=LIMIT),
        cost_estimate=pl.CostEstimate(flops=flops, bytes_accessed=moved, transcendentals=0),
    )(*operands, *after)


def lane_index(shape):
    return lax.broadcasted_iota(jnp.int32, shape, 1)


def sigmoid(values):
    return 0.5 * jnp.tanh(0.5 * values) + 0.5


def edges_kernel(place_ref, forcing_ref, hidden_ref, flat_ref, *rest):
    row_refs, (left_ref, right_ref, wide_ref) = rest[:-3], rest[-3:]
    inp, rows, width = forcing_ref.shape
    channels = inp + hidden_ref.shape[0]
    wide_ref[: inp * rows] = forcing_ref[...].astype(F32).reshape(inp * rows, width)
    wide_ref[inp * rows :] = hidden_ref[...].astype(F32).reshape((channels - inp) * rows, width)
    lane = lane_index((channels, width))
    left = jnp.zeros((channels, width), F32)
    right = jnp.zeros((channels, width), F32)
    ends = []
    for row in range(rows):
        slab = wide_ref[pl.ds(row, channels, stride=rows), :]
        flat_ref[:, row * width : (row + 1) * width] = slab.astype(BF16)
        left = jnp.where(lane == row, slab[:, :1], left)
        right = jnp.where(lane == row, slab[:, width - 1 :], right)
        if row in (0, rows - 1):
            ends.append(slab)
    left_ref[...] = left.astype(BF16)
    right_ref[...] = right.astype(BF16)
    if len(row_refs) == 1:
        row_refs[0][...] = jnp.where(place_ref[0] == 0, ends[-1], ends[0]).astype(BF16)
    else:
        row_refs[0][...] = ends[0].astype(BF16)
        row_refs[1][...] = ends[-1].astype(BF16)


def flatten_kernel(
    cell_ref, hcot_ref, ccot_ref, wt_ref, b_ref, cell_out, hcot_out, ccot_out, w_ref, bias_ref, wide_ref
):
    hid, rows, width = cell_ref.shape
    gates = wt_ref.shape[1]
    span = wt_ref.shape[0] // 3
    third = w_ref.shape[1] // 3
    for source, target in ((cell_ref, cell_out), (hcot_ref, hcot_out), (ccot_ref, ccot_out)):
        wide_ref[...] = source[...].astype(F32).reshape(hid * rows, width)
        for row in range(rows):
            target[:, row * width : (row + 1) * width] = wide_ref[
                pl.ds(row, hid, stride=rows), :
            ].astype(BF16)
    blank = jnp.zeros((third - span, gates), F32)
    for index in range(3):
        block = wt_ref[index * span : (index + 1) * span].astype(F32)
        w_ref[:, index * third : (index + 1) * third] = (
            jnp.concatenate([block, blank], 0).T.astype(BF16)
        )
    bias_ref[...] = jnp.broadcast_to(b_ref[...], (bias_ref.shape[1], gates)).T


def step_kernel(
    place_ref,
    wet_ref,
    owner_ref,
    flat_ref,
    up_ref,
    down_ref,
    up_left_ref,
    up_right_ref,
    down_left_ref,
    down_right_ref,
    left_ref,
    right_ref,
    cell_ref,
    hcot_ref,
    ccot_ref,
    w_ref,
    b_ref,
    hidden_next_ref,
    cell_grad_ref,
    tiles_ref,
    *rest,
):
    weight_refs, (delta_ref, taps_ref, wide_ref) = rest[:-3], rest[-3:]
    channels = flat_ref.shape[0]
    hid = cell_ref.shape[0]
    gates = w_ref.shape[0]
    width = up_ref.shape[1]
    rows = flat_ref.shape[1] // width
    tile_cols = width // TILE
    span = 3 * channels
    first_tile = place_ref[1] * tile_cols
    lane = lane_index((channels, width))

    def put(row, slab, before, after):
        lanes = slice(row * width, (row + 1) * width)
        shifted = jnp.where(lane == 0, before, pltpu.roll(slab, 1, 1))
        taps_ref[0:channels, lanes] = shifted.astype(BF16)
        taps_ref[channels : 2 * channels, lanes] = slab.astype(BF16)
        shifted = jnp.where(lane == width - 1, after, pltpu.roll(slab, width - 1, 1))
        taps_ref[2 * channels : span, lanes] = shifted.astype(BF16)

    for row, flag, refs in (
        (0, place_ref[2], (up_ref, up_left_ref, up_right_ref)),
        (rows + 1, place_ref[3], (down_ref, down_left_ref, down_right_ref)),
    ):
        slab, before, after = [
            jnp.where(flag == 1, ref[...].astype(F32), 0.0) for ref in refs
        ]
        put(row, slab, before[:, width - 1 :], after[:, :1])
    left = left_ref[...].astype(F32)
    right = right_ref[...].astype(F32)
    for row in range(rows):
        slab = flat_ref[:, row * width : (row + 1) * width].astype(F32)
        put(row + 1, slab, left[:, row : row + 1], right[:, row : row + 1])
    extra = taps_ref.shape[0] - span
    ones = lax.broadcasted_iota(jnp.int32, (extra, taps_ref.shape[1]), 0) == 0
    taps_ref[span:] = jnp.where(ones, 1.0, 0.0).astype(BF16)

    live = jnp.zeros((1, width), F32)
    live_lane = lane_index((1, width)) // TILE
    for tile in range(tile_cols):
        wet = (wet_ref[0, first_tile + tile] > 0).astype(F32)
        live = jnp.where(live_lane == tile, wet, live)
    step = 2 if rows % 2 == 0 else 1
    chunk = step * width
    live = jnp.concatenate([live] * step, 1)
    third = w_ref.shape[1] // 3
    blank = jnp.zeros((gates, 2 * width), BF16)
    delta_ref[:, : 2 * width] = blank
    delta_ref[:, (rows + 2) * width :] = blank
    bias = jnp.concatenate([b_ref[...]] * step, 1)
    group = 128 // TILE
    states = []
    for start in range(0, rows, step):
        pre = bias
        for row_off in range(3):
            low = (start + row_off) * width
            pre = pre + jnp.dot(
                w_ref[:, row_off * third : (row_off + 1) * third],
                taps_ref[:, low : low + chunk],
                preferred_element_type=F32,
            )
        gate_in = sigmoid(pre[:hid])
        gate_forget = sigmoid(pre[hid : 2 * hid])
        gate_out = sigmoid(pre[2 * hid : 3 * hid])
        candidate = jnp.tanh(pre[3 * hid :])
        lanes = slice(start * width, start * width + chunk)
        cell_in = cell_ref[:, lanes].astype(F32)
        cell_new = gate_forget * cell_in + gate_in * candidate
        squash = jnp.tanh(cell_new)
        hidden_new = live * gate_out * squash
        back_h = live * hcot_ref[:, lanes].astype(F32)
        back_c = live * ccot_ref[:, lanes].astype(F32) + back_h * gate_out * (1.0 - squash * squash)
        cell_back = back_c * gate_forget
        carried = back_c * gate_in
        terms = (
            carried * candidate * (1.0 - gate_in),
            cell_back * cell_in * (1.0 - gate_forget),
            back_h * squash * gate_out * (1.0 - gate_out),
            carried * (1.0 - candidate * candidate),
        )
        low = (start + 2) * width
        for index, term in enumerate(terms):
            delta_ref[index * hid : (index + 1) * hid, low : low + chunk] = term.astype(BF16)
        for part in range(step):
            piece = slice(part * width, (part + 1) * width)
            wide_ref[pl.ds(start + part, hid, stride=rows), :] = hidden_new[:, piece]
            cell_grad_ref[pl.ds(start + part, hid, stride=rows), :] = cell_back[:, piece]
            states.append(cell_new[:, piece])
        if len(states) == group:
            block_of = lane_index((hid, width)) // TILE
            half = (start + step) // group - 1
            stride = group // 2
            while stride:
                upper = (block_of & stride) != 0
                mixed = list(states)
                for low_index in range(group):
                    if low_index & stride == 0:
                        first, second = states[low_index], states[low_index + stride]
                        mixed[low_index] = jnp.where(
                            upper, pltpu.roll(second, stride * TILE, 1), first
                        )
                        mixed[low_index + stride] = jnp.where(
                            upper, second, pltpu.roll(first, width - stride * TILE, 1)
                        )
                states = mixed
                stride //= 2
            for tile in range(tile_cols):
                tiles_ref[tile, :, half * 128 : (half + 1) * 128] = states[tile].astype(BF16)
            states = []
    hidden_next_ref[...] = wide_ref[...].reshape(hid, rows, width).astype(BF16)
    delta = delta_ref[:, 2 * width : (rows + 2) * width]
    for row_off in range(3):
        part = lax.dot_general(
            taps_ref[:, row_off * width : (row_off + rows) * width],
            delta,
            (((1,), (1,)), ((), ())),
            preferred_element_type=F32,
        )
        place = slice(row_off * third, (row_off + 1) * third)
        if len(weight_refs) == 1:
            weight_refs[0][place] = part
        else:
            low, high = part[:, : gates // 2], part[:, gates // 2 :]
            weight_refs[0][place] = jnp.where(place_ref[0] == 0, low, high)
            weight_refs[1][place] = jnp.where(place_ref[0] == 0, high, low)


def spread_kernel(place_ref, delta_ref, wt_ref, grad_ref, *rest):
    row_refs, (left_ref, right_ref, side_ref) = rest[:-3], rest[-3:]
    hid = grad_ref.shape[0]
    width = left_ref.shape[1]
    rows = grad_ref.shape[1] // width
    channels = wt_ref.shape[0] // 9
    total = [None] * 3
    for col_off in range(3):
        for row_off in range(3):
            first = (row_off * 3 + col_off + 1) * channels - hid
            low = (2 - row_off) * width
            term = jnp.dot(
                wt_ref[first : first + hid],
                delta_ref[:, low : low + (rows + 2) * width],
                preferred_element_type=F32,
            )
            total[col_off] = term if row_off == 0 else total[col_off] + term
        side_ref[col_off] = total[col_off]
    lane = lane_index((hid, width))
    left = jnp.zeros((hid, width), F32)
    right = jnp.zeros((hid, width), F32)
    ends = []
    for row in range(rows + 2):
        lanes = slice(row * width, (row + 1) * width)
        before = side_ref[0, :, lanes]
        after = side_ref[2, :, lanes]
        slab = (
            side_ref[1, :, lanes]
            + jnp.where(lane == width - 1, 0.0, pltpu.roll(before, width - 1, 1))
            + jnp.where(lane == 0, 0.0, pltpu.roll(after, 1, 1))
        )
        if row in (0, rows + 1):
            corners = jnp.where(lane == 0, before[:, :1], 0.0)
            corners = jnp.where(lane == width - 1, after[:, width - 1 :], corners)
            ends.append((slab, corners))
        else:
            grad_ref[:, (row - 1) * width : row * width] = slab
            left = jnp.where(lane == row - 1, before[:, :1], left)
            right = jnp.where(lane == row - 1, after[:, width - 1 :], right)
    left_ref[...] = left.astype(BF16)
    right_ref[...] = right.astype(BF16)
    if len(row_refs) == 2:
        for index in range(2):
            row_refs[index][...] = jnp.where(
                place_ref[0] == 0, ends[1][index], ends[0][index]
            ).astype(BF16)
    else:
        for end in range(2):
            for index in range(2):
                row_refs[2 * end + index][...] = ends[end][index].astype(BF16)


def fold_kernel(
    place_ref,
    grad_ref,
    up_ref,
    down_ref,
    up_left_ref,
    up_right_ref,
    down_left_ref,
    down_right_ref,
    left_ref,
    right_ref,
    out_ref,
):
    hid = grad_ref.shape[0]
    width = up_ref.shape[1]
    rows = grad_ref.shape[1] // width
    lane = lane_index((hid, width))
    left = left_ref[...].astype(F32)
    right = right_ref[...].astype(F32)
    ends = {}
    for row, flag, refs in (
        (0, place_ref[2], (up_ref, up_left_ref, up_right_ref)),
        (rows - 1, place_ref[3], (down_ref, down_left_ref, down_right_ref)),
    ):
        slab, before, after = [ref[...].astype(F32) for ref in refs]
        slab = slab + jnp.where(lane == 0, before[:, width - 1 :], 0.0)
        slab = slab + jnp.where(lane == width - 1, after[:, :1], 0.0)
        ends[row] = jnp.where(flag == 1, slab, 0.0)
    for row in range(rows):
        slab = grad_ref[:, row * width : (row + 1) * width]
        slab = slab + jnp.where(lane == 0, left[:, row : row + 1], 0.0)
        slab = slab + jnp.where(lane == width - 1, right[:, row : row + 1], 0.0)
        if row in ends:
            slab = slab + ends[row]
        out_ref[pl.ds(row, hid, stride=rows), :] = slab


def split_bias(block, row):
    index = lax.broadcasted_iota(jnp.int32, block.shape, 0)
    rest = pltpu.roll(block - block.astype(BF16).astype(F32), 1, 0)
    return jnp.where(index == row + 1, rest, block)


def pack_kernel(span, place_ref, wet_ref, owner_ref, tiles_ref, *refs):
    out_ref = refs[-1]
    tile_cols, hid, cells = tiles_ref.shape
    lanes = out_ref.shape[2]
    pieces = cells // 128
    state_rows = hid * pieces * 128 // lanes
    slots = out_ref.shape[0]
    third = refs[0].shape[0] // 3
    out_ref[:, :state_rows] = jnp.zeros((slots, state_rows, lanes), BF16)
    for tile in range(tile_cols):
        index = place_ref[1] * tile_cols + tile

        @pl.when(wet_ref[0, index] > 0)
        def _():
            for piece in range(cells // lanes):
                out_ref[owner_ref[0, index], piece * hid : (piece + 1) * hid] = tiles_ref[
                    tile, :, piece * lanes : (piece + 1) * lanes
                ]

    total = refs[0][...]
    for ref in refs[1:-1]:
        total = total + ref[...]
    total = jnp.concatenate([split_bias(total[:third], span), total[third:]], 0)
    share = total.shape[0] // slots
    for slot in range(slots):
        out_ref[slot, state_rows:] = total[slot * share : (slot + 1) * share].astype(BF16)


def sum_kernel(scaling, state_rows, parts_ref, out_ref):
    total = parts_ref[0, state_rows:].astype(F32)
    for index in range(1, parts_ref.shape[0]):
        total = total + parts_ref[index, state_rows:].astype(F32)
    out_ref[...] = total * scaling


def share_kernel(span, place_ref, *refs):
    *parts, out_ref = refs
    lanes = parts[0].shape[1]
    share = out_ref.shape[1]
    row = span % share
    for side in range(len(parts)):
        total = parts[0][...]
        if len(parts) == 2:
            total = jnp.where(place_ref[0] == side, total, parts[1][...])
        index = lax.broadcasted_iota(jnp.int32, total.shape, 0)
        whole = jnp.where(index == row, total + pltpu.roll(total, share - 1, 0), total)
        total = jnp.where(place_ref[1] == span // share, split_bias(whole, row), total)
        total = total.astype(BF16)
        for slot in range(out_ref.shape[0]):
            out_ref[slot, :, side * lanes : (side + 1) * lanes] = total


def weights_kernel(span, parts_ref, weight_ref, bias_ref):
    third = parts_ref.shape[0] // 3
    for index in range(3):
        low = index * third
        weight_ref[index * span : (index + 1) * span] = parts_ref[low : low + span].astype(F32)
    pair = parts_ref[span:third].astype(F32)
    bias_ref[...] = pair[0:1] + pair[1:2]


def tiles_kernel(work_ref, arrived_ref, out_ref):
    hid, cells = out_ref.shape[1:]
    lanes = arrived_ref.shape[2]
    for index in range(out_ref.shape[0]):
        for piece in range(cells // lanes):
            out_ref[index, :, piece * lanes : (piece + 1) * lanes] = arrived_ref[
                work_ref[index], piece * hid : (piece + 1) * hid
            ].astype(F32)


def moved(values, lat_step, lon_step, lat_devices, lon_devices):
    pairs = []
    for lat in range(lat_devices):
        for lon in range(lon_devices):
            to_lat = lat + lat_step
            if lat_step and lat_devices == 2:
                to_lat = 1 - lat
            if 0 <= to_lat < lat_devices:
                to = to_lat * lon_devices + (lon + lon_step) % lon_devices
                pairs.append((lat * lon_devices + lon, to))
    return lax.ppermute(values, ("lat", "lon"), pairs)


def exchange(ends, corners, left, right, lat_devices, lon_devices):
    def go(values, lat_step, lon_step):
        return moved(values, lat_step, lon_step, lat_devices, lon_devices)

    from_left, from_right = go(right, 0, 1), go(left, 0, -1)
    if lat_devices == 2:
        row = go(ends[0], 1, 0)
        row_left, row_right = go(corners[0], 1, 1), go(corners[0], 1, -1)
        return (row, row, row_left, row_right, row_left, row_right, from_left, from_right)
    return (
        go(ends[1], 1, 0),
        go(ends[0], -1, 0),
        go(corners[1], 1, 1),
        go(corners[1], 1, -1),
        go(corners[0], -1, 1),
        go(corners[0], -1, -1),
        from_left,
        from_right,
    )


def body(forcing, hidden, cell, grad_hidden, grad_cell, wet_mask, tile_owner, w_gates, b_gates):
    lat_index = lax.axis_index("lat")
    lon_index = lax.axis_index("lon")
    lat_devices = lax.axis_size("lat")
    lon_devices = lax.axis_size("lon")
    inp, rows, width = forcing.shape
    hid = hidden.shape[0]
    channels = inp + hid
    gates = w_gates.shape[0]
    span = 3 * channels
    third = (span + 128) // 128 * 128
    cells = rows * width
    tile_cols = width // TILE
    capacity = tile_cols // 2
    place = jnp.stack(
        [
            lat_index,
            lon_index,
            (lat_index > 0).astype(jnp.int32),
            (lat_index < lat_devices - 1).astype(jnp.int32),
        ]
    ).astype(jnp.int32)

    def shaped(*shape, dtype=BF16):
        return jax.ShapeDtypeStruct(shape, dtype)

    end_count = 1 if lat_devices == 2 else 2
    edges = call(
        edges_kernel,
        (shaped(channels, cells),) + (shaped(channels, width),) * (end_count + 2),
        (place, forcing, hidden),
        scalars=1,
        scratch=[pltpu.VMEM((channels * rows, width), F32)],
        moved=4 * channels * cells,
    )
    flat, ends, (left, right) = edges[0], edges[1:-2], edges[-2:]
    halo = exchange(ends, ends, left, right, lat_devices, lon_devices)
    w_turned = w_gates.T
    cell_flat, hcot_flat, ccot_flat, w_rows, bias = call(
        flatten_kernel,
        (shaped(hid, cells),) * 3
        + (shaped(gates, 3 * third), shaped(gates, width, dtype=F32)),
        (cell, grad_hidden, grad_cell, w_turned, b_gates.reshape(1, gates)),
        scratch=[pltpu.VMEM((hid * rows, width), F32)],
        moved=12 * hid * cells,
    )
    halves = 2 if lat_devices == 2 else 1
    lanes = gates // halves
    hidden_next, cell_grad, tiles, *weight_parts, delta = call(
        step_kernel,
        (
            shaped(hid, rows, width),
            shaped(hid * rows, width, dtype=F32),
            shaped(tile_cols, hid, TILE * TILE),
        )
        + (shaped(3 * third, lanes, dtype=F32),) * halves
        + (shaped(gates, (rows + 4) * width),),
        (place, wet_mask, tile_owner, flat, *halo)
        + (cell_flat, hcot_flat, ccot_flat, w_rows, bias),
        scalars=3,
        scratch=[
            pltpu.VMEM((third, (rows + 2) * width), BF16),
            pltpu.VMEM((hid * rows, width), F32),
        ],
        flops=4 * gates * 3 * span * cells,
        moved=16 * hid * cells,
    )
    swap = [(0, 1), (1, 0)]
    if halves == 2:
        weight_parts = (weight_parts[0], lax.ppermute(weight_parts[1], "lat", swap))
    else:
        weight_parts = (lax.psum(weight_parts[0], "lat"),)
    state_rows = hid * TILE * TILE // lanes
    share = 3 * third // lon_devices
    outgoing = call(
        lambda *refs: pack_kernel(span, *refs),
        shaped(lon_devices, state_rows + share, lanes),
        (place, wet_mask, tile_owner, tiles, *weight_parts),
        scalars=3,
        moved=4 * lon_devices * hid * TILE * TILE,
    )
    incoming = lax.all_to_all(outgoing, "lon", 0, 0, tiled=True)
    scaling = 1.0 / math.sqrt(float(lat_devices * lon_devices * capacity * TILE * TILE))
    summed = call(
        lambda *refs: sum_kernel(scaling, state_rows, *refs),
        shaped(share, lanes, dtype=F32),
        (incoming,),
        moved=2 * gates * 3 * third,
    )
    around = (summed,)
    if halves == 2:
        around += (lax.ppermute(summed, "lat", swap),)
    shares = call(
        lambda *refs: share_kernel(span, *refs),
        shaped(lon_devices, share, gates),
        (place, *around),
        scalars=1,
        moved=2 * gates * 3 * third,
    )
    owned = (wet_mask > 0) & (tile_owner == lon_index)
    arrived = jnp.any(owned.reshape(lon_devices, tile_cols), 1)
    order = jnp.arange(lon_devices, dtype=jnp.int32)
    rank = jnp.sum((arrived[:, None] & (order[:, None] < order[None, :])).astype(jnp.int32), 0)
    placed = arrived[None, :] & (rank[None, :] == jnp.arange(capacity, dtype=jnp.int32)[:, None])
    work = jnp.sum(jnp.where(placed, order[None, :], 0), 1)
    cell_next = call(
        tiles_kernel,
        shaped(capacity, hid, TILE * TILE, dtype=F32),
        (work, incoming),
        scalars=1,
        moved=2 * lon_devices * hid * TILE * TILE,
        after=(shares,),
    )
    grad_parts = call(
        spread_kernel,
        (shaped(hid, cells, dtype=F32),) + (shaped(hid, width),) * (2 * end_count + 2),
        (place, delta, w_turned),
        scalars=1,
        scratch=[pltpu.VMEM((3, hid, (rows + 2) * width), F32)],
        flops=2 * gates * 9 * hid * cells,
        moved=8 * gates * cells,
        after=(shares,),
    )
    grad_flat, grad_ends, grad_sides = grad_parts[0], grad_parts[1:-2], grad_parts[-2:]
    grad_halo = exchange(
        grad_ends[0::2], grad_ends[1::2], *grad_sides, lat_devices, lon_devices
    )
    hidden_grad = call(
        fold_kernel,
        shaped(hid * rows, width, dtype=F32),
        (place, grad_flat, *grad_halo),
        scalars=1,
        moved=8 * hid * cells,
    )
    gathered = lax.all_to_all(shares, "lon", 0, 0, tiled=True)
    weight_grad, bias_grad = call(
        lambda *refs: weights_kernel(span, *refs),
        (shaped(3 * span, gates, dtype=F32), shaped(1, gates, dtype=F32)),
        (gathered.reshape(3 * third, gates),),
        moved=6 * gates * 3 * third,
    )
    return (
        hidden_next,
        cell_next,
        hidden_grad.reshape(hid, rows, width),
        cell_grad.reshape(hid, rows, width),
        weight_grad.T,
        bias_grad.reshape(gates),
    )


def solution(mesh):
    return jax.shard_map(
        body,
        mesh=mesh,
        in_specs=(
            P(None, "lat", "lon"),
            P(None, "lat", "lon"),
            P(None, "lat", "lon"),
            P(None, "lat", "lon"),
            P(None, "lat", "lon"),
            P("lat", None),
            P("lat", None),
            P(),
            P(),
        ),
        out_specs=(
            P(None, "lat", "lon"),
            P(("lat", "lon"), None, None),
            P(None, "lat", "lon"),
            P(None, "lat", "lon"),
            P(),
            P(),
        ),
        check_vma=False,
    )
```

```python
import math

import jax
import jax.numpy as jnp
from jax import lax
from jax.experimental import pallas as pl
from jax.experimental.pallas import tpu as pltpu
from jax.sharding import PartitionSpec as P

TILE = 16
F32 = jnp.float32
BF16 = jnp.bfloat16
LIMIT = 48 * 1024 * 1024
SMEM = pl.BlockSpec(memory_space=pltpu.SMEM)
VMEM = pl.BlockSpec(memory_space=pltpu.VMEM)


def call(kernel, outs, operands, scalars=0, scratch=(), flops=0, moved=0, after=(), fetched=0):
    count = len(operands)
    kept = count - fetched
    total = count + len(after)

    def run(*refs):
        if not fetched:
            kernel(*refs[:count], *refs[total:])
            return
        *rest, semaphores = refs[total:]
        buffers = rest[len(rest) - fetched :]
        copies = [
            pltpu.make_async_copy(source, target, semaphores.at[index])
            for index, (source, target) in enumerate(zip(refs[kept:count], buffers))
        ]
        for copy in copies:
            copy.start()
        waits = [copy.wait for copy in copies]
        kernel(waits, *refs[:kept], *buffers, *rest[: len(rest) - fetched])

    scratch = list(scratch)
    operands = list(operands)
    for index in range(kept, count):
        operands[index] = pltpu.with_memory_space_constraint(operands[index], pltpu.HBM)
    if fetched:
        scratch += [pltpu.VMEM(leaf.shape, leaf.dtype) for leaf in operands[kept:]]
        scratch.append(pltpu.SemaphoreType.DMA((fetched,)))

    return pl.pallas_call(
        run,
        out_shape=outs,
        in_specs=[SMEM] * scalars
        + [VMEM] * (kept - scalars)
        + [pl.BlockSpec(memory_space=pltpu.HBM)] * fetched
        + [VMEM] * len(after),
        out_specs=jax.tree.map(lambda _: VMEM, outs),
        scratch_shapes=scratch,
        compiler_params=pltpu.CompilerParams(vmem_limit_bytes=LIMIT),
        cost_estimate=pl.CostEstimate(flops=flops, bytes_accessed=moved, transcendentals=0),
    )(*operands, *after)


def lane_index(shape):
    return lax.broadcasted_iota(jnp.int32, shape, 1)


def sigmoid(values):
    return 0.5 * jnp.tanh(0.5 * values) + 0.5


def edges_kernel(waits, place_ref, forcing_ref, hidden_ref, flat_ref, *rest):
    row_refs, (left_ref, right_ref, wide_ref) = rest[:-3], rest[-3:]
    inp, rows, width = forcing_ref.shape
    channels = inp + hidden_ref.shape[0]
    for wait in waits:
        wait()
    wide_ref[: inp * rows] = forcing_ref[...].astype(F32).reshape(inp * rows, width)
    wide_ref[inp * rows :] = hidden_ref[...].astype(F32).reshape((channels - inp) * rows, width)
    lane = lane_index((channels, width))
    left = jnp.zeros((channels, width), F32)
    right = jnp.zeros((channels, width), F32)
    ends = []
    for row in range(rows):
        slab = wide_ref[pl.ds(row, channels, stride=rows), :]
        flat_ref[:, row * width : (row + 1) * width] = slab.astype(BF16)
        left = jnp.where(lane == row, slab[:, :1], left)
        right = jnp.where(lane == row, slab[:, width - 1 :], right)
        if row in (0, rows - 1):
            ends.append(slab)
    left_ref[...] = left.astype(BF16)
    right_ref[...] = right.astype(BF16)
    if len(row_refs) == 1:
        row_refs[0][...] = jnp.where(place_ref[0] == 0, ends[-1], ends[0]).astype(BF16)
    else:
        row_refs[0][...] = ends[0].astype(BF16)
        row_refs[1][...] = ends[-1].astype(BF16)


def flatten_kernel(
    waits,
    b_ref,
    wt_ref,
    cell_ref,
    hcot_ref,
    ccot_ref,
    cell_out,
    hcot_out,
    ccot_out,
    w_ref,
    bias_ref,
    wide_ref,
):
    hid, rows, width = cell_ref.shape
    gates = wt_ref.shape[1]
    span = wt_ref.shape[0] // 3
    third = w_ref.shape[1] // 3
    waits[0]()
    bias_ref[...] = jnp.broadcast_to(b_ref[...], (bias_ref.shape[1], gates)).T
    waits[1]()
    blank = jnp.zeros((third - span, gates), F32)
    for index in range(3):
        block = wt_ref[index * span : (index + 1) * span].astype(F32)
        w_ref[:, index * third : (index + 1) * third] = (
            jnp.concatenate([block, blank], 0).T.astype(BF16)
        )
    for wait, source, target in zip(
        waits[2:], (cell_ref, hcot_ref, ccot_ref), (cell_out, hcot_out, ccot_out)
    ):
        wait()
        wide_ref[...] = source[...].astype(F32).reshape(hid * rows, width)
        for row in range(rows):
            target[:, row * width : (row + 1) * width] = wide_ref[
                pl.ds(row, hid, stride=rows), :
            ].astype(BF16)


def step_kernel(
    place_ref,
    wet_ref,
    owner_ref,
    flat_ref,
    up_ref,
    down_ref,
    up_left_ref,
    up_right_ref,
    down_left_ref,
    down_right_ref,
    left_ref,
    right_ref,
    cell_ref,
    hcot_ref,
    ccot_ref,
    w_ref,
    b_ref,
    hidden_next_ref,
    cell_grad_ref,
    tiles_ref,
    *rest,
):
    weight_refs, (delta_ref, taps_ref, wide_ref) = rest[:-3], rest[-3:]
    channels = flat_ref.shape[0]
    hid = cell_ref.shape[0]
    gates = w_ref.shape[0]
    width = up_ref.shape[1]
    rows = flat_ref.shape[1] // width
    tile_cols = width // TILE
    span = 3 * channels
    first_tile = place_ref[1] * tile_cols
    lane = lane_index((channels, width))

    def put(row, slab, before, after):
        lanes = slice(row * width, (row + 1) * width)
        shifted = jnp.where(lane == 0, before, pltpu.roll(slab, 1, 1))
        taps_ref[0:channels, lanes] = shifted.astype(BF16)
        taps_ref[channels : 2 * channels, lanes] = slab.astype(BF16)
        shifted = jnp.where(lane == width - 1, after, pltpu.roll(slab, width - 1, 1))
        taps_ref[2 * channels : span, lanes] = shifted.astype(BF16)

    for row, flag, refs in (
        (0, place_ref[2], (up_ref, up_left_ref, up_right_ref)),
        (rows + 1, place_ref[3], (down_ref, down_left_ref, down_right_ref)),
    ):
        slab, before, after = [
            jnp.where(flag == 1, ref[...].astype(F32), 0.0) for ref in refs
        ]
        put(row, slab, before[:, width - 1 :], after[:, :1])
    left = left_ref[...].astype(F32)
    right = right_ref[...].astype(F32)
    for row in range(rows):
        slab = flat_ref[:, row * width : (row + 1) * width].astype(F32)
        put(row + 1, slab, left[:, row : row + 1], right[:, row : row + 1])
    extra = taps_ref.shape[0] - span
    ones = lax.broadcasted_iota(jnp.int32, (extra, taps_ref.shape[1]), 0) == 0
    taps_ref[span:] = jnp.where(ones, 1.0, 0.0).astype(BF16)

    live = jnp.zeros((1, width), F32)
    live_lane = lane_index((1, width)) // TILE
    for tile in range(tile_cols):
        wet = (wet_ref[0, first_tile + tile] > 0).astype(F32)
        live = jnp.where(live_lane == tile, wet, live)
    step = 2 if rows % 2 == 0 else 1
    chunk = step * width
    live = jnp.concatenate([live] * step, 1)
    third = w_ref.shape[1] // 3
    blank = jnp.zeros((gates, 2 * width), BF16)
    delta_ref[:, : 2 * width] = blank
    delta_ref[:, (rows + 2) * width :] = blank
    bias = jnp.concatenate([b_ref[...]] * step, 1)
    group = 128 // TILE
    states = []
    for start in range(0, rows, step):
        pre = bias
        for row_off in range(3):
            low = (start + row_off) * width
            pre = pre + jnp.dot(
                w_ref[:, row_off * third : (row_off + 1) * third],
                taps_ref[:, low : low + chunk],
                preferred_element_type=F32,
            )
        gate_in = sigmoid(pre[:hid])
        gate_forget = sigmoid(pre[hid : 2 * hid])
        gate_out = sigmoid(pre[2 * hid : 3 * hid])
        candidate = jnp.tanh(pre[3 * hid :])
        lanes = slice(start * width, start * width + chunk)
        cell_in = cell_ref[:, lanes].astype(F32)
        cell_new = gate_forget * cell_in + gate_in * candidate
        squash = jnp.tanh(cell_new)
        hidden_new = live * gate_out * squash
        back_h = live * hcot_ref[:, lanes].astype(F32)
        back_c = live * ccot_ref[:, lanes].astype(F32) + back_h * gate_out * (1.0 - squash * squash)
        cell_back = back_c * gate_forget
        carried = back_c * gate_in
        terms = (
            carried * candidate * (1.0 - gate_in),
            cell_back * cell_in * (1.0 - gate_forget),
            back_h * squash * gate_out * (1.0 - gate_out),
            carried * (1.0 - candidate * candidate),
        )
        low = (start + 2) * width
        for index, term in enumerate(terms):
            delta_ref[index * hid : (index + 1) * hid, low : low + chunk] = term.astype(BF16)
        for part in range(step):
            piece = slice(part * width, (part + 1) * width)
            wide_ref[pl.ds(start + part, hid, stride=rows), :] = hidden_new[:, piece]
            cell_grad_ref[pl.ds(start + part, hid, stride=rows), :] = cell_back[:, piece]
            states.append(cell_new[:, piece])
        if len(states) == group:
            block_of = lane_index((hid, width)) // TILE
            half = (start + step) // group - 1
            stride = group // 2
            while stride:
                upper = (block_of & stride) != 0
                mixed = list(states)
                for low_index in range(group):
                    if low_index & stride == 0:
                        first, second = states[low_index], states[low_index + stride]
                        mixed[low_index] = jnp.where(
                            upper, pltpu.roll(second, stride * TILE, 1), first
                        )
                        mixed[low_index + stride] = jnp.where(
                            upper, second, pltpu.roll(first, width - stride * TILE, 1)
                        )
                states = mixed
                stride //= 2
            for tile in range(tile_cols):
                tiles_ref[tile, :, half * 128 : (half + 1) * 128] = states[tile].astype(BF16)
            states = []
    hidden_next_ref[...] = wide_ref[...].reshape(hid, rows, width).astype(BF16)
    delta = delta_ref[:, 2 * width : (rows + 2) * width]
    for row_off in range(3):
        part = lax.dot_general(
            taps_ref[:, row_off * width : (row_off + rows) * width],
            delta,
            (((1,), (1,)), ((), ())),
            preferred_element_type=F32,
        )
        place = slice(row_off * third, (row_off + 1) * third)
        if len(weight_refs) == 1:
            weight_refs[0][place] = part
        else:
            low, high = part[:, : gates // 2], part[:, gates // 2 :]
            weight_refs[0][place] = jnp.where(place_ref[0] == 0, low, high)
            weight_refs[1][place] = jnp.where(place_ref[0] == 0, high, low)


def spread_kernel(place_ref, delta_ref, wt_ref, grad_ref, *rest):
    row_refs, (left_ref, right_ref, side_ref) = rest[:-3], rest[-3:]
    hid = grad_ref.shape[0]
    width = left_ref.shape[1]
    rows = grad_ref.shape[1] // width
    channels = wt_ref.shape[0] // 9
    total = [None] * 3
    for col_off in range(3):
        for row_off in range(3):
            first = (row_off * 3 + col_off + 1) * channels - hid
            low = (2 - row_off) * width
            term = jnp.dot(
                wt_ref[first : first + hid],
                delta_ref[:, low : low + (rows + 2) * width],
                preferred_element_type=F32,
            )
            total[col_off] = term if row_off == 0 else total[col_off] + term
        side_ref[col_off] = total[col_off]
    lane = lane_index((hid, width))
    left = jnp.zeros((hid, width), F32)
    right = jnp.zeros((hid, width), F32)
    ends = []
    for row in range(rows + 2):
        lanes = slice(row * width, (row + 1) * width)
        before = side_ref[0, :, lanes]
        after = side_ref[2, :, lanes]
        slab = (
            side_ref[1, :, lanes]
            + jnp.where(lane == width - 1, 0.0, pltpu.roll(before, width - 1, 1))
            + jnp.where(lane == 0, 0.0, pltpu.roll(after, 1, 1))
        )
        if row in (0, rows + 1):
            corners = jnp.where(lane == 0, before[:, :1], 0.0)
            corners = jnp.where(lane == width - 1, after[:, width - 1 :], corners)
            ends.append((slab, corners))
        else:
            grad_ref[:, (row - 1) * width : row * width] = slab
            left = jnp.where(lane == row - 1, before[:, :1], left)
            right = jnp.where(lane == row - 1, after[:, width - 1 :], right)
    left_ref[...] = left.astype(BF16)
    right_ref[...] = right.astype(BF16)
    if len(row_refs) == 2:
        for index in range(2):
            row_refs[index][...] = jnp.where(
                place_ref[0] == 0, ends[1][index], ends[0][index]
            ).astype(BF16)
    else:
        for end in range(2):
            for index in range(2):
                row_refs[2 * end + index][...] = ends[end][index].astype(BF16)


def fold_kernel(
    place_ref,
    grad_ref,
    up_ref,
    down_ref,
    up_left_ref,
    up_right_ref,
    down_left_ref,
    down_right_ref,
    left_ref,
    right_ref,
    out_ref,
    token_ref,
):
    token_ref[...] = jnp.zeros(token_ref.shape, F32)
    hid = grad_ref.shape[0]
    width = up_ref.shape[1]
    rows = grad_ref.shape[1] // width
    lane = lane_index((hid, width))
    left = left_ref[...].astype(F32)
    right = right_ref[...].astype(F32)
    ends = {}
    for row, flag, refs in (
        (0, place_ref[2], (up_ref, up_left_ref, up_right_ref)),
        (rows - 1, place_ref[3], (down_ref, down_left_ref, down_right_ref)),
    ):
        slab, before, after = [ref[...].astype(F32) for ref in refs]
        slab = slab + jnp.where(lane == 0, before[:, width - 1 :], 0.0)
        slab = slab + jnp.where(lane == width - 1, after[:, :1], 0.0)
        ends[row] = jnp.where(flag == 1, slab, 0.0)
    for row in range(rows):
        slab = grad_ref[:, row * width : (row + 1) * width]
        slab = slab + jnp.where(lane == 0, left[:, row : row + 1], 0.0)
        slab = slab + jnp.where(lane == width - 1, right[:, row : row + 1], 0.0)
        if row in ends:
            slab = slab + ends[row]
        out_ref[pl.ds(row, hid, stride=rows), :] = slab


def split_bias(block, row):
    index = lax.broadcasted_iota(jnp.int32, block.shape, 0)
    rest = pltpu.roll(block - block.astype(BF16).astype(F32), 1, 0)
    return jnp.where(index == row + 1, rest, block)


def pack_kernel(span, place_ref, wet_ref, owner_ref, tiles_ref, *refs):
    out_ref, token_ref = refs[-2:]
    token_ref[...] = jnp.zeros(token_ref.shape, F32)
    tile_cols, hid, cells = tiles_ref.shape
    lanes = out_ref.shape[2]
    pieces = cells // 128
    state_rows = hid * pieces * 128 // lanes
    slots = out_ref.shape[0]
    third = refs[0].shape[0] // 3
    out_ref[:, :state_rows] = jnp.zeros((slots, state_rows, lanes), BF16)
    for tile in range(tile_cols):
        index = place_ref[1] * tile_cols + tile

        @pl.when(wet_ref[0, index] > 0)
        def _():
            for piece in range(cells // lanes):
                out_ref[owner_ref[0, index], piece * hid : (piece + 1) * hid] = tiles_ref[
                    tile, :, piece * lanes : (piece + 1) * lanes
                ]

    total = refs[0][...]
    for ref in refs[1:-2]:
        total = total + ref[...]
    total = jnp.concatenate([split_bias(total[:third], span), total[third:]], 0)
    share = total.shape[0] // slots
    for slot in range(slots):
        out_ref[slot, state_rows:] = total[slot * share : (slot + 1) * share].astype(BF16)


def sum_kernel(scaling, span, state_rows, place_ref, parts_ref, out_ref):
    total = parts_ref[0, state_rows:].astype(F32)
    for index in range(1, parts_ref.shape[0]):
        total = total + parts_ref[index, state_rows:].astype(F32)
    total = total * scaling
    share = total.shape[0]
    row = span % share
    index = lax.broadcasted_iota(jnp.int32, total.shape, 0)
    whole = jnp.where(index == row, total + pltpu.roll(total, share - 1, 0), total)
    total = jnp.where(place_ref[1] == span // share, split_bias(whole, row), total)
    for index in range(out_ref.shape[0]):
        out_ref[index] = total.astype(BF16)


def weights_kernel(span, place_ref, *refs):
    *parts, weight_ref, bias_ref = refs
    third = parts[0].shape[0] // 3
    half = parts[0].shape[1]
    for side in range(len(parts)):
        if len(parts) == 1:
            pick = parts[0][...]
        else:
            pick = jnp.where(place_ref[0] == side, parts[0][...], parts[1][...])
        pick = pick.astype(F32)
        lanes = slice(side * half, (side + 1) * half)
        for index in range(3):
            weight_ref[index * span : (index + 1) * span, lanes] = pick[
                index * third : index * third + span
            ]
        bias_ref[:, lanes] = pick[span : span + 1] + pick[span + 1 : span + 2]


def tiles_kernel(work_ref, arrived_ref, out_ref):
    hid, cells = out_ref.shape[1:]
    lanes = arrived_ref.shape[2]
    for index in range(out_ref.shape[0]):
        for piece in range(cells // lanes):
            out_ref[index, :, piece * lanes : (piece + 1) * lanes] = arrived_ref[
                work_ref[index], piece * hid : (piece + 1) * hid
            ].astype(F32)


def moved(values, lat_step, lon_step, lat_devices, lon_devices):
    pairs = []
    for lat in range(lat_devices):
        for lon in range(lon_devices):
            to_lat = lat + lat_step
            if lat_step and lat_devices == 2:
                to_lat = 1 - lat
            if 0 <= to_lat < lat_devices:
                to = to_lat * lon_devices + (lon + lon_step) % lon_devices
                pairs.append((lat * lon_devices + lon, to))
    return lax.ppermute(values, ("lat", "lon"), pairs)


def exchange(ends, corners, left, right, lat_devices, lon_devices):
    def go(values, lat_step, lon_step):
        return moved(values, lat_step, lon_step, lat_devices, lon_devices)

    from_left, from_right = go(right, 0, 1), go(left, 0, -1)
    if lat_devices == 2:
        row = go(ends[0], 1, 0)
        row_left, row_right = go(corners[0], 1, 1), go(corners[0], 1, -1)
        return (row, row, row_left, row_right, row_left, row_right, from_left, from_right)
    return (
        go(ends[1], 1, 0),
        go(ends[0], -1, 0),
        go(corners[1], 1, 1),
        go(corners[1], 1, -1),
        go(corners[0], -1, 1),
        go(corners[0], -1, -1),
        from_left,
        from_right,
    )


def body(forcing, hidden, cell, grad_hidden, grad_cell, wet_mask, tile_owner, w_gates, b_gates):
    lat_index = lax.axis_index("lat")
    lon_index = lax.axis_index("lon")
    lat_devices = lax.axis_size("lat")
    lon_devices = lax.axis_size("lon")
    inp, rows, width = forcing.shape
    hid = hidden.shape[0]
    channels = inp + hid
    gates = w_gates.shape[0]
    span = 3 * channels
    third = (span + 128) // 128 * 128
    cells = rows * width
    tile_cols = width // TILE
    capacity = tile_cols // 2
    place = jnp.stack(
        [
            lat_index,
            lon_index,
            (lat_index > 0).astype(jnp.int32),
            (lat_index < lat_devices - 1).astype(jnp.int32),
        ]
    ).astype(jnp.int32)

    def shaped(*shape, dtype=BF16):
        return jax.ShapeDtypeStruct(shape, dtype)

    end_count = 1 if lat_devices == 2 else 2
    edges = call(
        edges_kernel,
        (shaped(channels, cells),) + (shaped(channels, width),) * (end_count + 2),
        (place, forcing, hidden),
        scalars=1,
        scratch=[pltpu.VMEM((channels * rows, width), F32)],
        moved=4 * channels * cells,
        fetched=2,
    )
    flat, ends, (left, right) = edges[0], edges[1:-2], edges[-2:]
    halo = exchange(ends, ends, left, right, lat_devices, lon_devices)
    w_turned = w_gates.T
    cell_flat, hcot_flat, ccot_flat, w_rows, bias = call(
        flatten_kernel,
        (shaped(hid, cells),) * 3
        + (shaped(gates, 3 * third), shaped(gates, width, dtype=F32)),
        (b_gates.reshape(1, gates), w_turned, cell, grad_hidden, grad_cell),
        scratch=[pltpu.VMEM((hid * rows, width), F32)],
        moved=12 * hid * cells,
        fetched=5,
    )
    halves = 2 if lat_devices == 2 else 1
    lanes = gates // halves
    hidden_next, cell_grad, tiles, *weight_parts, delta = call(
        step_kernel,
        (
            shaped(hid, rows, width),
            shaped(hid * rows, width, dtype=F32),
            shaped(tile_cols, hid, TILE * TILE),
        )
        + (shaped(3 * third, lanes, dtype=F32),) * halves
        + (shaped(gates, (rows + 4) * width),),
        (place, wet_mask, tile_owner, flat, *halo)
        + (cell_flat, hcot_flat, ccot_flat, w_rows, bias),
        scalars=3,
        scratch=[
            pltpu.VMEM((third, (rows + 2) * width), BF16),
            pltpu.VMEM((hid * rows, width), F32),
        ],
        flops=4 * gates * 3 * span * cells,
        moved=16 * hid * cells,
    )
    swap = [(0, 1), (1, 0)]
    if halves == 2:
        weight_parts = (weight_parts[0], lax.ppermute(weight_parts[1], "lat", swap))
    else:
        weight_parts = (lax.psum(weight_parts[0], "lat"),)
    state_rows = hid * TILE * TILE // lanes
    share = 3 * third // lon_devices
    outgoing, packed = call(
        lambda *refs: pack_kernel(span, *refs),
        (shaped(lon_devices, state_rows + share, lanes), shaped(8, 128, dtype=F32)),
        (place, wet_mask, tile_owner, tiles, *weight_parts),
        scalars=3,
        moved=4 * lon_devices * hid * TILE * TILE,
    )
    incoming = lax.all_to_all(outgoing, "lon", 0, 0, tiled=True)
    grad_parts = call(
        spread_kernel,
        (shaped(hid, cells, dtype=F32),) + (shaped(hid, width),) * (2 * end_count + 2),
        (place, delta, w_turned),
        scalars=1,
        scratch=[pltpu.VMEM((3, hid, (rows + 2) * width), F32)],
        flops=2 * gates * 9 * hid * cells,
        moved=8 * gates * cells,
        after=(packed,),
    )
    grad_flat, grad_ends, grad_sides = grad_parts[0], grad_parts[1:-2], grad_parts[-2:]
    grad_halo = exchange(
        grad_ends[0::2], grad_ends[1::2], *grad_sides, lat_devices, lon_devices
    )
    hidden_grad, folded = call(
        fold_kernel,
        (shaped(hid * rows, width, dtype=F32), shaped(8, 128, dtype=F32)),
        (place, grad_flat, *grad_halo),
        scalars=1,
        moved=8 * hid * cells,
    )
    scaling = 1.0 / math.sqrt(float(lat_devices * lon_devices * capacity * TILE * TILE))
    shares = call(
        lambda *refs: sum_kernel(scaling, span, state_rows, *refs),
        shaped(lon_devices, share, lanes),
        (place, incoming),
        scalars=1,
        moved=2 * gates * 3 * third,
        after=(folded,),
    )
    owned = (wet_mask > 0) & (tile_owner == lon_index)
    arrived = jnp.any(owned.reshape(lon_devices, tile_cols), 1)
    order = jnp.arange(lon_devices, dtype=jnp.int32)
    rank = jnp.sum((arrived[:, None] & (order[:, None] < order[None, :])).astype(jnp.int32), 0)
    placed = arrived[None, :] & (rank[None, :] == jnp.arange(capacity, dtype=jnp.int32)[:, None])
    work = jnp.sum(jnp.where(placed, order[None, :], 0), 1)
    cell_next = call(
        tiles_kernel,
        shaped(capacity, hid, TILE * TILE, dtype=F32),
        (work, incoming),
        scalars=1,
        moved=2 * lon_devices * hid * TILE * TILE,
    )
    gathered = lax.all_to_all(shares, "lon", 0, 0, tiled=True).reshape(3 * third, lanes)
    gathered = (gathered,)
    if halves == 2:
        gathered += (lax.ppermute(gathered[0], "lat", swap),)
    weight_grad, bias_grad = call(
        lambda *refs: weights_kernel(span, *refs),
        (shaped(3 * span, gates, dtype=F32), shaped(1, gates, dtype=F32)),
        (place, *gathered),
        scalars=1,
        moved=6 * gates * 3 * third,
    )
    return (
        hidden_next,
        cell_next,
        hidden_grad.reshape(hid, rows, width),
        cell_grad.reshape(hid, rows, width),
        weight_grad.T,
        bias_grad.reshape(gates),
    )


def solution(mesh):
    return jax.shard_map(
        body,
        mesh=mesh,
        in_specs=(
            P(None, "lat", "lon"),
            P(None, "lat", "lon"),
            P(None, "lat", "lon"),
            P(None, "lat", "lon"),
            P(None, "lat", "lon"),
            P("lat", None),
            P("lat", None),
            P(),
            P(),
        ),
        out_specs=(
            P(None, "lat", "lon"),
            P(("lat", "lon"), None, None),
            P(None, "lat", "lon"),
            P(None, "lat", "lon"),
            P(),
            P(),
        ),
        check_vma=False,
    )
```

```python
import math

import jax
import jax.numpy as jnp
from jax import lax
from jax.experimental import pallas as pl
from jax.experimental.pallas import tpu as pltpu
from jax.sharding import PartitionSpec as P

TILE = 16
F32 = jnp.float32
BF16 = jnp.bfloat16
LIMIT = 48 * 1024 * 1024
SMEM = pl.BlockSpec(memory_space=pltpu.SMEM)
VMEM = pl.BlockSpec(memory_space=pltpu.VMEM)


def call(kernel, outs, operands, scalars=0, scratch=(), flops=0, moved=0, after=(), fetched=0):
    count = len(operands)
    kept = count - fetched
    total = count + len(after)

    def run(*refs):
        if not fetched:
            kernel(*refs[:count], *refs[total:])
            return
        *rest, semaphores = refs[total:]
        buffers = rest[len(rest) - fetched :]
        copies = [
            pltpu.make_async_copy(source, target, semaphores.at[index])
            for index, (source, target) in enumerate(zip(refs[kept:count], buffers))
        ]
        for copy in copies:
            copy.start()
        waits = [copy.wait for copy in copies]
        kernel(waits, *refs[:kept], *buffers, *rest[: len(rest) - fetched])

    scratch = list(scratch)
    operands = list(operands)
    for index in range(kept, count):
        operands[index] = pltpu.with_memory_space_constraint(operands[index], pltpu.HBM)
    if fetched:
        scratch += [pltpu.VMEM(leaf.shape, leaf.dtype) for leaf in operands[kept:]]
        scratch.append(pltpu.SemaphoreType.DMA((fetched,)))

    return pl.pallas_call(
        run,
        out_shape=outs,
        in_specs=[SMEM] * scalars
        + [VMEM] * (kept - scalars)
        + [pl.BlockSpec(memory_space=pltpu.HBM)] * fetched
        + [VMEM] * len(after),
        out_specs=jax.tree.map(lambda _: VMEM, outs),
        scratch_shapes=scratch,
        compiler_params=pltpu.CompilerParams(vmem_limit_bytes=LIMIT),
        cost_estimate=pl.CostEstimate(flops=flops, bytes_accessed=moved, transcendentals=0),
    )(*operands, *after)


def lane_index(shape):
    return lax.broadcasted_iota(jnp.int32, shape, 1)


def sigmoid(values):
    return 0.5 * jnp.tanh(0.5 * values) + 0.5


def edges_kernel(waits, place_ref, forcing_ref, hidden_ref, flat_ref, *rest):
    row_refs, (left_ref, right_ref, wide_ref) = rest[:-3], rest[-3:]
    inp, rows, width = forcing_ref.shape
    channels = inp + hidden_ref.shape[0]
    for wait in waits:
        wait()
    wide_ref[: inp * rows] = forcing_ref[...].astype(F32).reshape(inp * rows, width)
    wide_ref[inp * rows :] = hidden_ref[...].astype(F32).reshape((channels - inp) * rows, width)
    lane = lane_index((channels, width))
    left = jnp.zeros((channels, width), F32)
    right = jnp.zeros((channels, width), F32)
    ends = []
    for row in range(rows):
        slab = wide_ref[pl.ds(row, channels, stride=rows), :]
        flat_ref[:, row * width : (row + 1) * width] = slab.astype(BF16)
        left = jnp.where(lane == row, slab[:, :1], left)
        right = jnp.where(lane == row, slab[:, width - 1 :], right)
        if row in (0, rows - 1):
            ends.append(slab)
    left_ref[...] = left.astype(BF16)
    right_ref[...] = right.astype(BF16)
    if len(row_refs) == 1:
        row_refs[0][...] = jnp.where(place_ref[0] == 0, ends[-1], ends[0]).astype(BF16)
    else:
        row_refs[0][...] = ends[0].astype(BF16)
        row_refs[1][...] = ends[-1].astype(BF16)


def flatten_kernel(
    waits,
    b_ref,
    wt_ref,
    cell_ref,
    hcot_ref,
    ccot_ref,
    cell_out,
    hcot_out,
    ccot_out,
    w_ref,
    bias_ref,
    wide_ref,
):
    hid, rows, width = cell_ref.shape
    gates = wt_ref.shape[1]
    span = wt_ref.shape[0] // 3
    third = w_ref.shape[1] // 3
    waits[0]()
    bias_ref[...] = jnp.broadcast_to(b_ref[...], (bias_ref.shape[1], gates)).T
    waits[1]()
    blank = jnp.zeros((third - span, gates), F32)
    for index in range(3):
        block = wt_ref[index * span : (index + 1) * span].astype(F32)
        w_ref[:, index * third : (index + 1) * third] = (
            jnp.concatenate([block, blank], 0).T.astype(BF16)
        )
    for wait, source, target in zip(
        waits[2:], (cell_ref, hcot_ref, ccot_ref), (cell_out, hcot_out, ccot_out)
    ):
        wait()
        wide_ref[...] = source[...].astype(F32).reshape(hid * rows, width)
        for row in range(rows):
            target[:, row * width : (row + 1) * width] = wide_ref[
                pl.ds(row, hid, stride=rows), :
            ].astype(BF16)


def corners_kernel(rows, up_ref, down_ref, left_ref, right_ref, left_out, right_out):
    lane = lane_index(left_ref.shape)
    width = up_ref.shape[1]
    up = up_ref[...].astype(F32)
    down = down_ref[...].astype(F32)
    for column, source, target in ((0, left_ref, left_out), (width - 1, right_ref, right_out)):
        values = source[...].astype(F32)
        values = jnp.where(lane == rows, up[:, column : column + 1], values)
        values = jnp.where(lane == rows + 1, down[:, column : column + 1], values)
        target[...] = values.astype(BF16)


def step_kernel(
    place_ref,
    wet_ref,
    owner_ref,
    flat_ref,
    up_ref,
    down_ref,
    left_ref,
    right_ref,
    cell_ref,
    hcot_ref,
    ccot_ref,
    w_ref,
    b_ref,
    hidden_next_ref,
    cell_grad_ref,
    tiles_ref,
    *rest,
):
    weight_refs, (delta_ref, taps_ref, wide_ref) = rest[:-3], rest[-3:]
    channels = flat_ref.shape[0]
    hid = cell_ref.shape[0]
    gates = w_ref.shape[0]
    width = up_ref.shape[1]
    rows = flat_ref.shape[1] // width
    tile_cols = width // TILE
    span = 3 * channels
    first_tile = place_ref[1] * tile_cols
    lane = lane_index((channels, width))

    def put(row, slab, before, after):
        lanes = slice(row * width, (row + 1) * width)
        shifted = jnp.where(lane == 0, before, pltpu.roll(slab, 1, 1))
        taps_ref[0:channels, lanes] = shifted.astype(BF16)
        taps_ref[channels : 2 * channels, lanes] = slab.astype(BF16)
        shifted = jnp.where(lane == width - 1, after, pltpu.roll(slab, width - 1, 1))
        taps_ref[2 * channels : span, lanes] = shifted.astype(BF16)

    left = left_ref[...].astype(F32)
    right = right_ref[...].astype(F32)
    for end, flag, ref in ((0, place_ref[2], up_ref), (1, place_ref[3], down_ref)):
        corner = slice(rows + end, rows + end + 1)
        slab, before, after = [
            jnp.where(flag == 1, values, 0.0)
            for values in (ref[...].astype(F32), left[:, corner], right[:, corner])
        ]
        put(end * (rows + 1), slab, before, after)
    for row in range(rows):
        slab = flat_ref[:, row * width : (row + 1) * width].astype(F32)
        put(row + 1, slab, left[:, row : row + 1], right[:, row : row + 1])
    extra = taps_ref.shape[0] - span
    ones = lax.broadcasted_iota(jnp.int32, (extra, taps_ref.shape[1]), 0) == 0
    taps_ref[span:] = jnp.where(ones, 1.0, 0.0).astype(BF16)

    live = jnp.zeros((1, width), F32)
    live_lane = lane_index((1, width)) // TILE
    for tile in range(tile_cols):
        wet = (wet_ref[0, first_tile + tile] > 0).astype(F32)
        live = jnp.where(live_lane == tile, wet, live)
    step = 2 if rows % 2 == 0 else 1
    chunk = step * width
    live = jnp.concatenate([live] * step, 1)
    third = w_ref.shape[1] // 3
    blank = jnp.zeros((gates, 2 * width), BF16)
    delta_ref[:, : 2 * width] = blank
    delta_ref[:, (rows + 2) * width :] = blank
    bias = jnp.concatenate([b_ref[...]] * step, 1)
    group = 128 // TILE
    states = []
    for start in range(0, rows, step):
        pre = bias
        for row_off in range(3):
            low = (start + row_off) * width
            pre = pre + jnp.dot(
                w_ref[:, row_off * third : (row_off + 1) * third],
                taps_ref[:, low : low + chunk],
                preferred_element_type=F32,
            )
        gate_in = sigmoid(pre[:hid])
        gate_forget = sigmoid(pre[hid : 2 * hid])
        gate_out = sigmoid(pre[2 * hid : 3 * hid])
        candidate = jnp.tanh(pre[3 * hid :])
        lanes = slice(start * width, start * width + chunk)
        cell_in = cell_ref[:, lanes].astype(F32)
        cell_new = gate_forget * cell_in + gate_in * candidate
        squash = jnp.tanh(cell_new)
        hidden_new = live * gate_out * squash
        back_h = live * hcot_ref[:, lanes].astype(F32)
        back_c = live * ccot_ref[:, lanes].astype(F32) + back_h * gate_out * (1.0 - squash * squash)
        cell_back = back_c * gate_forget
        carried = back_c * gate_in
        terms = (
            carried * candidate * (1.0 - gate_in),
            cell_back * cell_in * (1.0 - gate_forget),
            back_h * squash * gate_out * (1.0 - gate_out),
            carried * (1.0 - candidate * candidate),
        )
        low = (start + 2) * width
        for index, term in enumerate(terms):
            delta_ref[index * hid : (index + 1) * hid, low : low + chunk] = term.astype(BF16)
        for part in range(step):
            piece = slice(part * width, (part + 1) * width)
            wide_ref[pl.ds(start + part, hid, stride=rows), :] = hidden_new[:, piece]
            cell_grad_ref[pl.ds(start + part, hid, stride=rows), :] = cell_back[:, piece]
            states.append(cell_new[:, piece])
        if len(states) == group:
            block_of = lane_index((hid, width)) // TILE
            half = (start + step) // group - 1
            stride = group // 2
            while stride:
                upper = (block_of & stride) != 0
                mixed = list(states)
                for low_index in range(group):
                    if low_index & stride == 0:
                        first, second = states[low_index], states[low_index + stride]
                        mixed[low_index] = jnp.where(
                            upper, pltpu.roll(second, stride * TILE, 1), first
                        )
                        mixed[low_index + stride] = jnp.where(
                            upper, second, pltpu.roll(first, width - stride * TILE, 1)
                        )
                states = mixed
                stride //= 2
            for tile in range(tile_cols):
                tiles_ref[tile, :, half * 128 : (half + 1) * 128] = states[tile].astype(BF16)
            states = []
    hidden_next_ref[...] = wide_ref[...].reshape(hid, rows, width).astype(BF16)
    delta = delta_ref[:, 2 * width : (rows + 2) * width]
    for row_off in range(3):
        part = lax.dot_general(
            taps_ref[:, row_off * width : (row_off + rows) * width],
            delta,
            (((1,), (1,)), ((), ())),
            preferred_element_type=F32,
        )
        place = slice(row_off * third, (row_off + 1) * third)
        if len(weight_refs) == 1:
            weight_refs[0][place] = part
        else:
            low, high = part[:, : gates // 2], part[:, gates // 2 :]
            weight_refs[0][place] = jnp.where(place_ref[0] == 0, low, high)
            weight_refs[1][place] = jnp.where(place_ref[0] == 0, high, low)


def spread_kernel(place_ref, delta_ref, wt_ref, grad_ref, *rest):
    row_refs, (left_ref, right_ref, side_ref) = rest[:-3], rest[-3:]
    hid = grad_ref.shape[0]
    width = left_ref.shape[1]
    rows = grad_ref.shape[1] // width
    channels = wt_ref.shape[0] // 9
    total = [None] * 3
    for col_off in range(3):
        for row_off in range(3):
            first = (row_off * 3 + col_off + 1) * channels - hid
            low = (2 - row_off) * width
            term = jnp.dot(
                wt_ref[first : first + hid],
                delta_ref[:, low : low + (rows + 2) * width],
                preferred_element_type=F32,
            )
            total[col_off] = term if row_off == 0 else total[col_off] + term
        side_ref[col_off] = total[col_off]
    lane = lane_index((hid, width))
    left = jnp.zeros((hid, width), F32)
    right = jnp.zeros((hid, width), F32)
    ends = []
    for row in range(rows + 2):
        lanes = slice(row * width, (row + 1) * width)
        before = side_ref[0, :, lanes]
        after = side_ref[2, :, lanes]
        slab = (
            side_ref[1, :, lanes]
            + jnp.where(lane == width - 1, 0.0, pltpu.roll(before, width - 1, 1))
            + jnp.where(lane == 0, 0.0, pltpu.roll(after, 1, 1))
        )
        if row in (0, rows + 1):
            corners = jnp.where(lane == 0, before[:, :1], 0.0)
            corners = jnp.where(lane == width - 1, after[:, width - 1 :], corners)
            ends.append((slab, corners))
        else:
            grad_ref[:, (row - 1) * width : row * width] = slab
            left = jnp.where(lane == row - 1, before[:, :1], left)
            right = jnp.where(lane == row - 1, after[:, width - 1 :], right)
    left_ref[...] = left.astype(BF16)
    right_ref[...] = right.astype(BF16)
    if len(row_refs) == 2:
        for index in range(2):
            row_refs[index][...] = jnp.where(
                place_ref[0] == 0, ends[1][index], ends[0][index]
            ).astype(BF16)
    else:
        for end in range(2):
            for index in range(2):
                row_refs[2 * end + index][...] = ends[end][index].astype(BF16)


def fold_kernel(
    place_ref,
    grad_ref,
    up_ref,
    down_ref,
    up_left_ref,
    up_right_ref,
    down_left_ref,
    down_right_ref,
    left_ref,
    right_ref,
    out_ref,
):
    hid = grad_ref.shape[0]
    width = up_ref.shape[1]
    rows = grad_ref.shape[1] // width
    lane = lane_index((hid, width))
    left = left_ref[...].astype(F32)
    right = right_ref[...].astype(F32)
    ends = {}
    for row, flag, refs in (
        (0, place_ref[2], (up_ref, up_left_ref, up_right_ref)),
        (rows - 1, place_ref[3], (down_ref, down_left_ref, down_right_ref)),
    ):
        slab, before, after = [ref[...].astype(F32) for ref in refs]
        slab = slab + jnp.where(lane == 0, before[:, width - 1 :], 0.0)
        slab = slab + jnp.where(lane == width - 1, after[:, :1], 0.0)
        ends[row] = jnp.where(flag == 1, slab, 0.0)
    for row in range(rows):
        slab = grad_ref[:, row * width : (row + 1) * width]
        slab = slab + jnp.where(lane == 0, left[:, row : row + 1], 0.0)
        slab = slab + jnp.where(lane == width - 1, right[:, row : row + 1], 0.0)
        if row in ends:
            slab = slab + ends[row]
        out_ref[pl.ds(row, hid, stride=rows), :] = slab


def split_bias(block, row):
    index = lax.broadcasted_iota(jnp.int32, block.shape, 0)
    rest = pltpu.roll(block - block.astype(BF16).astype(F32), 1, 0)
    return jnp.where(index == row + 1, rest, block)


def pack_kernel(span, place_ref, wet_ref, owner_ref, tiles_ref, *refs):
    out_ref, token_ref = refs[-2:]
    token_ref[...] = jnp.zeros(token_ref.shape, F32)
    tile_cols, hid, cells = tiles_ref.shape
    lanes = out_ref.shape[2]
    pieces = cells // 128
    state_rows = hid * pieces * 128 // lanes
    slots = out_ref.shape[0]
    third = refs[0].shape[0] // 3
    out_ref[:, :state_rows] = jnp.zeros((slots, state_rows, lanes), BF16)
    for tile in range(tile_cols):
        index = place_ref[1] * tile_cols + tile

        @pl.when(wet_ref[0, index] > 0)
        def _():
            for piece in range(cells // lanes):
                out_ref[owner_ref[0, index], piece * hid : (piece + 1) * hid] = tiles_ref[
                    tile, :, piece * lanes : (piece + 1) * lanes
                ]

    total = refs[0][...]
    for ref in refs[1:-2]:
        total = total + ref[...]
    total = jnp.concatenate([split_bias(total[:third], span), total[third:]], 0)
    share = total.shape[0] // slots
    for slot in range(slots):
        out_ref[slot, state_rows:] = total[slot * share : (slot + 1) * share].astype(BF16)


def sum_kernel(scaling, span, state_rows, place_ref, parts_ref, out_ref):
    total = parts_ref[0, state_rows:].astype(F32)
    for index in range(1, parts_ref.shape[0]):
        total = total + parts_ref[index, state_rows:].astype(F32)
    total = total * scaling
    share = total.shape[0]
    row = span % share
    index = lax.broadcasted_iota(jnp.int32, total.shape, 0)
    whole = jnp.where(index == row, total + pltpu.roll(total, share - 1, 0), total)
    total = jnp.where(place_ref[1] == span // share, split_bias(whole, row), total)
    for index in range(out_ref.shape[0]):
        out_ref[index] = total.astype(BF16)


def weights_kernel(span, place_ref, *refs):
    *parts, weight_ref, bias_ref = refs
    third = parts[0].shape[0] // 3
    half = parts[0].shape[1]
    for side in range(len(parts)):
        if len(parts) == 1:
            pick = parts[0][...]
        else:
            pick = jnp.where(place_ref[0] == side, parts[0][...], parts[1][...])
        pick = pick.astype(F32)
        lanes = slice(side * half, (side + 1) * half)
        for index in range(3):
            weight_ref[index * span : (index + 1) * span, lanes] = pick[
                index * third : index * third + span
            ]
        bias_ref[:, lanes] = pick[span : span + 1] + pick[span + 1 : span + 2]


def tiles_kernel(work_ref, arrived_ref, out_ref):
    hid, cells = out_ref.shape[1:]
    lanes = arrived_ref.shape[2]
    for index in range(out_ref.shape[0]):
        for piece in range(cells // lanes):
            out_ref[index, :, piece * lanes : (piece + 1) * lanes] = arrived_ref[
                work_ref[index], piece * hid : (piece + 1) * hid
            ].astype(F32)


def moved(values, lat_step, lon_step, lat_devices, lon_devices):
    pairs = []
    for lat in range(lat_devices):
        for lon in range(lon_devices):
            to_lat = lat + lat_step
            if lat_step and lat_devices == 2:
                to_lat = 1 - lat
            if 0 <= to_lat < lat_devices:
                to = to_lat * lon_devices + (lon + lon_step) % lon_devices
                pairs.append((lat * lon_devices + lon, to))
    return lax.ppermute(values, ("lat", "lon"), pairs)


def exchange(ends, corners, left, right, lat_devices, lon_devices):
    def go(values, lat_step, lon_step):
        return moved(values, lat_step, lon_step, lat_devices, lon_devices)

    from_left, from_right = go(right, 0, 1), go(left, 0, -1)
    if lat_devices == 2:
        row = go(ends[0], 1, 0)
        row_left, row_right = go(corners[0], 1, 1), go(corners[0], 1, -1)
        return (row, row, row_left, row_right, row_left, row_right, from_left, from_right)
    return (
        go(ends[1], 1, 0),
        go(ends[0], -1, 0),
        go(corners[1], 1, 1),
        go(corners[1], 1, -1),
        go(corners[0], -1, 1),
        go(corners[0], -1, -1),
        from_left,
        from_right,
    )


def body(forcing, hidden, cell, grad_hidden, grad_cell, wet_mask, tile_owner, w_gates, b_gates):
    lat_index = lax.axis_index("lat")
    lon_index = lax.axis_index("lon")
    lat_devices = lax.axis_size("lat")
    lon_devices = lax.axis_size("lon")
    inp, rows, width = forcing.shape
    hid = hidden.shape[0]
    channels = inp + hid
    gates = w_gates.shape[0]
    span = 3 * channels
    third = (span + 128) // 128 * 128
    cells = rows * width
    tile_cols = width // TILE
    capacity = tile_cols // 2
    place = jnp.stack(
        [
            lat_index,
            lon_index,
            (lat_index > 0).astype(jnp.int32),
            (lat_index < lat_devices - 1).astype(jnp.int32),
        ]
    ).astype(jnp.int32)

    def shaped(*shape, dtype=BF16):
        return jax.ShapeDtypeStruct(shape, dtype)

    end_count = 1 if lat_devices == 2 else 2
    edges = call(
        edges_kernel,
        (shaped(channels, cells),) + (shaped(channels, width),) * (end_count + 2),
        (place, forcing, hidden),
        scalars=1,
        scratch=[pltpu.VMEM((channels * rows, width), F32)],
        moved=4 * channels * cells,
        fetched=2,
    )
    flat, ends, (left, right) = edges[0], edges[1:-2], edges[-2:]
    if lat_devices == 2:
        up = down = moved(ends[0], 1, 0, lat_devices, lon_devices)
    else:
        up = moved(ends[1], 1, 0, lat_devices, lon_devices)
        down = moved(ends[0], -1, 0, lat_devices, lon_devices)
    left, right = call(
        lambda *refs: corners_kernel(rows, *refs),
        (shaped(channels, width),) * 2,
        (up, down, left, right),
        moved=8 * channels * width,
    )
    halo = (
        up,
        down,
        moved(right, 0, 1, lat_devices, lon_devices),
        moved(left, 0, -1, lat_devices, lon_devices),
    )
    w_turned = w_gates.T
    cell_flat, hcot_flat, ccot_flat, w_rows, bias = call(
        flatten_kernel,
        (shaped(hid, cells),) * 3
        + (shaped(gates, 3 * third), shaped(gates, width, dtype=F32)),
        (b_gates.reshape(1, gates), w_turned, cell, grad_hidden, grad_cell),
        scratch=[pltpu.VMEM((hid * rows, width), F32)],
        moved=12 * hid * cells,
        fetched=5,
    )
    halves = 2 if lat_devices == 2 else 1
    lanes = gates // halves
    hidden_next, cell_grad, tiles, *weight_parts, delta = call(
        step_kernel,
        (
            shaped(hid, rows, width),
            shaped(hid * rows, width, dtype=F32),
            shaped(tile_cols, hid, TILE * TILE),
        )
        + (shaped(3 * third, lanes, dtype=F32),) * halves
        + (shaped(gates, (rows + 4) * width),),
        (place, wet_mask, tile_owner, flat, *halo)
        + (cell_flat, hcot_flat, ccot_flat, w_rows, bias),
        scalars=3,
        scratch=[
            pltpu.VMEM((third, (rows + 2) * width), BF16),
            pltpu.VMEM((hid * rows, width), F32),
        ],
        flops=4 * gates * 3 * span * cells,
        moved=16 * hid * cells,
    )
    swap = [(0, 1), (1, 0)]
    if halves == 2:
        weight_parts = (weight_parts[0], lax.ppermute(weight_parts[1], "lat", swap))
    else:
        weight_parts = (lax.psum(weight_parts[0], "lat"),)
    state_rows = hid * TILE * TILE // lanes
    share = 3 * third // lon_devices
    outgoing, packed = call(
        lambda *refs: pack_kernel(span, *refs),
        (shaped(lon_devices, state_rows + share, lanes), shaped(8, 128, dtype=F32)),
        (place, wet_mask, tile_owner, tiles, *weight_parts),
        scalars=3,
        moved=4 * lon_devices * hid * TILE * TILE,
    )
    incoming = lax.all_to_all(outgoing, "lon", 0, 0, tiled=True)
    grad_parts = call(
        spread_kernel,
        (shaped(hid, cells, dtype=F32),) + (shaped(hid, width),) * (2 * end_count + 2),
        (place, delta, w_turned),
        scalars=1,
        scratch=[pltpu.VMEM((3, hid, (rows + 2) * width), F32)],
        flops=2 * gates * 9 * hid * cells,
        moved=8 * gates * cells,
        after=(packed,),
    )
    grad_flat, grad_ends, grad_sides = grad_parts[0], grad_parts[1:-2], grad_parts[-2:]
    grad_halo = exchange(
        grad_ends[0::2], grad_ends[1::2], *grad_sides, lat_devices, lon_devices
    )
    hidden_grad = call(
        fold_kernel,
        shaped(hid * rows, width, dtype=F32),
        (place, grad_flat, *grad_halo),
        scalars=1,
        moved=8 * hid * cells,
    )
    scaling = 1.0 / math.sqrt(float(lat_devices * lon_devices * capacity * TILE * TILE))
    shares = call(
        lambda *refs: sum_kernel(scaling, span, state_rows, *refs),
        shaped(lon_devices, share, lanes),
        (place, incoming),
        scalars=1,
        moved=2 * gates * 3 * third,
        after=grad_halo,
    )
    owned = (wet_mask > 0) & (tile_owner == lon_index)
    arrived = jnp.any(owned.reshape(lon_devices, tile_cols), 1)
    order = jnp.arange(lon_devices, dtype=jnp.int32)
    rank = jnp.sum((arrived[:, None] & (order[:, None] < order[None, :])).astype(jnp.int32), 0)
    placed = arrived[None, :] & (rank[None, :] == jnp.arange(capacity, dtype=jnp.int32)[:, None])
    work = jnp.sum(jnp.where(placed, order[None, :], 0), 1)
    cell_next = call(
        tiles_kernel,
        shaped(capacity, hid, TILE * TILE, dtype=F32),
        (work, incoming),
        scalars=1,
        moved=2 * lon_devices * hid * TILE * TILE,
    )
    gathered = lax.all_to_all(shares, "lon", 0, 0, tiled=True).reshape(3 * third, lanes)
    gathered = (gathered,)
    if halves == 2:
        gathered += (lax.ppermute(gathered[0], "lat", swap),)
    weight_grad, bias_grad = call(
        lambda *refs: weights_kernel(span, *refs),
        (shaped(3 * span, gates, dtype=F32), shaped(1, gates, dtype=F32)),
        (place, *gathered),
        scalars=1,
        moved=6 * gates * 3 * third,
    )
    return (
        hidden_next,
        cell_next,
        hidden_grad.reshape(hid, rows, width),
        cell_grad.reshape(hid, rows, width),
        weight_grad.T,
        bias_grad.reshape(gates),
    )


def solution(mesh):
    return jax.shard_map(
        body,
        mesh=mesh,
        in_specs=(
            P(None, "lat", "lon"),
            P(None, "lat", "lon"),
            P(None, "lat", "lon"),
            P(None, "lat", "lon"),
            P(None, "lat", "lon"),
            P("lat", None),
            P("lat", None),
            P(),
            P(),
        ),
        out_specs=(
            P(None, "lat", "lon"),
            P(("lat", "lon"), None, None),
            P(None, "lat", "lon"),
            P(None, "lat", "lon"),
            P(),
            P(),
        ),
        check_vma=False,
    )
```

```python
import math

import jax
import jax.numpy as jnp
from jax import lax
from jax.experimental import pallas as pl
from jax.experimental.pallas import tpu as pltpu
from jax.sharding import PartitionSpec as P

TILE = 16
F32 = jnp.float32
BF16 = jnp.bfloat16
LIMIT = 48 * 1024 * 1024
SMEM = pl.BlockSpec(memory_space=pltpu.SMEM)
VMEM = pl.BlockSpec(memory_space=pltpu.VMEM)


def call(kernel, outs, operands, scalars=0, scratch=(), flops=0, moved=0, after=(), fetched=0):
    count = len(operands)
    kept = count - fetched
    total = count + len(after)

    def run(*refs):
        if not fetched:
            kernel(*refs[:count], *refs[total:])
            return
        *rest, semaphores = refs[total:]
        buffers = rest[len(rest) - fetched :]
        copies = [
            pltpu.make_async_copy(source, target, semaphores.at[index])
            for index, (source, target) in enumerate(zip(refs[kept:count], buffers))
        ]
        for copy in copies:
            copy.start()
        waits = [copy.wait for copy in copies]
        kernel(waits, *refs[:kept], *buffers, *rest[: len(rest) - fetched])

    scratch = list(scratch)
    operands = list(operands)
    for index in range(kept, count):
        operands[index] = pltpu.with_memory_space_constraint(operands[index], pltpu.HBM)
    if fetched:
        scratch += [pltpu.VMEM(leaf.shape, leaf.dtype) for leaf in operands[kept:]]
        scratch.append(pltpu.SemaphoreType.DMA((fetched,)))

    return pl.pallas_call(
        run,
        out_shape=outs,
        in_specs=[SMEM] * scalars
        + [VMEM] * (kept - scalars)
        + [pl.BlockSpec(memory_space=pltpu.HBM)] * fetched
        + [VMEM] * len(after),
        out_specs=jax.tree.map(lambda _: VMEM, outs),
        scratch_shapes=scratch,
        compiler_params=pltpu.CompilerParams(vmem_limit_bytes=LIMIT),
        cost_estimate=pl.CostEstimate(flops=flops, bytes_accessed=moved, transcendentals=0),
    )(*operands, *after)


def lane_index(shape):
    return lax.broadcasted_iota(jnp.int32, shape, 1)


def sigmoid(values):
    return 0.5 * jnp.tanh(0.5 * values) + 0.5


def edges_kernel(waits, place_ref, forcing_ref, hidden_ref, flat_ref, *rest):
    row_refs, (left_ref, right_ref, wide_ref) = rest[:-3], rest[-3:]
    inp, rows, width = forcing_ref.shape
    channels = inp + hidden_ref.shape[0]
    for wait in waits:
        wait()
    wide_ref[: inp * rows] = forcing_ref[...].astype(F32).reshape(inp * rows, width)
    wide_ref[inp * rows :] = hidden_ref[...].astype(F32).reshape((channels - inp) * rows, width)
    lane = lane_index((channels, width))
    left = jnp.zeros((channels, width), F32)
    right = jnp.zeros((channels, width), F32)
    ends = []
    for row in range(rows):
        slab = wide_ref[pl.ds(row, channels, stride=rows), :]
        flat_ref[:, row * width : (row + 1) * width] = slab.astype(BF16)
        left = jnp.where(lane == row, slab[:, :1], left)
        right = jnp.where(lane == row, slab[:, width - 1 :], right)
        if row in (0, rows - 1):
            ends.append(slab)
    left_ref[...] = left.astype(BF16)
    right_ref[...] = right.astype(BF16)
    if len(row_refs) == 1:
        row_refs[0][...] = jnp.where(place_ref[0] == 0, ends[-1], ends[0]).astype(BF16)
    else:
        row_refs[0][...] = ends[0].astype(BF16)
        row_refs[1][...] = ends[-1].astype(BF16)


def flatten_kernel(
    waits,
    b_ref,
    wt_ref,
    cell_ref,
    hcot_ref,
    ccot_ref,
    cell_out,
    hcot_out,
    ccot_out,
    w_ref,
    bias_ref,
    wide_ref,
):
    hid, rows, width = cell_ref.shape
    gates = wt_ref.shape[1]
    span = wt_ref.shape[0] // 3
    third = w_ref.shape[1] // 3
    waits[0]()
    bias_ref[...] = jnp.broadcast_to(b_ref[...], (bias_ref.shape[1], gates)).T
    waits[1]()
    blank = jnp.zeros((third - span, gates), F32)
    for index in range(3):
        block = wt_ref[index * span : (index + 1) * span].astype(F32)
        w_ref[:, index * third : (index + 1) * third] = (
            jnp.concatenate([block, blank], 0).T.astype(BF16)
        )
    for wait, source, target in zip(
        waits[2:], (cell_ref, hcot_ref, ccot_ref), (cell_out, hcot_out, ccot_out)
    ):
        wait()
        wide_ref[...] = source[...].astype(F32).reshape(hid * rows, width)
        for row in range(rows):
            target[:, row * width : (row + 1) * width] = wide_ref[
                pl.ds(row, hid, stride=rows), :
            ].astype(BF16)


def corners_kernel(rows, up_ref, down_ref, left_ref, right_ref, left_out, right_out):
    lane = lane_index(left_ref.shape)
    width = up_ref.shape[1]
    up = up_ref[...].astype(F32)
    down = down_ref[...].astype(F32)
    for column, source, target in ((0, left_ref, left_out), (width - 1, right_ref, right_out)):
        values = source[...].astype(F32)
        values = jnp.where(lane == rows, up[:, column : column + 1], values)
        values = jnp.where(lane == rows + 1, down[:, column : column + 1], values)
        target[...] = values.astype(BF16)


def step_kernel(
    place_ref,
    wet_ref,
    owner_ref,
    flat_ref,
    up_ref,
    down_ref,
    left_ref,
    right_ref,
    cell_ref,
    hcot_ref,
    ccot_ref,
    w_ref,
    b_ref,
    hidden_new_ref,
    cell_back_ref,
    tiles_ref,
    *rest,
):
    weight_refs, (delta_ref, taps_ref) = rest[:-2], rest[-2:]
    channels = flat_ref.shape[0]
    hid = cell_ref.shape[0]
    gates = w_ref.shape[0]
    width = up_ref.shape[1]
    rows = flat_ref.shape[1] // width
    tile_cols = width // TILE
    span = 3 * channels
    first_tile = place_ref[1] * tile_cols
    lane = lane_index((channels, width))

    def put(row, slab, before, after):
        lanes = slice(row * width, (row + 1) * width)
        shifted = jnp.where(lane == 0, before, pltpu.roll(slab, 1, 1))
        taps_ref[0:channels, lanes] = shifted.astype(BF16)
        taps_ref[channels : 2 * channels, lanes] = slab.astype(BF16)
        shifted = jnp.where(lane == width - 1, after, pltpu.roll(slab, width - 1, 1))
        taps_ref[2 * channels : span, lanes] = shifted.astype(BF16)

    left = left_ref[...].astype(F32)
    right = right_ref[...].astype(F32)
    for end, flag, ref in ((0, place_ref[2], up_ref), (1, place_ref[3], down_ref)):
        corner = slice(rows + end, rows + end + 1)
        slab, before, after = [
            jnp.where(flag == 1, values, 0.0)
            for values in (ref[...].astype(F32), left[:, corner], right[:, corner])
        ]
        put(end * (rows + 1), slab, before, after)
    for row in range(rows):
        slab = flat_ref[:, row * width : (row + 1) * width].astype(F32)
        put(row + 1, slab, left[:, row : row + 1], right[:, row : row + 1])
    extra = taps_ref.shape[0] - span
    ones = lax.broadcasted_iota(jnp.int32, (extra, taps_ref.shape[1]), 0) == 0
    taps_ref[span:] = jnp.where(ones, 1.0, 0.0).astype(BF16)

    live = jnp.zeros((1, width), F32)
    live_lane = lane_index((1, width)) // TILE
    for tile in range(tile_cols):
        wet = (wet_ref[0, first_tile + tile] > 0).astype(F32)
        live = jnp.where(live_lane == tile, wet, live)
    step = 2 if rows % 2 == 0 else 1
    chunk = step * width
    live = jnp.concatenate([live] * step, 1)
    third = w_ref.shape[1] // 3
    blank = jnp.zeros((gates, 2 * width), BF16)
    delta_ref[:, : 2 * width] = blank
    delta_ref[:, (rows + 2) * width :] = blank
    bias = jnp.concatenate([b_ref[...]] * step, 1)
    group = 128 // TILE
    states = []
    for start in range(0, rows, step):
        pre = bias
        for row_off in range(3):
            low = (start + row_off) * width
            pre = pre + jnp.dot(
                w_ref[:, row_off * third : (row_off + 1) * third],
                taps_ref[:, low : low + chunk],
                preferred_element_type=F32,
            )
        gate_in = sigmoid(pre[:hid])
        gate_forget = sigmoid(pre[hid : 2 * hid])
        gate_out = sigmoid(pre[2 * hid : 3 * hid])
        candidate = jnp.tanh(pre[3 * hid :])
        lanes = slice(start * width, start * width + chunk)
        cell_in = cell_ref[:, lanes].astype(F32)
        cell_new = gate_forget * cell_in + gate_in * candidate
        squash = jnp.tanh(cell_new)
        hidden_new = live * gate_out * squash
        back_h = live * hcot_ref[:, lanes].astype(F32)
        back_c = live * ccot_ref[:, lanes].astype(F32) + back_h * gate_out * (1.0 - squash * squash)
        cell_back = back_c * gate_forget
        carried = back_c * gate_in
        terms = (
            carried * candidate * (1.0 - gate_in),
            cell_back * cell_in * (1.0 - gate_forget),
            back_h * squash * gate_out * (1.0 - gate_out),
            carried * (1.0 - candidate * candidate),
        )
        low = (start + 2) * width
        for index, term in enumerate(terms):
            delta_ref[index * hid : (index + 1) * hid, low : low + chunk] = term.astype(BF16)
        hidden_new_ref[:, lanes] = hidden_new.astype(BF16)
        cell_back_ref[:, lanes] = cell_back
        for part in range(step):
            piece = slice(part * width, (part + 1) * width)
            states.append(cell_new[:, piece])
        if len(states) == group:
            block_of = lane_index((hid, width)) // TILE
            half = (start + step) // group - 1
            stride = group // 2
            while stride:
                upper = (block_of & stride) != 0
                mixed = list(states)
                for low_index in range(group):
                    if low_index & stride == 0:
                        first, second = states[low_index], states[low_index + stride]
                        mixed[low_index] = jnp.where(
                            upper, pltpu.roll(second, stride * TILE, 1), first
                        )
                        mixed[low_index + stride] = jnp.where(
                            upper, second, pltpu.roll(first, width - stride * TILE, 1)
                        )
                states = mixed
                stride //= 2
            for tile in range(tile_cols):
                tiles_ref[tile, :, half * 128 : (half + 1) * 128] = states[tile].astype(BF16)
            states = []
    delta = delta_ref[:, 2 * width : (rows + 2) * width]
    for row_off in range(3):
        part = lax.dot_general(
            taps_ref[:, row_off * width : (row_off + rows) * width],
            delta,
            (((1,), (1,)), ((), ())),
            preferred_element_type=F32,
        )
        place = slice(row_off * third, (row_off + 1) * third)
        if len(weight_refs) == 1:
            weight_refs[0][place] = part
        else:
            low, high = part[:, : gates // 2], part[:, gates // 2 :]
            weight_refs[0][place] = jnp.where(place_ref[0] == 0, low, high)
            weight_refs[1][place] = jnp.where(place_ref[0] == 0, high, low)


def spread_kernel(place_ref, delta_ref, wt_ref, grad_ref, *rest):
    row_refs, (left_ref, right_ref, side_ref) = rest[:-3], rest[-3:]
    hid = grad_ref.shape[0]
    width = left_ref.shape[1]
    rows = grad_ref.shape[1] // width
    channels = wt_ref.shape[0] // 9
    total = [None] * 3
    for col_off in range(3):
        for row_off in range(3):
            first = (row_off * 3 + col_off + 1) * channels - hid
            low = (2 - row_off) * width
            term = jnp.dot(
                wt_ref[first : first + hid],
                delta_ref[:, low : low + (rows + 2) * width],
                preferred_element_type=F32,
            )
            total[col_off] = term if row_off == 0 else total[col_off] + term
        side_ref[col_off] = total[col_off]
    lane = lane_index((hid, width))
    left = jnp.zeros((hid, width), F32)
    right = jnp.zeros((hid, width), F32)
    ends = []
    for row in range(rows + 2):
        lanes = slice(row * width, (row + 1) * width)
        before = side_ref[0, :, lanes]
        after = side_ref[2, :, lanes]
        slab = (
            side_ref[1, :, lanes]
            + jnp.where(lane == width - 1, 0.0, pltpu.roll(before, width - 1, 1))
            + jnp.where(lane == 0, 0.0, pltpu.roll(after, 1, 1))
        )
        if row in (0, rows + 1):
            corners = jnp.where(lane == 0, before[:, :1], 0.0)
            corners = jnp.where(lane == width - 1, after[:, width - 1 :], corners)
            ends.append((slab, corners))
        else:
            grad_ref[:, (row - 1) * width : row * width] = slab
            left = jnp.where(lane == row - 1, before[:, :1], left)
            right = jnp.where(lane == row - 1, after[:, width - 1 :], right)
    left_ref[...] = left.astype(BF16)
    right_ref[...] = right.astype(BF16)
    if len(row_refs) == 2:
        for index in range(2):
            row_refs[index][...] = jnp.where(
                place_ref[0] == 0, ends[1][index], ends[0][index]
            ).astype(BF16)
    else:
        for end in range(2):
            for index in range(2):
                row_refs[2 * end + index][...] = ends[end][index].astype(BF16)


def finish_kernel(
    place_ref,
    work_ref,
    hidden_new_ref,
    cell_back_ref,
    arrived_ref,
    grad_ref,
    up_ref,
    down_ref,
    up_left_ref,
    up_right_ref,
    down_left_ref,
    down_right_ref,
    left_ref,
    right_ref,
    hidden_next_ref,
    cell_grad_ref,
    cell_next_ref,
    hidden_grad_ref,
    wide_ref,
):
    hid = grad_ref.shape[0]
    width = up_ref.shape[1]
    rows = grad_ref.shape[1] // width
    lane = lane_index((hid, width))
    left = left_ref[...].astype(F32)
    right = right_ref[...].astype(F32)
    ends = {}
    for row, flag, refs in (
        (0, place_ref[2], (up_ref, up_left_ref, up_right_ref)),
        (rows - 1, place_ref[3], (down_ref, down_left_ref, down_right_ref)),
    ):
        slab, before, after = [ref[...].astype(F32) for ref in refs]
        slab = slab + jnp.where(lane == 0, before[:, width - 1 :], 0.0)
        slab = slab + jnp.where(lane == width - 1, after[:, :1], 0.0)
        ends[row] = jnp.where(flag == 1, slab, 0.0)
    for row in range(rows):
        lanes = slice(row * width, (row + 1) * width)
        slab = grad_ref[:, lanes]
        slab = slab + jnp.where(lane == 0, left[:, row : row + 1], 0.0)
        slab = slab + jnp.where(lane == width - 1, right[:, row : row + 1], 0.0)
        if row in ends:
            slab = slab + ends[row]
        hidden_grad_ref[pl.ds(row, hid, stride=rows), :] = slab
        cell_grad_ref[pl.ds(row, hid, stride=rows), :] = cell_back_ref[:, lanes]
        wide_ref[pl.ds(row, hid, stride=rows), :] = hidden_new_ref[:, lanes].astype(F32)
    hidden_next_ref[...] = wide_ref[...].reshape(hid, rows, width).astype(BF16)
    pieces = arrived_ref.shape[2]
    for index in range(cell_next_ref.shape[0]):
        for piece in range(cell_next_ref.shape[2] // pieces):
            cell_next_ref[index, :, piece * pieces : (piece + 1) * pieces] = arrived_ref[
                work_ref[index], piece * hid : (piece + 1) * hid
            ].astype(F32)


def split_bias(block, row):
    index = lax.broadcasted_iota(jnp.int32, block.shape, 0)
    rest = pltpu.roll(block - block.astype(BF16).astype(F32), 1, 0)
    return jnp.where(index == row + 1, rest, block)


def slots_kernel(place_ref, wet_ref, owner_ref, tiles_ref, out_ref):
    tile_cols, hid, cells = tiles_ref.shape
    slots, _, lanes = out_ref.shape
    out_ref[...] = jnp.zeros(out_ref.shape, BF16)
    for tile in range(tile_cols):
        index = place_ref[1] * tile_cols + tile

        @pl.when(wet_ref[0, index] > 0)
        def _():
            for piece in range(cells // lanes):
                out_ref[owner_ref[0, index], piece * hid : (piece + 1) * hid] = tiles_ref[
                    tile, :, piece * lanes : (piece + 1) * lanes
                ]


def pack_kernel(span, count, *refs):
    slots_ref, out_ref, token_ref, share_ref, semaphore = refs[count:]
    token_ref[...] = jnp.zeros(token_ref.shape, F32)
    slots, share, _ = share_ref.shape
    third = refs[0].shape[0] // 3
    total = refs[0][...]
    for ref in refs[1:count]:
        total = total + ref[...]
    total = jnp.concatenate([split_bias(total[:third], span), total[third:]], 0)
    for slot in range(slots):
        share_ref[slot] = total[slot * share : (slot + 1) * share].astype(BF16)
    state_rows = out_ref.shape[1] - share
    copy = pltpu.make_async_copy(share_ref, out_ref.at[:, pl.ds(state_rows, share)], semaphore)
    copy.start()
    copy.wait()


def sum_kernel(scaling, span, state_rows, place_ref, parts_ref, out_ref, token_ref):
    token_ref[...] = jnp.zeros(token_ref.shape, F32)
    total = parts_ref[0, state_rows:].astype(F32)
    for index in range(1, parts_ref.shape[0]):
        total = total + parts_ref[index, state_rows:].astype(F32)
    total = total * scaling
    share = total.shape[0]
    row = span % share
    index = lax.broadcasted_iota(jnp.int32, total.shape, 0)
    whole = jnp.where(index == row, total + pltpu.roll(total, share - 1, 0), total)
    total = jnp.where(place_ref[1] == span // share, split_bias(whole, row), total)
    for index in range(out_ref.shape[0]):
        out_ref[index] = total.astype(BF16)


def weights_kernel(span, place_ref, *refs):
    *parts, weight_ref, bias_ref = refs
    third = parts[0].shape[0] // 3
    half = parts[0].shape[1]
    for side in range(len(parts)):
        if len(parts) == 1:
            pick = parts[0][...]
        else:
            pick = jnp.where(place_ref[0] == side, parts[0][...], parts[1][...])
        pick = pick.astype(F32)
        lanes = slice(side * half, (side + 1) * half)
        for index in range(3):
            weight_ref[index * span : (index + 1) * span, lanes] = pick[
                index * third : index * third + span
            ]
        bias_ref[:, lanes] = pick[span : span + 1] + pick[span + 1 : span + 2]


def moved(values, lat_step, lon_step, lat_devices, lon_devices):
    pairs = []
    for lat in range(lat_devices):
        for lon in range(lon_devices):
            to_lat = lat + lat_step
            if lat_step and lat_devices == 2:
                to_lat = 1 - lat
            if 0 <= to_lat < lat_devices:
                to = to_lat * lon_devices + (lon + lon_step) % lon_devices
                pairs.append((lat * lon_devices + lon, to))
    return lax.ppermute(values, ("lat", "lon"), pairs)


def exchange(ends, corners, left, right, lat_devices, lon_devices):
    def go(values, lat_step, lon_step):
        return moved(values, lat_step, lon_step, lat_devices, lon_devices)

    from_left, from_right = go(right, 0, 1), go(left, 0, -1)
    if lat_devices == 2:
        row = go(ends[0], 1, 0)
        row_left, row_right = go(corners[0], 1, 1), go(corners[0], 1, -1)
        return (row, row, row_left, row_right, row_left, row_right, from_left, from_right)
    return (
        go(ends[1], 1, 0),
        go(ends[0], -1, 0),
        go(corners[1], 1, 1),
        go(corners[1], 1, -1),
        go(corners[0], -1, 1),
        go(corners[0], -1, -1),
        from_left,
        from_right,
    )


def body(forcing, hidden, cell, grad_hidden, grad_cell, wet_mask, tile_owner, w_gates, b_gates):
    lat_index = lax.axis_index("lat")
    lon_index = lax.axis_index("lon")
    lat_devices = lax.axis_size("lat")
    lon_devices = lax.axis_size("lon")
    inp, rows, width = forcing.shape
    hid = hidden.shape[0]
    channels = inp + hid
    gates = w_gates.shape[0]
    span = 3 * channels
    third = (span + 128) // 128 * 128
    cells = rows * width
    tile_cols = width // TILE
    capacity = tile_cols // 2
    place = jnp.stack(
        [
            lat_index,
            lon_index,
            (lat_index > 0).astype(jnp.int32),
            (lat_index < lat_devices - 1).astype(jnp.int32),
        ]
    ).astype(jnp.int32)

    def shaped(*shape, dtype=BF16):
        return jax.ShapeDtypeStruct(shape, dtype)

    end_count = 1 if lat_devices == 2 else 2
    edges = call(
        edges_kernel,
        (shaped(channels, cells),) + (shaped(channels, width),) * (end_count + 2),
        (place, forcing, hidden),
        scalars=1,
        scratch=[pltpu.VMEM((channels * rows, width), F32)],
        moved=4 * channels * cells,
        fetched=2,
    )
    flat, ends, (left, right) = edges[0], edges[1:-2], edges[-2:]
    if lat_devices == 2:
        up = down = moved(ends[0], 1, 0, lat_devices, lon_devices)
    else:
        up = moved(ends[1], 1, 0, lat_devices, lon_devices)
        down = moved(ends[0], -1, 0, lat_devices, lon_devices)
    left, right = call(
        lambda *refs: corners_kernel(rows, *refs),
        (shaped(channels, width),) * 2,
        (up, down, left, right),
        moved=8 * channels * width,
    )
    halo = (
        up,
        down,
        moved(right, 0, 1, lat_devices, lon_devices),
        moved(left, 0, -1, lat_devices, lon_devices),
    )
    w_turned = w_gates.T
    cell_flat, hcot_flat, ccot_flat, w_rows, bias = call(
        flatten_kernel,
        (shaped(hid, cells),) * 3
        + (shaped(gates, 3 * third), shaped(gates, width, dtype=F32)),
        (b_gates.reshape(1, gates), w_turned, cell, grad_hidden, grad_cell),
        scratch=[pltpu.VMEM((hid * rows, width), F32)],
        moved=12 * hid * cells,
        fetched=5,
    )
    halves = 2 if lat_devices == 2 else 1
    lanes = gates // halves
    hidden_new, cell_back, tiles, *weight_parts, delta = call(
        step_kernel,
        (
            shaped(hid, cells),
            shaped(hid, cells, dtype=F32),
            shaped(tile_cols, hid, TILE * TILE),
        )
        + (shaped(3 * third, lanes, dtype=F32),) * halves
        + (shaped(gates, (rows + 4) * width),),
        (place, wet_mask, tile_owner, flat, *halo)
        + (cell_flat, hcot_flat, ccot_flat, w_rows, bias),
        scalars=3,
        scratch=[pltpu.VMEM((third, (rows + 2) * width), BF16)],
        flops=4 * gates * 3 * span * cells,
        moved=16 * hid * cells,
    )
    swap = [(0, 1), (1, 0)]
    if halves == 2:
        weight_parts = (weight_parts[0], lax.ppermute(weight_parts[1], "lat", swap))
    else:
        weight_parts = (lax.psum(weight_parts[0], "lat"),)
    state_rows = hid * TILE * TILE // lanes
    share = 3 * third // lon_devices
    slots = call(
        slots_kernel,
        shaped(lon_devices, state_rows + share, lanes),
        (place, wet_mask, tile_owner, tiles),
        scalars=3,
        moved=4 * lon_devices * hid * TILE * TILE,
    )
    anywhere = pl.BlockSpec(memory_space=pl.ANY)
    count = len(weight_parts)
    outgoing, packed = pl.pallas_call(
        lambda *refs: pack_kernel(span, count, *refs),
        out_shape=(shaped(*slots.shape), shaped(8, 128, dtype=F32)),
        in_specs=[VMEM] * count + [anywhere],
        out_specs=(anywhere, VMEM),
        scratch_shapes=[
            pltpu.VMEM((lon_devices, share, lanes), BF16),
            pltpu.SemaphoreType.DMA(()),
        ],
        input_output_aliases={count: 0},
        compiler_params=pltpu.CompilerParams(vmem_limit_bytes=LIMIT),
        cost_estimate=pl.CostEstimate(
            flops=0, bytes_accessed=8 * gates * 3 * third, transcendentals=0
        ),
    )(*weight_parts, slots)
    incoming = lax.all_to_all(outgoing, "lon", 0, 0, tiled=True)
    grad_parts = call(
        spread_kernel,
        (shaped(hid, cells, dtype=F32),) + (shaped(hid, width),) * (2 * end_count + 2),
        (place, delta, w_turned),
        scalars=1,
        scratch=[pltpu.VMEM((3, hid, (rows + 2) * width), F32)],
        flops=2 * gates * 9 * hid * cells,
        moved=8 * gates * cells,
        after=(packed,),
    )
    grad_flat, grad_ends, grad_sides = grad_parts[0], grad_parts[1:-2], grad_parts[-2:]
    grad_halo = exchange(
        grad_ends[0::2], grad_ends[1::2], *grad_sides, lat_devices, lon_devices
    )
    scaling = 1.0 / math.sqrt(float(lat_devices * lon_devices * capacity * TILE * TILE))
    shares, shared = call(
        lambda *refs: sum_kernel(scaling, span, state_rows, *refs),
        (shaped(lon_devices, share, lanes), shaped(8, 128, dtype=F32)),
        (place, incoming),
        scalars=1,
        moved=2 * gates * 3 * third,
        after=grad_halo,
    )
    owned = (wet_mask > 0) & (tile_owner == lon_index)
    arrived = jnp.any(owned.reshape(lon_devices, tile_cols), 1)
    order = jnp.arange(lon_devices, dtype=jnp.int32)
    rank = jnp.sum((arrived[:, None] & (order[:, None] < order[None, :])).astype(jnp.int32), 0)
    placed = arrived[None, :] & (rank[None, :] == jnp.arange(capacity, dtype=jnp.int32)[:, None])
    work = jnp.sum(jnp.where(placed, order[None, :], 0), 1)
    finished = call(
        finish_kernel,
        (
            shaped(hid, rows, width),
            shaped(hid * rows, width, dtype=F32),
            shaped(capacity, hid, TILE * TILE, dtype=F32),
            shaped(hid * rows, width, dtype=F32),
        ),
        (place, work, hidden_new, cell_back, incoming, grad_flat, *grad_halo),
        scalars=2,
        scratch=[pltpu.VMEM((hid * rows, width), F32)],
        moved=32 * hid * cells,
        after=(shared,),
    )
    gathered = lax.all_to_all(shares, "lon", 0, 0, tiled=True).reshape(3 * third, lanes)
    gathered, finished = lax.optimization_barrier((gathered, finished))
    hidden_next, cell_grad, cell_next, hidden_grad = finished
    gathered = (gathered,)
    if halves == 2:
        gathered += (lax.ppermute(gathered[0], "lat", swap),)
    weight_grad, bias_grad = call(
        lambda *refs: weights_kernel(span, *refs),
        (shaped(3 * span, gates, dtype=F32), shaped(1, gates, dtype=F32)),
        (place, *gathered),
        scalars=1,
        moved=6 * gates * 3 * third,
    )
    return (
        hidden_next,
        cell_next,
        hidden_grad.reshape(hid, rows, width),
        cell_grad.reshape(hid, rows, width),
        weight_grad.T,
        bias_grad.reshape(gates),
    )


def solution(mesh):
    return jax.shard_map(
        body,
        mesh=mesh,
        in_specs=(
            P(None, "lat", "lon"),
            P(None, "lat", "lon"),
            P(None, "lat", "lon"),
            P(None, "lat", "lon"),
            P(None, "lat", "lon"),
            P("lat", None),
            P("lat", None),
            P(),
            P(),
        ),
        out_specs=(
            P(None, "lat", "lon"),
            P(("lat", "lon"), None, None),
            P(None, "lat", "lon"),
            P(None, "lat", "lon"),
            P(),
            P(),
        ),
        check_vma=False,
    )
```

```python
import math

import jax
import jax.numpy as jnp
from jax import lax
from jax.experimental import pallas as pl
from jax.experimental.pallas import tpu as pltpu
from jax.sharding import PartitionSpec as P

TILE = 16
F32 = jnp.float32
BF16 = jnp.bfloat16
LIMIT = 24 * 1024 * 1024
SMEM = pl.BlockSpec(memory_space=pltpu.SMEM)
VMEM = pl.BlockSpec(memory_space=pltpu.VMEM)


def call(kernel, outs, operands, scalars=0, scratch=(), flops=0, moved=0, after=(), fetched=0):
    count = len(operands)
    kept = count - fetched
    total = count + len(after)

    def run(*refs):
        if not fetched:
            kernel(*refs[:count], *refs[total:])
            return
        *rest, semaphores = refs[total:]
        buffers = rest[len(rest) - fetched :]
        copies = [
            pltpu.make_async_copy(source, target, semaphores.at[index])
            for index, (source, target) in enumerate(zip(refs[kept:count], buffers))
        ]
        for copy in copies:
            copy.start()
        waits = [copy.wait for copy in copies]
        kernel(waits, *refs[:kept], *buffers, *rest[: len(rest) - fetched])

    scratch = list(scratch)
    operands = list(operands)
    for index in range(kept, count):
        operands[index] = pltpu.with_memory_space_constraint(operands[index], pltpu.HBM)
    if fetched:
        scratch += [pltpu.VMEM(leaf.shape, leaf.dtype) for leaf in operands[kept:]]
        scratch.append(pltpu.SemaphoreType.DMA((fetched,)))

    return pl.pallas_call(
        run,
        out_shape=outs,
        in_specs=[SMEM] * scalars
        + [VMEM] * (kept - scalars)
        + [pl.BlockSpec(memory_space=pltpu.HBM)] * fetched
        + [VMEM] * len(after),
        out_specs=jax.tree.map(lambda _: VMEM, outs),
        scratch_shapes=scratch,
        compiler_params=pltpu.CompilerParams(vmem_limit_bytes=LIMIT),
        cost_estimate=pl.CostEstimate(flops=flops, bytes_accessed=moved, transcendentals=0),
    )(*operands, *after)


def lane_index(shape):
    return lax.broadcasted_iota(jnp.int32, shape, 1)


def sigmoid(values):
    return 0.5 * jnp.tanh(0.5 * values) + 0.5


def edges_kernel(waits, place_ref, forcing_ref, hidden_ref, *rest):
    row_refs, (left_ref, right_ref, wide_ref) = rest[:-3], rest[-3:]
    inp, rows, width = forcing_ref.shape
    channels = inp + hidden_ref.shape[0]
    for wait in waits:
        wait()
    wide_ref[: inp * rows] = forcing_ref[...].astype(F32).reshape(inp * rows, width)
    wide_ref[inp * rows :] = hidden_ref[...].astype(F32).reshape((channels - inp) * rows, width)
    lane = lane_index((channels, width))
    left = jnp.zeros((channels, width), F32)
    right = jnp.zeros((channels, width), F32)
    ends = []
    for row in range(rows):
        slab = wide_ref[pl.ds(row, channels, stride=rows), :]
        left = jnp.where(lane == row, slab[:, :1], left)
        right = jnp.where(lane == row, slab[:, width - 1 :], right)
        if row in (0, rows - 1):
            ends.append(slab)
    left_ref[...] = left.astype(BF16)
    right_ref[...] = right.astype(BF16)
    if len(row_refs) == 1:
        row_refs[0][...] = jnp.where(place_ref[0] == 0, ends[-1], ends[0]).astype(BF16)
    else:
        row_refs[0][...] = ends[0].astype(BF16)
        row_refs[1][...] = ends[-1].astype(BF16)


def middle_kernel(
    waits,
    place_ref,
    up_ref,
    down_ref,
    b_ref,
    wt_ref,
    forcing_ref,
    hidden_ref,
    cell_ref,
    hcot_ref,
    ccot_ref,
    cell_out,
    hcot_out,
    ccot_out,
    taps_ref,
    pre_ref,
    sides_ref,
    w_ref,
    fields_ref,
    wide_ref,
):
    hid, rows, width = cell_ref.shape
    gates = wt_ref.shape[1]
    span = wt_ref.shape[0] // 3
    third = w_ref.shape[1] // 3
    inp = forcing_ref.shape[0]
    channels = inp + hid
    wait_b, wait_w, wait_forcing, wait_hidden, *wait_cells = waits
    wait_b()
    bias = jnp.broadcast_to(b_ref[...], (width, gates)).T
    wait_w()
    blank = jnp.zeros((third - span, gates), F32)

    def turned(blocks):
        blocks = [block.astype(F32) for block in blocks]
        return jnp.concatenate(blocks + [blank], 0).T.astype(BF16)

    for index in range(3):
        w_ref[:, index * third : (index + 1) * third] = turned(
            [wt_ref[index * span : (index + 1) * span]]
        )
    for side, tap in enumerate((0, 2)):
        starts = [index * span + tap * channels for index in range(3)]
        sides_ref[side] = turned([wt_ref[first : first + channels] for first in starts])
    wait_forcing()
    fields_ref[: inp * rows] = forcing_ref[...].astype(F32).reshape(inp * rows, width)
    wait_hidden()
    fields_ref[inp * rows :] = hidden_ref[...].astype(F32).reshape(hid * rows, width)
    lane = lane_index((channels, width))

    def put(row, slab):
        lanes = slice(row * width, (row + 1) * width)
        shifted = jnp.where(lane == 0, 0.0, pltpu.roll(slab, 1, 1))
        taps_ref[0:channels, lanes] = shifted.astype(BF16)
        taps_ref[channels : 2 * channels, lanes] = slab.astype(BF16)
        shifted = jnp.where(lane == width - 1, 0.0, pltpu.roll(slab, width - 1, 1))
        taps_ref[2 * channels : span, lanes] = shifted.astype(BF16)

    put(0, jnp.where(place_ref[2] == 1, up_ref[...].astype(F32), 0.0))
    put(rows + 1, jnp.where(place_ref[3] == 1, down_ref[...].astype(F32), 0.0))
    for row in range(rows):
        put(row + 1, fields_ref[pl.ds(row, channels, stride=rows), :])
    ones = lax.broadcasted_iota(jnp.int32, (third - span, taps_ref.shape[1]), 0) == 0
    taps_ref[span:] = jnp.where(ones, 1.0, 0.0).astype(BF16)
    step = 2 if rows % 2 == 0 else 1
    chunk = step * width
    bias = jnp.concatenate([bias] * step, 1)
    for start in range(0, rows, step):
        pre = bias
        for row_off in range(3):
            low = (start + row_off) * width
            pre = pre + jnp.dot(
                w_ref[:, row_off * third : (row_off + 1) * third],
                taps_ref[:, low : low + chunk],
                preferred_element_type=F32,
            )
        pre_ref[:, start * width : start * width + chunk] = pre
    for wait, source, target in zip(
        wait_cells, (cell_ref, hcot_ref, ccot_ref), (cell_out, hcot_out, ccot_out)
    ):
        wait()
        wide_ref[...] = source[...].astype(F32).reshape(hid * rows, width)
        for row in range(rows):
            target[:, row * width : (row + 1) * width] = wide_ref[
                pl.ds(row, hid, stride=rows), :
            ].astype(BF16)


def corners_kernel(rows, up_ref, down_ref, left_ref, right_ref, left_out, right_out):
    lane = lane_index(left_ref.shape)
    width = up_ref.shape[1]
    up = up_ref[...].astype(F32)
    down = down_ref[...].astype(F32)
    for column, source, target in ((0, left_ref, left_out), (width - 1, right_ref, right_out)):
        values = source[...].astype(F32)
        values = jnp.where(lane == rows, up[:, column : column + 1], values)
        values = jnp.where(lane == rows + 1, down[:, column : column + 1], values)
        target[...] = values.astype(BF16)


def step_kernel(
    place_ref,
    wet_ref,
    left_ref,
    right_ref,
    cell_ref,
    hcot_ref,
    ccot_ref,
    early_ref,
    pre_ref,
    sides_ref,
    hidden_new_ref,
    cell_back_ref,
    tiles_ref,
    *rest,
):
    weight_refs, (delta_ref, taps_ref) = rest[:-2], rest[-2:]
    channels, width = left_ref.shape
    hid = cell_ref.shape[0]
    gates = pre_ref.shape[0]
    rows = pre_ref.shape[1] // width
    tile_cols = width // TILE
    span = 3 * channels
    third = early_ref.shape[0]
    first_tile = place_ref[1] * tile_cols
    lane = lane_index((channels, width))
    taps_ref[...] = early_ref[...]
    fixes = []
    for side, ref in enumerate((left_ref, right_ref)):
        halo = ref[...].astype(F32)
        above = jnp.where(place_ref[2] == 1, halo[:, rows : rows + 1], 0.0)
        below = jnp.where(place_ref[3] == 1, halo[:, rows + 1 : rows + 2], 0.0)
        column = jnp.where(lane == 0, above, pltpu.roll(halo, 1, 1))
        column = jnp.where(lane == rows + 1, below, column)
        place = slice(2 * side * channels, (2 * side + 1) * channels)
        edge = side * (width - 1)
        for row in range(rows + 2):
            lanes = slice(row * width, (row + 1) * width)
            slab = early_ref[place, lanes].astype(F32)
            slab = jnp.where(lane == edge, column[:, row : row + 1], slab)
            taps_ref[place, lanes] = slab.astype(BF16)
        parts = [column] + [pltpu.roll(column, width - row_off, 1) for row_off in (1, 2)]
        parts.append(jnp.zeros((third - span, width), F32))
        fixes.append(
            jnp.dot(
                sides_ref[side],
                jnp.concatenate(parts, 0).astype(BF16),
                preferred_element_type=F32,
            )
        )
    gate_lane = lane_index((gates, width))

    live = jnp.zeros((1, width), F32)
    live_lane = lane_index((1, width)) // TILE
    for tile in range(tile_cols):
        wet = (wet_ref[0, first_tile + tile] > 0).astype(F32)
        live = jnp.where(live_lane == tile, wet, live)
    step = 2 if rows % 2 == 0 else 1
    chunk = step * width
    live = jnp.concatenate([live] * step, 1)
    blank = jnp.zeros((gates, 2 * width), BF16)
    delta_ref[:, : 2 * width] = blank
    delta_ref[:, (rows + 2) * width :] = blank
    group = 128 // TILE
    states = []
    for start in range(0, rows, step):
        pre = []
        for row in range(start, start + step):
            part = pre_ref[:, row * width : (row + 1) * width]
            part = part + jnp.where(gate_lane == 0, fixes[0][:, row : row + 1], 0.0)
            part = part + jnp.where(gate_lane == width - 1, fixes[1][:, row : row + 1], 0.0)
            pre.append(part)
        pre = jnp.concatenate(pre, 1)
        gate_in = sigmoid(pre[:hid])
        gate_forget = sigmoid(pre[hid : 2 * hid])
        gate_out = sigmoid(pre[2 * hid : 3 * hid])
        candidate = jnp.tanh(pre[3 * hid :])
        lanes = slice(start * width, start * width + chunk)
        cell_in = cell_ref[:, lanes].astype(F32)
        cell_new = gate_forget * cell_in + gate_in * candidate
        squash = jnp.tanh(cell_new)
        hidden_new = live * gate_out * squash
        back_h = live * hcot_ref[:, lanes].astype(F32)
        back_c = live * ccot_ref[:, lanes].astype(F32) + back_h * gate_out * (1.0 - squash * squash)
        cell_back = back_c * gate_forget
        carried = back_c * gate_in
        terms = (
            carried * candidate * (1.0 - gate_in),
            cell_back * cell_in * (1.0 - gate_forget),
            back_h * squash * gate_out * (1.0 - gate_out),
            carried * (1.0 - candidate * candidate),
        )
        low = (start + 2) * width
        for index, term in enumerate(terms):
            delta_ref[index * hid : (index + 1) * hid, low : low + chunk] = term.astype(BF16)
        hidden_new_ref[:, lanes] = hidden_new.astype(BF16)
        cell_back_ref[:, lanes] = cell_back
        for part in range(step):
            piece = slice(part * width, (part + 1) * width)
            states.append(cell_new[:, piece])
        if len(states) == group:
            block_of = lane_index((hid, width)) // TILE
            half = (start + step) // group - 1
            stride = group // 2
            while stride:
                upper = (block_of & stride) != 0
                mixed = list(states)
                for low_index in range(group):
                    if low_index & stride == 0:
                        first, second = states[low_index], states[low_index + stride]
                        mixed[low_index] = jnp.where(
                            upper, pltpu.roll(second, stride * TILE, 1), first
                        )
                        mixed[low_index + stride] = jnp.where(
                            upper, second, pltpu.roll(first, width - stride * TILE, 1)
                        )
                states = mixed
                stride //= 2
            for tile in range(tile_cols):
                tiles_ref[tile, :, half * 128 : (half + 1) * 128] = states[tile].astype(BF16)
            states = []
    delta = delta_ref[:, 2 * width : (rows + 2) * width]
    for row_off in range(3):
        part = lax.dot_general(
            taps_ref[:, row_off * width : (row_off + rows) * width],
            delta,
            (((1,), (1,)), ((), ())),
            preferred_element_type=F32,
        )
        place = slice(row_off * third, (row_off + 1) * third)
        if len(weight_refs) == 1:
            weight_refs[0][place] = part
        else:
            low, high = part[:, : gates // 2], part[:, gates // 2 :]
            weight_refs[0][place] = jnp.where(place_ref[0] == 0, low, high)
            weight_refs[1][place] = jnp.where(place_ref[0] == 0, high, low)


def spread_kernel(place_ref, delta_ref, wt_ref, grad_ref, *rest):
    row_refs, (left_ref, right_ref, side_ref) = rest[:-3], rest[-3:]
    hid = grad_ref.shape[0]
    width = left_ref.shape[1]
    rows = grad_ref.shape[1] // width
    channels = wt_ref.shape[0] // 9
    total = [None] * 3
    for col_off in range(3):
        for row_off in range(3):
            first = (row_off * 3 + col_off + 1) * channels - hid
            low = (2 - row_off) * width
            term = jnp.dot(
                wt_ref[first : first + hid],
                delta_ref[:, low : low + (rows + 2) * width],
                preferred_element_type=F32,
            )
            total[col_off] = term if row_off == 0 else total[col_off] + term
        side_ref[col_off] = total[col_off]
    lane = lane_index((hid, width))
    left = jnp.zeros((hid, width), F32)
    right = jnp.zeros((hid, width), F32)
    ends = []
    for row in range(rows + 2):
        lanes = slice(row * width, (row + 1) * width)
        before = side_ref[0, :, lanes]
        after = side_ref[2, :, lanes]
        slab = (
            side_ref[1, :, lanes]
            + jnp.where(lane == width - 1, 0.0, pltpu.roll(before, width - 1, 1))
            + jnp.where(lane == 0, 0.0, pltpu.roll(after, 1, 1))
        )
        if row in (0, rows + 1):
            corners = jnp.where(lane == 0, before[:, :1], 0.0)
            corners = jnp.where(lane == width - 1, after[:, width - 1 :], corners)
            ends.append((slab, corners))
        else:
            grad_ref[:, (row - 1) * width : row * width] = slab
            left = jnp.where(lane == row - 1, before[:, :1], left)
            right = jnp.where(lane == row - 1, after[:, width - 1 :], right)
    left_ref[...] = left.astype(BF16)
    right_ref[...] = right.astype(BF16)
    if len(row_refs) == 2:
        for index in range(2):
            row_refs[index][...] = jnp.where(
                place_ref[0] == 0, ends[1][index], ends[0][index]
            ).astype(BF16)
    else:
        for end in range(2):
            for index in range(2):
                row_refs[2 * end + index][...] = ends[end][index].astype(BF16)


def finish_kernel(
    place_ref,
    work_ref,
    hidden_new_ref,
    cell_back_ref,
    arrived_ref,
    grad_ref,
    up_ref,
    down_ref,
    up_left_ref,
    up_right_ref,
    down_left_ref,
    down_right_ref,
    left_ref,
    right_ref,
    hidden_next_ref,
    cell_grad_ref,
    cell_next_ref,
    hidden_grad_ref,
    wide_ref,
):
    hid = grad_ref.shape[0]
    width = up_ref.shape[1]
    rows = grad_ref.shape[1] // width
    lane = lane_index((hid, width))
    left = left_ref[...].astype(F32)
    right = right_ref[...].astype(F32)
    ends = {}
    for row, flag, refs in (
        (0, place_ref[2], (up_ref, up_left_ref, up_right_ref)),
        (rows - 1, place_ref[3], (down_ref, down_left_ref, down_right_ref)),
    ):
        slab, before, after = [ref[...].astype(F32) for ref in refs]
        slab = slab + jnp.where(lane == 0, before[:, width - 1 :], 0.0)
        slab = slab + jnp.where(lane == width - 1, after[:, :1], 0.0)
        ends[row] = jnp.where(flag == 1, slab, 0.0)
    for row in range(rows):
        lanes = slice(row * width, (row + 1) * width)
        slab = grad_ref[:, lanes]
        slab = slab + jnp.where(lane == 0, left[:, row : row + 1], 0.0)
        slab = slab + jnp.where(lane == width - 1, right[:, row : row + 1], 0.0)
        if row in ends:
            slab = slab + ends[row]
        hidden_grad_ref[pl.ds(row, hid, stride=rows), :] = slab
        cell_grad_ref[pl.ds(row, hid, stride=rows), :] = cell_back_ref[:, lanes]
        wide_ref[pl.ds(row, hid, stride=rows), :] = hidden_new_ref[:, lanes].astype(F32)
    hidden_next_ref[...] = wide_ref[...].reshape(hid, rows, width).astype(BF16)
    pieces = arrived_ref.shape[2]
    for index in range(cell_next_ref.shape[0]):
        for piece in range(cell_next_ref.shape[2] // pieces):
            cell_next_ref[index, :, piece * pieces : (piece + 1) * pieces] = arrived_ref[
                work_ref[index], piece * hid : (piece + 1) * hid
            ].astype(F32)


def split_bias(block, row):
    index = lax.broadcasted_iota(jnp.int32, block.shape, 0)
    rest = pltpu.roll(block - block.astype(BF16).astype(F32), 1, 0)
    return jnp.where(index == row + 1, rest, block)


def slots_kernel(place_ref, wet_ref, owner_ref, tiles_ref, out_ref):
    tile_cols, hid, cells = tiles_ref.shape
    slots, _, lanes = out_ref.shape
    out_ref[...] = jnp.zeros(out_ref.shape, BF16)
    for tile in range(tile_cols):
        index = place_ref[1] * tile_cols + tile

        @pl.when(wet_ref[0, index] > 0)
        def _():
            for piece in range(cells // lanes):
                out_ref[owner_ref[0, index], piece * hid : (piece + 1) * hid] = tiles_ref[
                    tile, :, piece * lanes : (piece + 1) * lanes
                ]


def pack_kernel(span, count, *refs):
    slots_ref, out_ref, token_ref, share_ref, semaphore = refs[count:]
    token_ref[...] = jnp.zeros(token_ref.shape, F32)
    slots, share, _ = share_ref.shape
    third = refs[0].shape[0] // 3
    total = refs[0][...]
    for ref in refs[1:count]:
        total = total + ref[...]
    total = jnp.concatenate([split_bias(total[:third], span), total[third:]], 0)
    for slot in range(slots):
        share_ref[slot] = total[slot * share : (slot + 1) * share].astype(BF16)
    state_rows = out_ref.shape[1] - share
    copy = pltpu.make_async_copy(share_ref, out_ref.at[:, pl.ds(state_rows, share)], semaphore)
    copy.start()
    copy.wait()


def sum_kernel(scaling, span, state_rows, place_ref, parts_ref, out_ref, token_ref):
    token_ref[...] = jnp.zeros(token_ref.shape, F32)
    total = parts_ref[0, state_rows:].astype(F32)
    for index in range(1, parts_ref.shape[0]):
        total = total + parts_ref[index, state_rows:].astype(F32)
    total = total * scaling
    share = total.shape[0]
    row = span % share
    index = lax.broadcasted_iota(jnp.int32, total.shape, 0)
    whole = jnp.where(index == row, total + pltpu.roll(total, share - 1, 0), total)
    total = jnp.where(place_ref[1] == span // share, split_bias(whole, row), total)
    for index in range(out_ref.shape[0]):
        out_ref[index] = total.astype(BF16)


def weights_kernel(span, place_ref, *refs):
    *parts, weight_ref, bias_ref = refs
    third = parts[0].shape[0] // 3
    half = parts[0].shape[1]
    for side in range(len(parts)):
        if len(parts) == 1:
            pick = parts[0][...]
        else:
            pick = jnp.where(place_ref[0] == side, parts[0][...], parts[1][...])
        pick = pick.astype(F32)
        lanes = slice(side * half, (side + 1) * half)
        for index in range(3):
            weight_ref[index * span : (index + 1) * span, lanes] = pick[
                index * third : index * third + span
            ]
        bias_ref[:, lanes] = pick[span : span + 1] + pick[span + 1 : span + 2]


def moved(values, lat_step, lon_step, lat_devices, lon_devices):
    pairs = []
    for lat in range(lat_devices):
        for lon in range(lon_devices):
            to_lat = lat + lat_step
            if lat_step and lat_devices == 2:
                to_lat = 1 - lat
            if 0 <= to_lat < lat_devices:
                to = to_lat * lon_devices + (lon + lon_step) % lon_devices
                pairs.append((lat * lon_devices + lon, to))
    return lax.ppermute(values, ("lat", "lon"), pairs)


def exchange(ends, corners, left, right, lat_devices, lon_devices):
    def go(values, lat_step, lon_step):
        return moved(values, lat_step, lon_step, lat_devices, lon_devices)

    from_left, from_right = go(right, 0, 1), go(left, 0, -1)
    if lat_devices == 2:
        row = go(ends[0], 1, 0)
        row_left, row_right = go(corners[0], 1, 1), go(corners[0], 1, -1)
        return (row, row, row_left, row_right, row_left, row_right, from_left, from_right)
    return (
        go(ends[1], 1, 0),
        go(ends[0], -1, 0),
        go(corners[1], 1, 1),
        go(corners[1], 1, -1),
        go(corners[0], -1, 1),
        go(corners[0], -1, -1),
        from_left,
        from_right,
    )


def body(forcing, hidden, cell, grad_hidden, grad_cell, wet_mask, tile_owner, w_gates, b_gates):
    lat_index = lax.axis_index("lat")
    lon_index = lax.axis_index("lon")
    lat_devices = lax.axis_size("lat")
    lon_devices = lax.axis_size("lon")
    inp, rows, width = forcing.shape
    hid = hidden.shape[0]
    channels = inp + hid
    gates = w_gates.shape[0]
    span = 3 * channels
    third = (span + 128) // 128 * 128
    cells = rows * width
    tile_cols = width // TILE
    capacity = tile_cols // 2
    place = jnp.stack(
        [
            lat_index,
            lon_index,
            (lat_index > 0).astype(jnp.int32),
            (lat_index < lat_devices - 1).astype(jnp.int32),
        ]
    ).astype(jnp.int32)

    def shaped(*shape, dtype=BF16):
        return jax.ShapeDtypeStruct(shape, dtype)

    end_count = 1 if lat_devices == 2 else 2
    edges = call(
        edges_kernel,
        (shaped(channels, width),) * (end_count + 2),
        (place, forcing, hidden),
        scalars=1,
        scratch=[pltpu.VMEM((channels * rows, width), F32)],
        moved=4 * channels * cells,
        fetched=2,
    )
    ends, (left, right) = edges[:-2], edges[-2:]
    if lat_devices == 2:
        up = down = moved(ends[0], 1, 0, lat_devices, lon_devices)
    else:
        up = moved(ends[1], 1, 0, lat_devices, lon_devices)
        down = moved(ends[0], -1, 0, lat_devices, lon_devices)
    left, right = call(
        lambda *refs: corners_kernel(rows, *refs),
        (shaped(channels, width),) * 2,
        (up, down, left, right),
        moved=8 * channels * width,
    )
    halo = (
        moved(right, 0, 1, lat_devices, lon_devices),
        moved(left, 0, -1, lat_devices, lon_devices),
    )
    w_turned = w_gates.T
    early = call(
        middle_kernel,
        (shaped(hid, cells),) * 3
        + (
            shaped(third, (rows + 2) * width),
            shaped(gates, cells, dtype=F32),
            shaped(2, gates, third),
        ),
        (place, up, down)
        + (b_gates.reshape(1, gates), w_turned, forcing, hidden, cell, grad_hidden, grad_cell),
        scalars=1,
        scratch=[
            pltpu.VMEM((gates, 3 * third), BF16),
            pltpu.VMEM((channels * rows, width), F32),
            pltpu.VMEM((hid * rows, width), F32),
        ],
        flops=2 * gates * 3 * span * cells,
        moved=12 * hid * cells,
        fetched=7,
    )
    halves = 2 if lat_devices == 2 else 1
    lanes = gates // halves
    hidden_new, cell_back, tiles, *weight_parts, delta = call(
        step_kernel,
        (
            shaped(hid, cells),
            shaped(hid, cells, dtype=F32),
            shaped(tile_cols, hid, TILE * TILE),
        )
        + (shaped(3 * third, lanes, dtype=F32),) * halves
        + (shaped(gates, (rows + 4) * width),),
        (place, wet_mask, *halo, *early),
        scalars=2,
        scratch=[pltpu.VMEM((third, (rows + 2) * width), BF16)],
        flops=2 * gates * 3 * span * cells,
        moved=16 * hid * cells,
    )
    swap = [(0, 1), (1, 0)]
    if halves == 2:
        weight_parts = (weight_parts[0], lax.ppermute(weight_parts[1], "lat", swap))
    else:
        weight_parts = (lax.psum(weight_parts[0], "lat"),)
    state_rows = hid * TILE * TILE // lanes
    share = 3 * third // lon_devices
    slots = call(
        slots_kernel,
        shaped(lon_devices, state_rows + share, lanes),
        (place, wet_mask, tile_owner, tiles),
        scalars=3,
        moved=4 * lon_devices * hid * TILE * TILE,
    )
    anywhere = pl.BlockSpec(memory_space=pl.ANY)
    count = len(weight_parts)
    outgoing, packed = pl.pallas_call(
        lambda *refs: pack_kernel(span, count, *refs),
        out_shape=(shaped(*slots.shape), shaped(8, 128, dtype=F32)),
        in_specs=[VMEM] * count + [anywhere],
        out_specs=(anywhere, VMEM),
        scratch_shapes=[
            pltpu.VMEM((lon_devices, share, lanes), BF16),
            pltpu.SemaphoreType.DMA(()),
        ],
        input_output_aliases={count: 0},
        compiler_params=pltpu.CompilerParams(vmem_limit_bytes=LIMIT),
        cost_estimate=pl.CostEstimate(
            flops=0, bytes_accessed=8 * gates * 3 * third, transcendentals=0
        ),
    )(*weight_parts, slots)
    incoming = lax.all_to_all(outgoing, "lon", 0, 0, tiled=True)
    grad_parts = call(
        spread_kernel,
        (shaped(hid, cells, dtype=F32),) + (shaped(hid, width),) * (2 * end_count + 2),
        (place, delta, w_turned),
        scalars=1,
        scratch=[pltpu.VMEM((3, hid, (rows + 2) * width), F32)],
        flops=2 * gates * 9 * hid * cells,
        moved=8 * gates * cells,
        after=(packed,),
    )
    grad_flat, grad_ends, grad_sides = grad_parts[0], grad_parts[1:-2], grad_parts[-2:]
    grad_halo = exchange(
        grad_ends[0::2], grad_ends[1::2], *grad_sides, lat_devices, lon_devices
    )
    scaling = 1.0 / math.sqrt(float(lat_devices * lon_devices * capacity * TILE * TILE))
    shares, shared = call(
        lambda *refs: sum_kernel(scaling, span, state_rows, *refs),
        (shaped(lon_devices, share, lanes), shaped(8, 128, dtype=F32)),
        (place, incoming),
        scalars=1,
        moved=2 * gates * 3 * third,
        after=grad_halo,
    )
    owned = (wet_mask > 0) & (tile_owner == lon_index)
    arrived = jnp.any(owned.reshape(lon_devices, tile_cols), 1)
    order = jnp.arange(lon_devices, dtype=jnp.int32)
    rank = jnp.sum((arrived[:, None] & (order[:, None] < order[None, :])).astype(jnp.int32), 0)
    placed = arrived[None, :] & (rank[None, :] == jnp.arange(capacity, dtype=jnp.int32)[:, None])
    work = jnp.sum(jnp.where(placed, order[None, :], 0), 1)
    finished = call(
        finish_kernel,
        (
            shaped(hid, rows, width),
            shaped(hid * rows, width, dtype=F32),
            shaped(capacity, hid, TILE * TILE, dtype=F32),
            shaped(hid * rows, width, dtype=F32),
        ),
        (place, work, hidden_new, cell_back, incoming, grad_flat, *grad_halo),
        scalars=2,
        scratch=[pltpu.VMEM((hid * rows, width), F32)],
        moved=32 * hid * cells,
        after=(shared,),
    )
    gathered = lax.all_to_all(shares, "lon", 0, 0, tiled=True).reshape(3 * third, lanes)
    gathered, finished = lax.optimization_barrier((gathered, finished))
    hidden_next, cell_grad, cell_next, hidden_grad = finished
    gathered = (gathered,)
    if halves == 2:
        gathered += (lax.ppermute(gathered[0], "lat", swap),)
    weight_grad, bias_grad = call(
        lambda *refs: weights_kernel(span, *refs),
        (shaped(3 * span, gates, dtype=F32), shaped(1, gates, dtype=F32)),
        (place, *gathered),
        scalars=1,
        moved=6 * gates * 3 * third,
    )
    return (
        hidden_next,
        cell_next,
        hidden_grad.reshape(hid, rows, width),
        cell_grad.reshape(hid, rows, width),
        weight_grad.T,
        bias_grad.reshape(gates),
    )


def solution(mesh):
    return jax.shard_map(
        body,
        mesh=mesh,
        in_specs=(
            P(None, "lat", "lon"),
            P(None, "lat", "lon"),
            P(None, "lat", "lon"),
            P(None, "lat", "lon"),
            P(None, "lat", "lon"),
            P("lat", None),
            P("lat", None),
            P(),
            P(),
        ),
        out_specs=(
            P(None, "lat", "lon"),
            P(("lat", "lon"), None, None),
            P(None, "lat", "lon"),
            P(None, "lat", "lon"),
            P(),
            P(),
        ),
        check_vma=False,
    )
```

```python
import math

import jax
import jax.numpy as jnp
from jax import lax
from jax.experimental import pallas as pl
from jax.experimental.pallas import tpu as pltpu
from jax.sharding import PartitionSpec as P

TILE = 16
F32 = jnp.float32
BF16 = jnp.bfloat16
LIMIT = 48 * 1024 * 1024
SMEM = pl.BlockSpec(memory_space=pltpu.SMEM)
VMEM = pl.BlockSpec(memory_space=pltpu.VMEM)


def call(kernel, outs, operands, scalars=0, scratch=(), flops=0, moved=0, after=(), fetched=0):
    count = len(operands)
    kept = count - fetched
    total = count + len(after)

    def run(*refs):
        if not fetched:
            kernel(*refs[:count], *refs[total:])
            return
        *rest, semaphores = refs[total:]
        buffers = rest[len(rest) - fetched :]
        copies = [
            pltpu.make_async_copy(source, target, semaphores.at[index])
            for index, (source, target) in enumerate(zip(refs[kept:count], buffers))
        ]
        for copy in copies:
            copy.start()
        waits = [copy.wait for copy in copies]
        kernel(waits, *refs[:kept], *buffers, *rest[: len(rest) - fetched])

    scratch = list(scratch)
    operands = list(operands)
    for index in range(kept, count):
        operands[index] = pltpu.with_memory_space_constraint(operands[index], pltpu.HBM)
    if fetched:
        scratch += [pltpu.VMEM(leaf.shape, leaf.dtype) for leaf in operands[kept:]]
        scratch.append(pltpu.SemaphoreType.DMA((fetched,)))

    return pl.pallas_call(
        run,
        out_shape=outs,
        in_specs=[SMEM] * scalars
        + [VMEM] * (kept - scalars)
        + [pl.BlockSpec(memory_space=pltpu.HBM)] * fetched
        + [VMEM] * len(after),
        out_specs=jax.tree.map(lambda _: VMEM, outs),
        scratch_shapes=scratch,
        compiler_params=pltpu.CompilerParams(vmem_limit_bytes=LIMIT),
        cost_estimate=pl.CostEstimate(flops=flops, bytes_accessed=moved, transcendentals=0),
    )(*operands, *after)


def lane_index(shape):
    return lax.broadcasted_iota(jnp.int32, shape, 1)


def sigmoid(values):
    return 0.5 * jnp.tanh(0.5 * values) + 0.5


def edges_kernel(waits, place_ref, forcing_ref, hidden_ref, wide_ref, *row_refs):
    inp, rows, width = forcing_ref.shape
    channels = inp + hidden_ref.shape[0]
    for wait in waits:
        wait()
    wide_ref[: inp * rows] = forcing_ref[...].astype(F32).reshape(inp * rows, width)
    wide_ref[inp * rows :] = hidden_ref[...].astype(F32).reshape((channels - inp) * rows, width)
    ends = [wide_ref[pl.ds(row, channels, stride=rows), :] for row in (0, rows - 1)]
    if len(row_refs) == 1:
        row_refs[0][...] = jnp.where(place_ref[0] == 0, ends[1], ends[0]).astype(BF16)
    else:
        for ref, end in zip(row_refs, ends):
            ref[...] = end.astype(BF16)


def columns_kernel(wide_ref, flat_ref, left_ref, right_ref):
    channels, width = left_ref.shape
    rows = wide_ref.shape[0] // channels
    lane = lane_index((channels, width))
    left = jnp.zeros((channels, width), F32)
    right = jnp.zeros((channels, width), F32)
    for row in range(rows):
        slab = wide_ref[pl.ds(row, channels, stride=rows), :]
        flat_ref[:, row * width : (row + 1) * width] = slab.astype(BF16)
        left = jnp.where(lane == row, slab[:, :1], left)
        right = jnp.where(lane == row, slab[:, width - 1 :], right)
    left_ref[...] = left.astype(BF16)
    right_ref[...] = right.astype(BF16)


def flatten_kernel(
    waits,
    b_ref,
    wt_ref,
    cell_ref,
    hcot_ref,
    ccot_ref,
    cell_out,
    hcot_out,
    ccot_out,
    w_ref,
    bias_ref,
    wide_ref,
):
    hid, rows, width = cell_ref.shape
    gates = wt_ref.shape[1]
    span = wt_ref.shape[0] // 3
    third = w_ref.shape[1] // 3
    waits[0]()
    bias_ref[...] = jnp.broadcast_to(b_ref[...], (bias_ref.shape[1], gates)).T
    waits[1]()
    blank = jnp.zeros((third - span, gates), F32)
    for index in range(3):
        block = wt_ref[index * span : (index + 1) * span].astype(F32)
        w_ref[:, index * third : (index + 1) * third] = (
            jnp.concatenate([block, blank], 0).T.astype(BF16)
        )
    for wait, source, target in zip(
        waits[2:], (cell_ref, hcot_ref, ccot_ref), (cell_out, hcot_out, ccot_out)
    ):
        wait()
        wide_ref[...] = source[...].astype(F32).reshape(hid * rows, width)
        for row in range(rows):
            target[:, row * width : (row + 1) * width] = wide_ref[
                pl.ds(row, hid, stride=rows), :
            ].astype(BF16)


def corners_kernel(rows, up_ref, down_ref, left_ref, right_ref, left_out, right_out):
    lane = lane_index(left_ref.shape)
    width = up_ref.shape[1]
    up = up_ref[...].astype(F32)
    down = down_ref[...].astype(F32)
    for column, source, target in ((0, left_ref, left_out), (width - 1, right_ref, right_out)):
        values = source[...].astype(F32)
        values = jnp.where(lane == rows, up[:, column : column + 1], values)
        values = jnp.where(lane == rows + 1, down[:, column : column + 1], values)
        target[...] = values.astype(BF16)


def step_kernel(
    place_ref,
    wet_ref,
    owner_ref,
    flat_ref,
    up_ref,
    down_ref,
    left_ref,
    right_ref,
    cell_ref,
    hcot_ref,
    ccot_ref,
    w_ref,
    b_ref,
    hidden_new_ref,
    cell_back_ref,
    tiles_ref,
    *rest,
):
    weight_refs, (delta_ref, taps_ref) = rest[:-2], rest[-2:]
    channels = flat_ref.shape[0]
    hid = cell_ref.shape[0]
    gates = w_ref.shape[0]
    width = up_ref.shape[1]
    rows = flat_ref.shape[1] // width
    tile_cols = width // TILE
    span = 3 * channels
    first_tile = place_ref[1] * tile_cols
    lane = lane_index((channels, width))

    def put(row, slab, before, after):
        lanes = slice(row * width, (row + 1) * width)
        shifted = jnp.where(lane == 0, before, pltpu.roll(slab, 1, 1))
        taps_ref[0:channels, lanes] = shifted.astype(BF16)
        taps_ref[channels : 2 * channels, lanes] = slab.astype(BF16)
        shifted = jnp.where(lane == width - 1, after, pltpu.roll(slab, width - 1, 1))
        taps_ref[2 * channels : span, lanes] = shifted.astype(BF16)

    left = left_ref[...].astype(F32)
    right = right_ref[...].astype(F32)
    for end, flag, ref in ((0, place_ref[2], up_ref), (1, place_ref[3], down_ref)):
        corner = slice(rows + end, rows + end + 1)
        slab, before, after = [
            jnp.where(flag == 1, values, 0.0)
            for values in (ref[...].astype(F32), left[:, corner], right[:, corner])
        ]
        put(end * (rows + 1), slab, before, after)
    for row in range(rows):
        slab = flat_ref[:, row * width : (row + 1) * width].astype(F32)
        put(row + 1, slab, left[:, row : row + 1], right[:, row : row + 1])
    extra = taps_ref.shape[0] - span
    ones = lax.broadcasted_iota(jnp.int32, (extra, taps_ref.shape[1]), 0) == 0
    taps_ref[span:] = jnp.where(ones, 1.0, 0.0).astype(BF16)

    live = jnp.zeros((1, width), F32)
    live_lane = lane_index((1, width)) // TILE
    for tile in range(tile_cols):
        wet = (wet_ref[0, first_tile + tile] > 0).astype(F32)
        live = jnp.where(live_lane == tile, wet, live)
    step = 2 if rows % 2 == 0 else 1
    chunk = step * width
    live = jnp.concatenate([live] * step, 1)
    third = w_ref.shape[1] // 3
    blank = jnp.zeros((gates, 2 * width), BF16)
    delta_ref[:, : 2 * width] = blank
    delta_ref[:, (rows + 2) * width :] = blank
    bias = jnp.concatenate([b_ref[...]] * step, 1)
    group = 128 // TILE
    states = []
    for start in range(0, rows, step):
        pre = bias
        for row_off in range(3):
            low = (start + row_off) * width
            pre = pre + jnp.dot(
                w_ref[:, row_off * third : (row_off + 1) * third],
                taps_ref[:, low : low + chunk],
                preferred_element_type=F32,
            )
        gate_in = sigmoid(pre[:hid])
        gate_forget = sigmoid(pre[hid : 2 * hid])
        gate_out = sigmoid(pre[2 * hid : 3 * hid])
        candidate = jnp.tanh(pre[3 * hid :])
        lanes = slice(start * width, start * width + chunk)
        cell_in = cell_ref[:, lanes].astype(F32)
        cell_new = gate_forget * cell_in + gate_in * candidate
        squash = jnp.tanh(cell_new)
        hidden_new = live * gate_out * squash
        back_h = live * hcot_ref[:, lanes].astype(F32)
        back_c = live * ccot_ref[:, lanes].astype(F32) + back_h * gate_out * (1.0 - squash * squash)
        cell_back = back_c * gate_forget
        carried = back_c * gate_in
        terms = (
            carried * candidate * (1.0 - gate_in),
            cell_back * cell_in * (1.0 - gate_forget),
            back_h * squash * gate_out * (1.0 - gate_out),
            carried * (1.0 - candidate * candidate),
        )
        low = (start + 2) * width
        for index, term in enumerate(terms):
            delta_ref[index * hid : (index + 1) * hid, low : low + chunk] = term.astype(BF16)
        hidden_new_ref[:, lanes] = hidden_new.astype(BF16)
        cell_back_ref[:, lanes] = cell_back
        for part in range(step):
            piece = slice(part * width, (part + 1) * width)
            states.append(cell_new[:, piece])
        if len(states) == group:
            block_of = lane_index((hid, width)) // TILE
            half = (start + step) // group - 1
            stride = group // 2
            while stride:
                upper = (block_of & stride) != 0
                mixed = list(states)
                for low_index in range(group):
                    if low_index & stride == 0:
                        first, second = states[low_index], states[low_index + stride]
                        mixed[low_index] = jnp.where(
                            upper, pltpu.roll(second, stride * TILE, 1), first
                        )
                        mixed[low_index + stride] = jnp.where(
                            upper, second, pltpu.roll(first, width - stride * TILE, 1)
                        )
                states = mixed
                stride //= 2
            for tile in range(tile_cols):
                tiles_ref[tile, :, half * 128 : (half + 1) * 128] = states[tile].astype(BF16)
            states = []
    delta = delta_ref[:, 2 * width : (rows + 2) * width]
    for row_off in range(3):
        part = lax.dot_general(
            taps_ref[:, row_off * width : (row_off + rows) * width],
            delta,
            (((1,), (1,)), ((), ())),
            preferred_element_type=F32,
        )
        place = slice(row_off * third, (row_off + 1) * third)
        if len(weight_refs) == 1:
            weight_refs[0][place] = part
        else:
            low, high = part[:, : gates // 2], part[:, gates // 2 :]
            weight_refs[0][place] = jnp.where(place_ref[0] == 0, low, high)
            weight_refs[1][place] = jnp.where(place_ref[0] == 0, high, low)


def spread_kernel(place_ref, delta_ref, wt_ref, grad_ref, *rest):
    row_refs, (left_ref, right_ref, side_ref) = rest[:-3], rest[-3:]
    hid = grad_ref.shape[0]
    width = left_ref.shape[1]
    rows = grad_ref.shape[1] // width
    channels = wt_ref.shape[0] // 9
    total = [None] * 3
    for col_off in range(3):
        for row_off in range(3):
            first = (row_off * 3 + col_off + 1) * channels - hid
            low = (2 - row_off) * width
            term = jnp.dot(
                wt_ref[first : first + hid],
                delta_ref[:, low : low + (rows + 2) * width],
                preferred_element_type=F32,
            )
            total[col_off] = term if row_off == 0 else total[col_off] + term
        side_ref[col_off] = total[col_off]
    lane = lane_index((hid, width))
    left = jnp.zeros((hid, width), F32)
    right = jnp.zeros((hid, width), F32)
    ends = []
    for row in range(rows + 2):
        lanes = slice(row * width, (row + 1) * width)
        before = side_ref[0, :, lanes]
        after = side_ref[2, :, lanes]
        slab = (
            side_ref[1, :, lanes]
            + jnp.where(lane == width - 1, 0.0, pltpu.roll(before, width - 1, 1))
            + jnp.where(lane == 0, 0.0, pltpu.roll(after, 1, 1))
        )
        if row in (0, rows + 1):
            corners = jnp.where(lane == 0, before[:, :1], 0.0)
            corners = jnp.where(lane == width - 1, after[:, width - 1 :], corners)
            ends.append((slab, corners))
        else:
            grad_ref[:, (row - 1) * width : row * width] = slab
            left = jnp.where(lane == row - 1, before[:, :1], left)
            right = jnp.where(lane == row - 1, after[:, width - 1 :], right)
    left_ref[...] = left.astype(BF16)
    right_ref[...] = right.astype(BF16)
    if len(row_refs) == 2:
        for index in range(2):
            row_refs[index][...] = jnp.where(
                place_ref[0] == 0, ends[1][index], ends[0][index]
            ).astype(BF16)
    else:
        for end in range(2):
            for index in range(2):
                row_refs[2 * end + index][...] = ends[end][index].astype(BF16)


def finish_kernel(
    place_ref,
    work_ref,
    hidden_new_ref,
    cell_back_ref,
    arrived_ref,
    grad_ref,
    up_ref,
    down_ref,
    up_left_ref,
    up_right_ref,
    down_left_ref,
    down_right_ref,
    left_ref,
    right_ref,
    hidden_next_ref,
    cell_grad_ref,
    cell_next_ref,
    hidden_grad_ref,
    wide_ref,
):
    hid = grad_ref.shape[0]
    width = up_ref.shape[1]
    rows = grad_ref.shape[1] // width
    lane = lane_index((hid, width))
    left = left_ref[...].astype(F32)
    right = right_ref[...].astype(F32)
    ends = {}
    for row, flag, refs in (
        (0, place_ref[2], (up_ref, up_left_ref, up_right_ref)),
        (rows - 1, place_ref[3], (down_ref, down_left_ref, down_right_ref)),
    ):
        slab, before, after = [ref[...].astype(F32) for ref in refs]
        slab = slab + jnp.where(lane == 0, before[:, width - 1 :], 0.0)
        slab = slab + jnp.where(lane == width - 1, after[:, :1], 0.0)
        ends[row] = jnp.where(flag == 1, slab, 0.0)
    for row in range(rows):
        lanes = slice(row * width, (row + 1) * width)
        slab = grad_ref[:, lanes]
        slab = slab + jnp.where(lane == 0, left[:, row : row + 1], 0.0)
        slab = slab + jnp.where(lane == width - 1, right[:, row : row + 1], 0.0)
        if row in ends:
            slab = slab + ends[row]
        hidden_grad_ref[pl.ds(row, hid, stride=rows), :] = slab
        cell_grad_ref[pl.ds(row, hid, stride=rows), :] = cell_back_ref[:, lanes]
        wide_ref[pl.ds(row, hid, stride=rows), :] = hidden_new_ref[:, lanes].astype(F32)
    hidden_next_ref[...] = wide_ref[...].reshape(hid, rows, width).astype(BF16)
    pieces = arrived_ref.shape[2]
    for index in range(cell_next_ref.shape[0]):
        for piece in range(cell_next_ref.shape[2] // pieces):
            cell_next_ref[index, :, piece * pieces : (piece + 1) * pieces] = arrived_ref[
                work_ref[index], piece * hid : (piece + 1) * hid
            ].astype(F32)


def split_bias(block, row):
    index = lax.broadcasted_iota(jnp.int32, block.shape, 0)
    rest = pltpu.roll(block - block.astype(BF16).astype(F32), 1, 0)
    return jnp.where(index == row + 1, rest, block)


def slots_kernel(place_ref, wet_ref, owner_ref, tiles_ref, out_ref):
    tile_cols, hid, cells = tiles_ref.shape
    slots, _, lanes = out_ref.shape
    out_ref[...] = jnp.zeros(out_ref.shape, BF16)
    for tile in range(tile_cols):
        index = place_ref[1] * tile_cols + tile

        @pl.when(wet_ref[0, index] > 0)
        def _():
            for piece in range(cells // lanes):
                out_ref[owner_ref[0, index], piece * hid : (piece + 1) * hid] = tiles_ref[
                    tile, :, piece * lanes : (piece + 1) * lanes
                ]


def pack_kernel(span, count, *refs):
    slots_ref, out_ref, token_ref, share_ref, semaphore = refs[count:]
    token_ref[...] = jnp.zeros(token_ref.shape, F32)
    slots, share, _ = share_ref.shape
    third = refs[0].shape[0] // 3
    total = refs[0][...]
    for ref in refs[1:count]:
        total = total + ref[...]
    total = jnp.concatenate([split_bias(total[:third], span), total[third:]], 0)
    for slot in range(slots):
        share_ref[slot] = total[slot * share : (slot + 1) * share].astype(BF16)
    state_rows = out_ref.shape[1] - share
    copy = pltpu.make_async_copy(share_ref, out_ref.at[:, pl.ds(state_rows, share)], semaphore)
    copy.start()
    copy.wait()


def sum_kernel(scaling, span, state_rows, place_ref, parts_ref, out_ref, token_ref):
    token_ref[...] = jnp.zeros(token_ref.shape, F32)
    total = parts_ref[0, state_rows:].astype(F32)
    for index in range(1, parts_ref.shape[0]):
        total = total + parts_ref[index, state_rows:].astype(F32)
    total = total * scaling
    share = total.shape[0]
    row = span % share
    index = lax.broadcasted_iota(jnp.int32, total.shape, 0)
    whole = jnp.where(index == row, total + pltpu.roll(total, share - 1, 0), total)
    total = jnp.where(place_ref[1] == span // share, split_bias(whole, row), total)
    for index in range(out_ref.shape[0]):
        out_ref[index] = total.astype(BF16)


def weights_kernel(span, other, place_ref, *refs):
    *parts, weight_ref, bias_ref, block_ref, semaphore = refs
    pick_ref = parts[1] if other else parts[0]
    third = pick_ref.shape[0] // 3
    half = pick_ref.shape[1]
    for index in range(3):
        block_ref[index * span : (index + 1) * span] = pick_ref[
            index * third : index * third + span
        ].astype(F32)
    lanes = slice(None)
    if weight_ref.shape[1] > half:
        side = 1 - place_ref[0] if other else place_ref[0]
        lanes = pl.ds(pl.multiple_of(side * half, half), half)
    copy = pltpu.make_async_copy(block_ref, weight_ref.at[:, lanes], semaphore)
    copy.start()
    halves = weight_ref.shape[1] // half
    for side in range(halves):
        rows = parts[0][span:third].astype(F32)
        if other:
            rows = jnp.where(place_ref[0] == side, rows, parts[1][span:third].astype(F32))
        bias_ref[:, side * half : (side + 1) * half] = rows[0:1] + rows[1:2]
    copy.wait()


def moved(values, lat_step, lon_step, lat_devices, lon_devices):
    pairs = []
    for lat in range(lat_devices):
        for lon in range(lon_devices):
            to_lat = lat + lat_step
            if lat_step and lat_devices == 2:
                to_lat = 1 - lat
            if 0 <= to_lat < lat_devices:
                to = to_lat * lon_devices + (lon + lon_step) % lon_devices
                pairs.append((lat * lon_devices + lon, to))
    return lax.ppermute(values, ("lat", "lon"), pairs)


def exchange(ends, corners, left, right, lat_devices, lon_devices):
    def go(values, lat_step, lon_step):
        return moved(values, lat_step, lon_step, lat_devices, lon_devices)

    from_left, from_right = go(right, 0, 1), go(left, 0, -1)
    if lat_devices == 2:
        row = go(ends[0], 1, 0)
        row_left, row_right = go(corners[0], 1, 1), go(corners[0], 1, -1)
        return (row, row, row_left, row_right, row_left, row_right, from_left, from_right)
    return (
        go(ends[1], 1, 0),
        go(ends[0], -1, 0),
        go(corners[1], 1, 1),
        go(corners[1], 1, -1),
        go(corners[0], -1, 1),
        go(corners[0], -1, -1),
        from_left,
        from_right,
    )


def body(forcing, hidden, cell, grad_hidden, grad_cell, wet_mask, tile_owner, w_gates, b_gates):
    lat_index = lax.axis_index("lat")
    lon_index = lax.axis_index("lon")
    lat_devices = lax.axis_size("lat")
    lon_devices = lax.axis_size("lon")
    inp, rows, width = forcing.shape
    hid = hidden.shape[0]
    channels = inp + hid
    gates = w_gates.shape[0]
    span = 3 * channels
    third = (span + 128) // 128 * 128
    cells = rows * width
    tile_cols = width // TILE
    capacity = tile_cols // 2
    place = jnp.stack(
        [
            lat_index,
            lon_index,
            (lat_index > 0).astype(jnp.int32),
            (lat_index < lat_devices - 1).astype(jnp.int32),
        ]
    ).astype(jnp.int32)

    def shaped(*shape, dtype=BF16):
        return jax.ShapeDtypeStruct(shape, dtype)

    end_count = 1 if lat_devices == 2 else 2
    wide, *ends = call(
        edges_kernel,
        (shaped(channels * rows, width, dtype=F32),) + (shaped(channels, width),) * end_count,
        (place, forcing, hidden),
        scalars=1,
        moved=4 * channels * cells,
        fetched=2,
    )
    flat, left, right = call(
        columns_kernel,
        (shaped(channels, cells),) + (shaped(channels, width),) * 2,
        (wide,),
        moved=6 * channels * cells,
    )
    if lat_devices == 2:
        up = down = moved(ends[0], 1, 0, lat_devices, lon_devices)
    else:
        up = moved(ends[1], 1, 0, lat_devices, lon_devices)
        down = moved(ends[0], -1, 0, lat_devices, lon_devices)
    left, right = call(
        lambda *refs: corners_kernel(rows, *refs),
        (shaped(channels, width),) * 2,
        (up, down, left, right),
        moved=8 * channels * width,
    )
    halo = (
        up,
        down,
        moved(right, 0, 1, lat_devices, lon_devices),
        moved(left, 0, -1, lat_devices, lon_devices),
    )
    w_turned = w_gates.T
    cell_flat, hcot_flat, ccot_flat, w_rows, bias = call(
        flatten_kernel,
        (shaped(hid, cells),) * 3
        + (shaped(gates, 3 * third), shaped(gates, width, dtype=F32)),
        (b_gates.reshape(1, gates), w_turned, cell, grad_hidden, grad_cell),
        scratch=[pltpu.VMEM((hid * rows, width), F32)],
        moved=12 * hid * cells,
        fetched=5,
    )
    halves = 2 if lat_devices == 2 else 1
    lanes = gates // halves
    hidden_new, cell_back, tiles, *weight_parts, delta = call(
        step_kernel,
        (
            shaped(hid, cells),
            shaped(hid, cells, dtype=F32),
            shaped(tile_cols, hid, TILE * TILE),
        )
        + (shaped(3 * third, lanes, dtype=F32),) * halves
        + (shaped(gates, (rows + 4) * width),),
        (place, wet_mask, tile_owner, flat, *halo)
        + (cell_flat, hcot_flat, ccot_flat, w_rows, bias),
        scalars=3,
        scratch=[pltpu.VMEM((third, (rows + 2) * width), BF16)],
        flops=4 * gates * 3 * span * cells,
        moved=16 * hid * cells,
    )
    swap = [(0, 1), (1, 0)]
    if halves == 2:
        weight_parts = (weight_parts[0], lax.ppermute(weight_parts[1], "lat", swap))
    else:
        weight_parts = (lax.psum(weight_parts[0], "lat"),)
    state_rows = hid * TILE * TILE // lanes
    share = 3 * third // lon_devices
    slots = call(
        slots_kernel,
        shaped(lon_devices, state_rows + share, lanes),
        (place, wet_mask, tile_owner, tiles),
        scalars=3,
        moved=4 * lon_devices * hid * TILE * TILE,
    )
    anywhere = pl.BlockSpec(memory_space=pl.ANY)
    count = len(weight_parts)
    outgoing, packed = pl.pallas_call(
        lambda *refs: pack_kernel(span, count, *refs),
        out_shape=(shaped(*slots.shape), shaped(8, 128, dtype=F32)),
        in_specs=[VMEM] * count + [anywhere],
        out_specs=(anywhere, VMEM),
        scratch_shapes=[
            pltpu.VMEM((lon_devices, share, lanes), BF16),
            pltpu.SemaphoreType.DMA(()),
        ],
        input_output_aliases={count: 0},
        compiler_params=pltpu.CompilerParams(vmem_limit_bytes=LIMIT),
        cost_estimate=pl.CostEstimate(
            flops=0, bytes_accessed=8 * gates * 3 * third, transcendentals=0
        ),
    )(*weight_parts, slots)
    incoming = lax.all_to_all(outgoing, "lon", 0, 0, tiled=True)
    grad_parts = call(
        spread_kernel,
        (shaped(hid, cells, dtype=F32),) + (shaped(hid, width),) * (2 * end_count + 2),
        (place, delta, w_turned),
        scalars=1,
        scratch=[pltpu.VMEM((3, hid, (rows + 2) * width), F32)],
        flops=2 * gates * 9 * hid * cells,
        moved=8 * gates * cells,
        after=(packed,),
    )
    grad_flat, grad_ends, grad_sides = grad_parts[0], grad_parts[1:-2], grad_parts[-2:]
    grad_halo = exchange(
        grad_ends[0::2], grad_ends[1::2], *grad_sides, lat_devices, lon_devices
    )
    scaling = 1.0 / math.sqrt(float(lat_devices * lon_devices * capacity * TILE * TILE))
    shares, shared = call(
        lambda *refs: sum_kernel(scaling, span, state_rows, *refs),
        (shaped(lon_devices, share, lanes), shaped(8, 128, dtype=F32)),
        (place, incoming),
        scalars=1,
        moved=2 * gates * 3 * third,
        after=grad_halo,
    )
    owned = (wet_mask > 0) & (tile_owner == lon_index)
    arrived = jnp.any(owned.reshape(lon_devices, tile_cols), 1)
    order = jnp.arange(lon_devices, dtype=jnp.int32)
    rank = jnp.sum((arrived[:, None] & (order[:, None] < order[None, :])).astype(jnp.int32), 0)
    placed = arrived[None, :] & (rank[None, :] == jnp.arange(capacity, dtype=jnp.int32)[:, None])
    work = jnp.sum(jnp.where(placed, order[None, :], 0), 1)
    finished = call(
        finish_kernel,
        (
            shaped(hid, rows, width),
            shaped(hid * rows, width, dtype=F32),
            shaped(capacity, hid, TILE * TILE, dtype=F32),
            shaped(hid * rows, width, dtype=F32),
        ),
        (place, work, hidden_new, cell_back, incoming, grad_flat, *grad_halo),
        scalars=2,
        scratch=[pltpu.VMEM((hid * rows, width), F32)],
        moved=32 * hid * cells,
        after=(shared,),
    )
    gathered = lax.all_to_all(shares, "lon", 0, 0, tiled=True).reshape(3 * third, lanes)
    gathered, finished = lax.optimization_barrier((gathered, finished))

    def write(parts, other, filled=()):
        count = len(parts)
        return pl.pallas_call(
            lambda *refs: weights_kernel(span, other, *refs[: 1 + count], *refs[-4:]),
            out_shape=(shaped(3 * span, gates, dtype=F32), shaped(1, gates, dtype=F32)),
            in_specs=[SMEM] + [VMEM] * count + [anywhere] * len(filled),
            out_specs=(anywhere, VMEM),
            scratch_shapes=[pltpu.VMEM((3 * span, lanes), F32), pltpu.SemaphoreType.DMA(())],
            input_output_aliases={1 + count: 0} if filled else {},
            compiler_params=pltpu.CompilerParams(vmem_limit_bytes=LIMIT),
            cost_estimate=pl.CostEstimate(
                flops=0, bytes_accessed=6 * lanes * 3 * third, transcendentals=0
            ),
        )(place, *parts, *filled)

    hidden_next, cell_grad, cell_next, hidden_grad = finished
    weight_grad, bias_grad = write((gathered,), False)
    if halves == 2:
        partner = lax.ppermute(gathered, "lat", swap)
        weight_grad, bias_grad = write((gathered, partner), True, (weight_grad,))
    return (
        hidden_next,
        cell_next,
        hidden_grad.reshape(hid, rows, width),
        cell_grad.reshape(hid, rows, width),
        weight_grad.T,
        bias_grad.reshape(gates),
    )


def solution(mesh):
    return jax.shard_map(
        body,
        mesh=mesh,
        in_specs=(
            P(None, "lat", "lon"),
            P(None, "lat", "lon"),
            P(None, "lat", "lon"),
            P(None, "lat", "lon"),
            P(None, "lat", "lon"),
            P("lat", None),
            P("lat", None),
            P(),
            P(),
        ),
        out_specs=(
            P(None, "lat", "lon"),
            P(("lat", "lon"), None, None),
            P(None, "lat", "lon"),
            P(None, "lat", "lon"),
            P(),
            P(),
        ),
        check_vma=False,
    )
```

```python
import math

import jax
import jax.numpy as jnp
from jax import lax
from jax.experimental import pallas as pl
from jax.experimental.pallas import tpu as pltpu
from jax.sharding import PartitionSpec as P

TILE = 16
F32 = jnp.float32
BF16 = jnp.bfloat16
LIMIT = 48 * 1024 * 1024
SMEM = pl.BlockSpec(memory_space=pltpu.SMEM)
VMEM = pl.BlockSpec(memory_space=pltpu.VMEM)


def call(kernel, outs, operands, scalars=0, scratch=(), flops=0, moved=0, after=(), fetched=0):
    count = len(operands)
    kept = count - fetched
    total = count + len(after)

    def run(*refs):
        if not fetched:
            kernel(*refs[:count], *refs[total:])
            return
        *rest, semaphores = refs[total:]
        buffers = rest[len(rest) - fetched :]
        copies = [
            pltpu.make_async_copy(source, target, semaphores.at[index])
            for index, (source, target) in enumerate(zip(refs[kept:count], buffers))
        ]
        for copy in copies:
            copy.start()
        waits = [copy.wait for copy in copies]
        kernel(waits, *refs[:kept], *buffers, *rest[: len(rest) - fetched])

    scratch = list(scratch)
    operands = list(operands)
    for index in range(kept, count):
        operands[index] = pltpu.with_memory_space_constraint(operands[index], pltpu.HBM)
    if fetched:
        scratch += [pltpu.VMEM(leaf.shape, leaf.dtype) for leaf in operands[kept:]]
        scratch.append(pltpu.SemaphoreType.DMA((fetched,)))

    return pl.pallas_call(
        run,
        out_shape=outs,
        in_specs=[SMEM] * scalars
        + [VMEM] * (kept - scalars)
        + [pl.BlockSpec(memory_space=pltpu.HBM)] * fetched
        + [VMEM] * len(after),
        out_specs=jax.tree.map(lambda _: VMEM, outs),
        scratch_shapes=scratch,
        compiler_params=pltpu.CompilerParams(vmem_limit_bytes=LIMIT),
        cost_estimate=pl.CostEstimate(flops=flops, bytes_accessed=moved, transcendentals=0),
    )(*operands, *after)


def lane_index(shape):
    return lax.broadcasted_iota(jnp.int32, shape, 1)


def sigmoid(values):
    return 0.5 * jnp.tanh(0.5 * values) + 0.5


def edges_kernel(waits, place_ref, forcing_ref, hidden_ref, wide_ref, *row_refs):
    inp, rows, width = forcing_ref.shape
    channels = inp + hidden_ref.shape[0]
    for wait in waits:
        wait()
    wide_ref[: inp * rows] = forcing_ref[...].astype(F32).reshape(inp * rows, width)
    wide_ref[inp * rows :] = hidden_ref[...].astype(F32).reshape((channels - inp) * rows, width)
    ends = [wide_ref[pl.ds(row, channels, stride=rows), :] for row in (0, rows - 1)]
    if len(row_refs) == 1:
        row_refs[0][...] = jnp.where(place_ref[0] == 0, ends[1], ends[0]).astype(BF16)
    else:
        for ref, end in zip(row_refs, ends):
            ref[...] = end.astype(BF16)


def columns_kernel(wide_ref, flat_ref, left_ref, right_ref):
    channels, width = left_ref.shape
    rows = wide_ref.shape[0] // channels
    lane = lane_index((channels, width))
    left = jnp.zeros((channels, width), F32)
    right = jnp.zeros((channels, width), F32)
    for row in range(rows):
        slab = wide_ref[pl.ds(row, channels, stride=rows), :]
        flat_ref[:, row * width : (row + 1) * width] = slab.astype(BF16)
        left = jnp.where(lane == row, slab[:, :1], left)
        right = jnp.where(lane == row, slab[:, width - 1 :], right)
    left_ref[...] = left.astype(BF16)
    right_ref[...] = right.astype(BF16)


def flatten_kernel(
    waits,
    b_ref,
    wt_ref,
    cell_ref,
    hcot_ref,
    ccot_ref,
    cell_out,
    hcot_out,
    ccot_out,
    w_ref,
    bias_ref,
    wide_ref,
):
    hid, rows, width = cell_ref.shape
    gates = wt_ref.shape[1]
    span = wt_ref.shape[0] // 3
    third = w_ref.shape[1] // 3
    waits[0]()
    bias_ref[...] = jnp.broadcast_to(b_ref[...], (bias_ref.shape[1], gates)).T
    waits[1]()
    blank = jnp.zeros((third - span, gates), F32)
    for index in range(3):
        block = wt_ref[index * span : (index + 1) * span].astype(F32)
        w_ref[:, index * third : (index + 1) * third] = (
            jnp.concatenate([block, blank], 0).T.astype(BF16)
        )
    for wait, source, target in zip(
        waits[2:], (cell_ref, hcot_ref, ccot_ref), (cell_out, hcot_out, ccot_out)
    ):
        wait()
        wide_ref[...] = source[...].astype(F32).reshape(hid * rows, width)
        for row in range(rows):
            target[:, row * width : (row + 1) * width] = wide_ref[
                pl.ds(row, hid, stride=rows), :
            ].astype(BF16)


def corners_kernel(rows, up_ref, down_ref, left_ref, right_ref, left_out, right_out):
    lane = lane_index(left_ref.shape)
    width = up_ref.shape[1]
    up = up_ref[...].astype(F32)
    down = down_ref[...].astype(F32)
    for column, source, target in ((0, left_ref, left_out), (width - 1, right_ref, right_out)):
        values = source[...].astype(F32)
        values = jnp.where(lane == rows, up[:, column : column + 1], values)
        values = jnp.where(lane == rows + 1, down[:, column : column + 1], values)
        target[...] = values.astype(BF16)


def step_kernel(
    place_ref,
    wet_ref,
    owner_ref,
    flat_ref,
    up_ref,
    down_ref,
    left_ref,
    right_ref,
    cell_ref,
    hcot_ref,
    ccot_ref,
    w_ref,
    b_ref,
    hidden_new_ref,
    cell_back_ref,
    tiles_ref,
    *rest,
):
    weight_refs, (delta_ref, taps_ref) = rest[:-2], rest[-2:]
    channels = flat_ref.shape[0]
    hid = cell_ref.shape[0]
    gates = w_ref.shape[0]
    width = up_ref.shape[1]
    rows = flat_ref.shape[1] // width
    tile_cols = width // TILE
    span = 3 * channels
    first_tile = place_ref[1] * tile_cols
    lane = lane_index((channels, width))

    def put(row, slab, before, after):
        lanes = slice(row * width, (row + 1) * width)
        shifted = jnp.where(lane == 0, before, pltpu.roll(slab, 1, 1))
        taps_ref[0:channels, lanes] = shifted.astype(BF16)
        taps_ref[channels : 2 * channels, lanes] = slab.astype(BF16)
        shifted = jnp.where(lane == width - 1, after, pltpu.roll(slab, width - 1, 1))
        taps_ref[2 * channels : span, lanes] = shifted.astype(BF16)

    left = left_ref[...].astype(F32)
    right = right_ref[...].astype(F32)
    for end, flag, ref in ((0, place_ref[2], up_ref), (1, place_ref[3], down_ref)):
        corner = slice(rows + end, rows + end + 1)
        slab, before, after = [
            jnp.where(flag == 1, values, 0.0)
            for values in (ref[...].astype(F32), left[:, corner], right[:, corner])
        ]
        put(end * (rows + 1), slab, before, after)
    for row in range(rows):
        slab = flat_ref[:, row * width : (row + 1) * width].astype(F32)
        put(row + 1, slab, left[:, row : row + 1], right[:, row : row + 1])
    extra = taps_ref.shape[0] - span
    ones = lax.broadcasted_iota(jnp.int32, (extra, taps_ref.shape[1]), 0) == 0
    taps_ref[span:] = jnp.where(ones, 1.0, 0.0).astype(BF16)

    live = jnp.zeros((1, width), F32)
    live_lane = lane_index((1, width)) // TILE
    for tile in range(tile_cols):
        wet = (wet_ref[0, first_tile + tile] > 0).astype(F32)
        live = jnp.where(live_lane == tile, wet, live)
    step = 2 if rows % 2 == 0 else 1
    chunk = step * width
    live = jnp.concatenate([live] * step, 1)
    third = w_ref.shape[1] // 3
    blank = jnp.zeros((gates, 2 * width), BF16)
    delta_ref[:, : 2 * width] = blank
    delta_ref[:, (rows + 2) * width :] = blank
    bias = jnp.concatenate([b_ref[...]] * step, 1)
    group = 128 // TILE
    states = []
    late = (rows // step // 2) * step

    def product(first, count):
        return [
            lax.dot_general(
                taps_ref[:, (first + row_off) * width : (first + row_off + count) * width],
                delta_ref[:, (first + 2) * width : (first + 2 + count) * width],
                (((1,), (1,)), ((), ())),
                preferred_element_type=F32,
            )
            for row_off in range(3)
        ]

    for start in range(0, rows, step):
        pre = bias
        for row_off in range(3):
            low = (start + row_off) * width
            pre = pre + jnp.dot(
                w_ref[:, row_off * third : (row_off + 1) * third],
                taps_ref[:, low : low + chunk],
                preferred_element_type=F32,
            )
        gate_in = sigmoid(pre[:hid])
        gate_forget = sigmoid(pre[hid : 2 * hid])
        gate_out = sigmoid(pre[2 * hid : 3 * hid])
        candidate = jnp.tanh(pre[3 * hid :])
        lanes = slice(start * width, start * width + chunk)
        cell_in = cell_ref[:, lanes].astype(F32)
        cell_new = gate_forget * cell_in + gate_in * candidate
        squash = jnp.tanh(cell_new)
        hidden_new = live * gate_out * squash
        back_h = live * hcot_ref[:, lanes].astype(F32)
        back_c = live * ccot_ref[:, lanes].astype(F32) + back_h * gate_out * (1.0 - squash * squash)
        cell_back = back_c * gate_forget
        carried = back_c * gate_in
        terms = (
            carried * candidate * (1.0 - gate_in),
            cell_back * cell_in * (1.0 - gate_forget),
            back_h * squash * gate_out * (1.0 - gate_out),
            carried * (1.0 - candidate * candidate),
        )
        low = (start + 2) * width
        for index, term in enumerate(terms):
            delta_ref[index * hid : (index + 1) * hid, low : low + chunk] = term.astype(BF16)
        if start + step == rows - late:
            products = product(0, rows - late)
        hidden_new_ref[:, lanes] = hidden_new.astype(BF16)
        cell_back_ref[:, lanes] = cell_back
        for part in range(step):
            piece = slice(part * width, (part + 1) * width)
            states.append(cell_new[:, piece])
        if len(states) == group:
            block_of = lane_index((hid, width)) // TILE
            half = (start + step) // group - 1
            stride = group // 2
            while stride:
                upper = (block_of & stride) != 0
                mixed = list(states)
                for low_index in range(group):
                    if low_index & stride == 0:
                        first, second = states[low_index], states[low_index + stride]
                        mixed[low_index] = jnp.where(
                            upper, pltpu.roll(second, stride * TILE, 1), first
                        )
                        mixed[low_index + stride] = jnp.where(
                            upper, second, pltpu.roll(first, width - stride * TILE, 1)
                        )
                states = mixed
                stride //= 2
            for tile in range(tile_cols):
                tiles_ref[tile, :, half * 128 : (half + 1) * 128] = states[tile].astype(BF16)
            states = []
    products = [first + second for first, second in zip(products, product(rows - late, late))]
    for row_off, part in enumerate(products):
        place = slice(row_off * third, (row_off + 1) * third)
        if len(weight_refs) == 1:
            weight_refs[0][place] = part
        else:
            low, high = part[:, : gates // 2], part[:, gates // 2 :]
            weight_refs[0][place] = jnp.where(place_ref[0] == 0, low, high)
            weight_refs[1][place] = jnp.where(place_ref[0] == 0, high, low)


def spread_kernel(place_ref, delta_ref, wt_ref, grad_ref, *rest):
    row_refs, (left_ref, right_ref, side_ref) = rest[:-3], rest[-3:]
    hid = grad_ref.shape[0]
    width = left_ref.shape[1]
    rows = grad_ref.shape[1] // width
    channels = wt_ref.shape[0] // 9
    total = [None] * 3
    for col_off in range(3):
        for row_off in range(3):
            first = (row_off * 3 + col_off + 1) * channels - hid
            low = (2 - row_off) * width
            term = jnp.dot(
                wt_ref[first : first + hid],
                delta_ref[:, low : low + (rows + 2) * width],
                preferred_element_type=F32,
            )
            total[col_off] = term if row_off == 0 else total[col_off] + term
        side_ref[col_off] = total[col_off]
    lane = lane_index((hid, width))
    left = jnp.zeros((hid, width), F32)
    right = jnp.zeros((hid, width), F32)
    ends = []
    for row in range(rows + 2):
        lanes = slice(row * width, (row + 1) * width)
        before = side_ref[0, :, lanes]
        after = side_ref[2, :, lanes]
        slab = (
            side_ref[1, :, lanes]
            + jnp.where(lane == width - 1, 0.0, pltpu.roll(before, width - 1, 1))
            + jnp.where(lane == 0, 0.0, pltpu.roll(after, 1, 1))
        )
        if row in (0, rows + 1):
            corners = jnp.where(lane == 0, before[:, :1], 0.0)
            corners = jnp.where(lane == width - 1, after[:, width - 1 :], corners)
            ends.append((slab, corners))
        else:
            grad_ref[:, (row - 1) * width : row * width] = slab
            left = jnp.where(lane == row - 1, before[:, :1], left)
            right = jnp.where(lane == row - 1, after[:, width - 1 :], right)
    left_ref[...] = left.astype(BF16)
    right_ref[...] = right.astype(BF16)
    if len(row_refs) == 2:
        for index in range(2):
            row_refs[index][...] = jnp.where(
                place_ref[0] == 0, ends[1][index], ends[0][index]
            ).astype(BF16)
    else:
        for end in range(2):
            for index in range(2):
                row_refs[2 * end + index][...] = ends[end][index].astype(BF16)


def finish_kernel(
    place_ref,
    work_ref,
    hidden_new_ref,
    cell_back_ref,
    arrived_ref,
    grad_ref,
    up_ref,
    down_ref,
    up_left_ref,
    up_right_ref,
    down_left_ref,
    down_right_ref,
    left_ref,
    right_ref,
    hidden_next_ref,
    cell_grad_ref,
    cell_next_ref,
    hidden_grad_ref,
    wide_ref,
):
    hid = grad_ref.shape[0]
    width = up_ref.shape[1]
    rows = grad_ref.shape[1] // width
    lane = lane_index((hid, width))
    left = left_ref[...].astype(F32)
    right = right_ref[...].astype(F32)
    ends = {}
    for row, flag, refs in (
        (0, place_ref[2], (up_ref, up_left_ref, up_right_ref)),
        (rows - 1, place_ref[3], (down_ref, down_left_ref, down_right_ref)),
    ):
        slab, before, after = [ref[...].astype(F32) for ref in refs]
        slab = slab + jnp.where(lane == 0, before[:, width - 1 :], 0.0)
        slab = slab + jnp.where(lane == width - 1, after[:, :1], 0.0)
        ends[row] = jnp.where(flag == 1, slab, 0.0)
    for row in range(rows):
        lanes = slice(row * width, (row + 1) * width)
        slab = grad_ref[:, lanes]
        slab = slab + jnp.where(lane == 0, left[:, row : row + 1], 0.0)
        slab = slab + jnp.where(lane == width - 1, right[:, row : row + 1], 0.0)
        if row in ends:
            slab = slab + ends[row]
        hidden_grad_ref[pl.ds(row, hid, stride=rows), :] = slab
        cell_grad_ref[pl.ds(row, hid, stride=rows), :] = cell_back_ref[:, lanes]
        wide_ref[pl.ds(row, hid, stride=rows), :] = hidden_new_ref[:, lanes].astype(F32)
    hidden_next_ref[...] = wide_ref[...].reshape(hid, rows, width).astype(BF16)
    pieces = arrived_ref.shape[2]
    for index in range(cell_next_ref.shape[0]):
        for piece in range(cell_next_ref.shape[2] // pieces):
            cell_next_ref[index, :, piece * pieces : (piece + 1) * pieces] = arrived_ref[
                work_ref[index], piece * hid : (piece + 1) * hid
            ].astype(F32)


def split_bias(block, row):
    index = lax.broadcasted_iota(jnp.int32, block.shape, 0)
    rest = pltpu.roll(block - block.astype(BF16).astype(F32), 1, 0)
    return jnp.where(index == row + 1, rest, block)


def slots_kernel(place_ref, wet_ref, owner_ref, tiles_ref, out_ref):
    tile_cols, hid, cells = tiles_ref.shape
    slots, _, lanes = out_ref.shape
    out_ref[...] = jnp.zeros(out_ref.shape, BF16)
    for tile in range(tile_cols):
        index = place_ref[1] * tile_cols + tile

        @pl.when(wet_ref[0, index] > 0)
        def _():
            for piece in range(cells // lanes):
                out_ref[owner_ref[0, index], piece * hid : (piece + 1) * hid] = tiles_ref[
                    tile, :, piece * lanes : (piece + 1) * lanes
                ]


def pack_kernel(span, count, *refs):
    slots_ref, out_ref, token_ref, share_ref, semaphore = refs[count:]
    token_ref[...] = jnp.zeros(token_ref.shape, F32)
    slots, share, _ = share_ref.shape
    third = refs[0].shape[0] // 3
    total = refs[0][...]
    for ref in refs[1:count]:
        total = total + ref[...]
    total = jnp.concatenate([split_bias(total[:third], span), total[third:]], 0)
    for slot in range(slots):
        share_ref[slot] = total[slot * share : (slot + 1) * share].astype(BF16)
    state_rows = out_ref.shape[1] - share
    copy = pltpu.make_async_copy(share_ref, out_ref.at[:, pl.ds(state_rows, share)], semaphore)
    copy.start()
    copy.wait()


def sum_kernel(scaling, span, state_rows, place_ref, parts_ref, out_ref, token_ref):
    token_ref[...] = jnp.zeros(token_ref.shape, F32)
    total = parts_ref[0, state_rows:].astype(F32)
    for index in range(1, parts_ref.shape[0]):
        total = total + parts_ref[index, state_rows:].astype(F32)
    total = total * scaling
    share = total.shape[0]
    row = span % share
    index = lax.broadcasted_iota(jnp.int32, total.shape, 0)
    whole = jnp.where(index == row, total + pltpu.roll(total, share - 1, 0), total)
    total = jnp.where(place_ref[1] == span // share, split_bias(whole, row), total)
    for index in range(out_ref.shape[0]):
        out_ref[index] = total.astype(BF16)


def weights_kernel(span, count, place_ref, *refs):
    parts = refs[:count]
    weight_ref, bias_ref, block_ref, semaphores = refs[count:]
    third = parts[0].shape[0] // 3
    half = parts[0].shape[1]
    copies = []
    for index in range(3):
        rows = slice(index * span, (index + 1) * span)
        for side in range(count):
            pick = parts[0][index * third : index * third + span]
            if count == 2:
                other = parts[1][index * third : index * third + span]
                pick = jnp.where(place_ref[0] == side, pick.astype(F32), other.astype(F32))
            block_ref[rows, side * half : (side + 1) * half] = pick.astype(F32)
        copy = pltpu.make_async_copy(
            block_ref.at[rows], weight_ref.at[rows], semaphores.at[index]
        )
        copy.start()
        copies.append(copy)
    for side in range(count):
        pair = parts[0][span:third].astype(F32)
        if count == 2:
            pair = jnp.where(place_ref[0] == side, pair, parts[1][span:third].astype(F32))
        bias_ref[:, side * half : (side + 1) * half] = pair[0:1] + pair[1:2]
    for copy in copies:
        copy.wait()


def moved(values, lat_step, lon_step, lat_devices, lon_devices):
    pairs = []
    for lat in range(lat_devices):
        for lon in range(lon_devices):
            to_lat = lat + lat_step
            if lat_step and lat_devices == 2:
                to_lat = 1 - lat
            if 0 <= to_lat < lat_devices:
                to = to_lat * lon_devices + (lon + lon_step) % lon_devices
                pairs.append((lat * lon_devices + lon, to))
    return lax.ppermute(values, ("lat", "lon"), pairs)


def exchange(ends, corners, left, right, lat_devices, lon_devices):
    def go(values, lat_step, lon_step):
        return moved(values, lat_step, lon_step, lat_devices, lon_devices)

    from_left, from_right = go(right, 0, 1), go(left, 0, -1)
    if lat_devices == 2:
        row = go(ends[0], 1, 0)
        row_left, row_right = go(corners[0], 1, 1), go(corners[0], 1, -1)
        return (row, row, row_left, row_right, row_left, row_right, from_left, from_right)
    return (
        go(ends[1], 1, 0),
        go(ends[0], -1, 0),
        go(corners[1], 1, 1),
        go(corners[1], 1, -1),
        go(corners[0], -1, 1),
        go(corners[0], -1, -1),
        from_left,
        from_right,
    )


def body(forcing, hidden, cell, grad_hidden, grad_cell, wet_mask, tile_owner, w_gates, b_gates):
    lat_index = lax.axis_index("lat")
    lon_index = lax.axis_index("lon")
    lat_devices = lax.axis_size("lat")
    lon_devices = lax.axis_size("lon")
    inp, rows, width = forcing.shape
    hid = hidden.shape[0]
    channels = inp + hid
    gates = w_gates.shape[0]
    span = 3 * channels
    third = (span + 128) // 128 * 128
    cells = rows * width
    tile_cols = width // TILE
    capacity = tile_cols // 2
    place = jnp.stack(
        [
            lat_index,
            lon_index,
            (lat_index > 0).astype(jnp.int32),
            (lat_index < lat_devices - 1).astype(jnp.int32),
        ]
    ).astype(jnp.int32)

    def shaped(*shape, dtype=BF16):
        return jax.ShapeDtypeStruct(shape, dtype)

    end_count = 1 if lat_devices == 2 else 2
    wide, *ends = call(
        edges_kernel,
        (shaped(channels * rows, width, dtype=F32),) + (shaped(channels, width),) * end_count,
        (place, forcing, hidden),
        scalars=1,
        moved=4 * channels * cells,
        fetched=2,
    )
    flat, left, right = call(
        columns_kernel,
        (shaped(channels, cells),) + (shaped(channels, width),) * 2,
        (wide,),
        moved=6 * channels * cells,
    )
    if lat_devices == 2:
        up = down = moved(ends[0], 1, 0, lat_devices, lon_devices)
    else:
        up = moved(ends[1], 1, 0, lat_devices, lon_devices)
        down = moved(ends[0], -1, 0, lat_devices, lon_devices)
    left, right = call(
        lambda *refs: corners_kernel(rows, *refs),
        (shaped(channels, width),) * 2,
        (up, down, left, right),
        moved=8 * channels * width,
    )
    halo = (
        up,
        down,
        moved(right, 0, 1, lat_devices, lon_devices),
        moved(left, 0, -1, lat_devices, lon_devices),
    )
    w_turned = w_gates.T
    cell_flat, hcot_flat, ccot_flat, w_rows, bias = call(
        flatten_kernel,
        (shaped(hid, cells),) * 3
        + (shaped(gates, 3 * third), shaped(gates, width, dtype=F32)),
        (b_gates.reshape(1, gates), w_turned, cell, grad_hidden, grad_cell),
        scratch=[pltpu.VMEM((hid * rows, width), F32)],
        moved=12 * hid * cells,
        fetched=5,
    )
    halves = 2 if lat_devices == 2 else 1
    lanes = gates // halves
    hidden_new, cell_back, tiles, *weight_parts, delta = call(
        step_kernel,
        (
            shaped(hid, cells),
            shaped(hid, cells, dtype=F32),
            shaped(tile_cols, hid, TILE * TILE),
        )
        + (shaped(3 * third, lanes, dtype=F32),) * halves
        + (shaped(gates, (rows + 4) * width),),
        (place, wet_mask, tile_owner, flat, *halo)
        + (cell_flat, hcot_flat, ccot_flat, w_rows, bias),
        scalars=3,
        scratch=[pltpu.VMEM((third, (rows + 2) * width), BF16)],
        flops=4 * gates * 3 * span * cells,
        moved=16 * hid * cells,
    )
    swap = [(0, 1), (1, 0)]
    if halves == 2:
        weight_parts = (weight_parts[0], lax.ppermute(weight_parts[1], "lat", swap))
    else:
        weight_parts = (lax.psum(weight_parts[0], "lat"),)
    state_rows = hid * TILE * TILE // lanes
    share = 3 * third // lon_devices
    slots = call(
        slots_kernel,
        shaped(lon_devices, state_rows + share, lanes),
        (place, wet_mask, tile_owner, tiles),
        scalars=3,
        moved=4 * lon_devices * hid * TILE * TILE,
    )
    anywhere = pl.BlockSpec(memory_space=pl.ANY)
    count = len(weight_parts)
    outgoing, packed = pl.pallas_call(
        lambda *refs: pack_kernel(span, count, *refs),
        out_shape=(shaped(*slots.shape), shaped(8, 128, dtype=F32)),
        in_specs=[VMEM] * count + [anywhere],
        out_specs=(anywhere, VMEM),
        scratch_shapes=[
            pltpu.VMEM((lon_devices, share, lanes), BF16),
            pltpu.SemaphoreType.DMA(()),
        ],
        input_output_aliases={count: 0},
        compiler_params=pltpu.CompilerParams(vmem_limit_bytes=LIMIT),
        cost_estimate=pl.CostEstimate(
            flops=0, bytes_accessed=8 * gates * 3 * third, transcendentals=0
        ),
    )(*weight_parts, slots)
    incoming = lax.all_to_all(outgoing, "lon", 0, 0, tiled=True)
    grad_parts = call(
        spread_kernel,
        (shaped(hid, cells, dtype=F32),) + (shaped(hid, width),) * (2 * end_count + 2),
        (place, delta, w_turned),
        scalars=1,
        scratch=[pltpu.VMEM((3, hid, (rows + 2) * width), F32)],
        flops=2 * gates * 9 * hid * cells,
        moved=8 * gates * cells,
        after=(packed,),
    )
    grad_flat, grad_ends, grad_sides = grad_parts[0], grad_parts[1:-2], grad_parts[-2:]
    grad_halo = exchange(
        grad_ends[0::2], grad_ends[1::2], *grad_sides, lat_devices, lon_devices
    )
    scaling = 1.0 / math.sqrt(float(lat_devices * lon_devices * capacity * TILE * TILE))
    shares, shared = call(
        lambda *refs: sum_kernel(scaling, span, state_rows, *refs),
        (shaped(lon_devices, share, lanes), shaped(8, 128, dtype=F32)),
        (place, incoming),
        scalars=1,
        moved=2 * gates * 3 * third,
        after=grad_halo,
    )
    owned = (wet_mask > 0) & (tile_owner == lon_index)
    arrived = jnp.any(owned.reshape(lon_devices, tile_cols), 1)
    order = jnp.arange(lon_devices, dtype=jnp.int32)
    rank = jnp.sum((arrived[:, None] & (order[:, None] < order[None, :])).astype(jnp.int32), 0)
    placed = arrived[None, :] & (rank[None, :] == jnp.arange(capacity, dtype=jnp.int32)[:, None])
    work = jnp.sum(jnp.where(placed, order[None, :], 0), 1)
    finished = call(
        finish_kernel,
        (
            shaped(hid, rows, width),
            shaped(hid * rows, width, dtype=F32),
            shaped(capacity, hid, TILE * TILE, dtype=F32),
            shaped(hid * rows, width, dtype=F32),
        ),
        (place, work, hidden_new, cell_back, incoming, grad_flat, *grad_halo),
        scalars=2,
        scratch=[pltpu.VMEM((hid * rows, width), F32)],
        moved=32 * hid * cells,
        after=(shared,),
    )
    gathered = lax.all_to_all(shares, "lon", 0, 0, tiled=True).reshape(3 * third, lanes)
    gathered, finished = lax.optimization_barrier((gathered, finished))

    hidden_next, cell_grad, cell_next, hidden_grad = finished
    gathered = (gathered,)
    if halves == 2:
        gathered += (lax.ppermute(gathered[0], "lat", swap),)
    weight_grad, bias_grad = pl.pallas_call(
        lambda *refs: weights_kernel(span, count, *refs),
        out_shape=(shaped(3 * span, gates, dtype=F32), shaped(1, gates, dtype=F32)),
        in_specs=[SMEM] + [VMEM] * count,
        out_specs=(anywhere, VMEM),
        scratch_shapes=[pltpu.VMEM((3 * span, gates), F32), pltpu.SemaphoreType.DMA((3,))],
        compiler_params=pltpu.CompilerParams(vmem_limit_bytes=LIMIT),
        cost_estimate=pl.CostEstimate(
            flops=0, bytes_accessed=6 * gates * 3 * third, transcendentals=0
        ),
    )(place, *gathered)
    return (
        hidden_next,
        cell_next,
        hidden_grad.reshape(hid, rows, width),
        cell_grad.reshape(hid, rows, width),
        weight_grad.T,
        bias_grad.reshape(gates),
    )


def solution(mesh):
    return jax.shard_map(
        body,
        mesh=mesh,
        in_specs=(
            P(None, "lat", "lon"),
            P(None, "lat", "lon"),
            P(None, "lat", "lon"),
            P(None, "lat", "lon"),
            P(None, "lat", "lon"),
            P("lat", None),
            P("lat", None),
            P(),
            P(),
        ),
        out_specs=(
            P(None, "lat", "lon"),
            P(("lat", "lon"), None, None),
            P(None, "lat", "lon"),
            P(None, "lat", "lon"),
            P(),
            P(),
        ),
        check_vma=False,
    )
```

```python
import math

import jax
import jax.numpy as jnp
from jax import lax
from jax.experimental import pallas as pl
from jax.experimental.pallas import tpu as pltpu
from jax.sharding import PartitionSpec as P

TILE = 16
F32 = jnp.float32
BF16 = jnp.bfloat16
LIMIT = 48 * 1024 * 1024
SMEM = pl.BlockSpec(memory_space=pltpu.SMEM)
VMEM = pl.BlockSpec(memory_space=pltpu.VMEM)


def call(kernel, outs, operands, scalars=0, scratch=(), flops=0, moved=0, after=(), fetched=0):
    count = len(operands)
    kept = count - fetched
    total = count + len(after)

    def run(*refs):
        if not fetched:
            kernel(*refs[:count], *refs[total:])
            return
        *rest, semaphores = refs[total:]
        buffers = rest[len(rest) - fetched :]
        copies = [
            pltpu.make_async_copy(source, target, semaphores.at[index])
            for index, (source, target) in enumerate(zip(refs[kept:count], buffers))
        ]
        for copy in copies:
            copy.start()
        waits = [copy.wait for copy in copies]
        kernel(waits, *refs[:kept], *buffers, *rest[: len(rest) - fetched])

    scratch = list(scratch)
    operands = list(operands)
    for index in range(kept, count):
        operands[index] = pltpu.with_memory_space_constraint(operands[index], pltpu.HBM)
    if fetched:
        scratch += [pltpu.VMEM(leaf.shape, leaf.dtype) for leaf in operands[kept:]]
        scratch.append(pltpu.SemaphoreType.DMA((fetched,)))

    return pl.pallas_call(
        run,
        out_shape=outs,
        in_specs=[SMEM] * scalars
        + [VMEM] * (kept - scalars)
        + [pl.BlockSpec(memory_space=pltpu.HBM)] * fetched
        + [VMEM] * len(after),
        out_specs=jax.tree.map(lambda _: VMEM, outs),
        scratch_shapes=scratch,
        compiler_params=pltpu.CompilerParams(vmem_limit_bytes=LIMIT),
        cost_estimate=pl.CostEstimate(flops=flops, bytes_accessed=moved, transcendentals=0),
    )(*operands, *after)


def lane_index(shape):
    return lax.broadcasted_iota(jnp.int32, shape, 1)


def sigmoid(values):
    return 0.5 * jnp.tanh(0.5 * values) + 0.5


def edges_kernel(waits, place_ref, forcing_ref, hidden_ref, wide_ref, *row_refs):
    inp, rows, width = forcing_ref.shape
    channels = inp + hidden_ref.shape[0]
    for wait in waits:
        wait()
    wide_ref[: inp * rows] = forcing_ref[...].astype(F32).reshape(inp * rows, width)
    wide_ref[inp * rows :] = hidden_ref[...].astype(F32).reshape((channels - inp) * rows, width)
    ends = [wide_ref[pl.ds(row, channels, stride=rows), :] for row in (0, rows - 1)]
    if len(row_refs) == 1:
        row_refs[0][...] = jnp.where(place_ref[0] == 0, ends[1], ends[0]).astype(BF16)
    else:
        for ref, end in zip(row_refs, ends):
            ref[...] = end.astype(BF16)


def columns_kernel(wide_ref, flat_ref, left_ref, right_ref):
    channels, width = left_ref.shape
    rows = wide_ref.shape[0] // channels
    lane = lane_index((channels, width))
    left = jnp.zeros((channels, width), F32)
    right = jnp.zeros((channels, width), F32)
    for row in range(rows):
        slab = wide_ref[pl.ds(row, channels, stride=rows), :]
        flat_ref[:, row * width : (row + 1) * width] = slab.astype(BF16)
        left = jnp.where(lane == row, slab[:, :1], left)
        right = jnp.where(lane == row, slab[:, width - 1 :], right)
    left_ref[...] = left.astype(BF16)
    right_ref[...] = right.astype(BF16)


def flatten_kernel(
    waits,
    b_ref,
    wt_ref,
    cell_ref,
    hcot_ref,
    ccot_ref,
    cell_out,
    hcot_out,
    ccot_out,
    w_ref,
    bias_ref,
    wide_ref,
):
    hid, rows, width = cell_ref.shape
    gates = wt_ref.shape[1]
    span = wt_ref.shape[0] // 3
    third = w_ref.shape[1] // 3
    waits[0]()
    bias_ref[...] = jnp.broadcast_to(b_ref[...], (bias_ref.shape[1], gates)).T
    waits[1]()
    blank = jnp.zeros((third - span, gates), F32)
    for index in range(3):
        block = wt_ref[index * span : (index + 1) * span].astype(F32)
        w_ref[:, index * third : (index + 1) * third] = (
            jnp.concatenate([block, blank], 0).T.astype(BF16)
        )
    for wait, source, target in zip(
        waits[2:], (cell_ref, hcot_ref, ccot_ref), (cell_out, hcot_out, ccot_out)
    ):
        wait()
        wide_ref[...] = source[...].astype(F32).reshape(hid * rows, width)
        for row in range(rows):
            target[:, row * width : (row + 1) * width] = wide_ref[
                pl.ds(row, hid, stride=rows), :
            ].astype(BF16)


def corners_kernel(rows, up_ref, down_ref, left_ref, right_ref, left_out, right_out):
    lane = lane_index(left_ref.shape)
    width = up_ref.shape[1]
    up = up_ref[...].astype(F32)
    down = down_ref[...].astype(F32)
    for column, source, target in ((0, left_ref, left_out), (width - 1, right_ref, right_out)):
        values = source[...].astype(F32)
        values = jnp.where(lane == rows, up[:, column : column + 1], values)
        values = jnp.where(lane == rows + 1, down[:, column : column + 1], values)
        target[...] = values.astype(BF16)


def step_kernel(
    place_ref,
    wet_ref,
    owner_ref,
    flat_ref,
    up_ref,
    down_ref,
    left_ref,
    right_ref,
    cell_ref,
    hcot_ref,
    ccot_ref,
    w_ref,
    b_ref,
    hidden_new_ref,
    cell_back_ref,
    tiles_ref,
    *rest,
):
    weight_refs, (delta_ref, taps_ref) = rest[:-2], rest[-2:]
    channels = flat_ref.shape[0]
    hid = cell_ref.shape[0]
    gates = w_ref.shape[0]
    width = up_ref.shape[1]
    rows = flat_ref.shape[1] // width
    tile_cols = width // TILE
    span = 3 * channels
    first_tile = place_ref[1] * tile_cols
    lane = lane_index((channels, width))

    def put(row, slab, before, after):
        lanes = slice(row * width, (row + 1) * width)
        shifted = jnp.where(lane == 0, before, pltpu.roll(slab, 1, 1))
        taps_ref[0:channels, lanes] = shifted.astype(BF16)
        taps_ref[channels : 2 * channels, lanes] = slab.astype(BF16)
        shifted = jnp.where(lane == width - 1, after, pltpu.roll(slab, width - 1, 1))
        taps_ref[2 * channels : span, lanes] = shifted.astype(BF16)

    left = left_ref[...].astype(F32)
    right = right_ref[...].astype(F32)
    for end, flag, ref in ((0, place_ref[2], up_ref), (1, place_ref[3], down_ref)):
        corner = slice(rows + end, rows + end + 1)
        slab, before, after = [
            jnp.where(flag == 1, values, 0.0)
            for values in (ref[...].astype(F32), left[:, corner], right[:, corner])
        ]
        put(end * (rows + 1), slab, before, after)
    for row in range(rows):
        slab = flat_ref[:, row * width : (row + 1) * width].astype(F32)
        put(row + 1, slab, left[:, row : row + 1], right[:, row : row + 1])
    extra = taps_ref.shape[0] - span
    ones = lax.broadcasted_iota(jnp.int32, (extra, taps_ref.shape[1]), 0) == 0
    taps_ref[span:] = jnp.where(ones, 1.0, 0.0).astype(BF16)

    live = jnp.zeros((1, width), F32)
    live_lane = lane_index((1, width)) // TILE
    for tile in range(tile_cols):
        wet = (wet_ref[0, first_tile + tile] > 0).astype(F32)
        live = jnp.where(live_lane == tile, wet, live)
    step = 2 if rows % 2 == 0 else 1
    chunk = step * width
    live = jnp.concatenate([live] * step, 1)
    third = w_ref.shape[1] // 3
    blank = jnp.zeros((gates, 2 * width), BF16)
    delta_ref[:, : 2 * width] = blank
    delta_ref[:, (rows + 2) * width :] = blank
    bias = jnp.concatenate([b_ref[...]] * step, 1)
    group = 128 // TILE
    states = []
    for start in range(0, rows, step):
        lows = [(start + row_off) * width for row_off in range(3)]
        stacked = jnp.concatenate([taps_ref[:, low : low + chunk] for low in lows], 0)
        pre = bias + jnp.dot(w_ref[...], stacked, preferred_element_type=F32)
        gate_in = sigmoid(pre[:hid])
        gate_forget = sigmoid(pre[hid : 2 * hid])
        gate_out = sigmoid(pre[2 * hid : 3 * hid])
        candidate = jnp.tanh(pre[3 * hid :])
        lanes = slice(start * width, start * width + chunk)
        cell_in = cell_ref[:, lanes].astype(F32)
        cell_new = gate_forget * cell_in + gate_in * candidate
        squash = jnp.tanh(cell_new)
        hidden_new = live * gate_out * squash
        back_h = live * hcot_ref[:, lanes].astype(F32)
        back_c = live * ccot_ref[:, lanes].astype(F32) + back_h * gate_out * (1.0 - squash * squash)
        cell_back = back_c * gate_forget
        carried = back_c * gate_in
        terms = (
            carried * candidate * (1.0 - gate_in),
            cell_back * cell_in * (1.0 - gate_forget),
            back_h * squash * gate_out * (1.0 - gate_out),
            carried * (1.0 - candidate * candidate),
        )
        low = (start + 2) * width
        for index, term in enumerate(terms):
            delta_ref[index * hid : (index + 1) * hid, low : low + chunk] = term.astype(BF16)
        hidden_new_ref[:, lanes] = hidden_new.astype(BF16)
        cell_back_ref[:, lanes] = cell_back
        for part in range(step):
            piece = slice(part * width, (part + 1) * width)
            states.append(cell_new[:, piece])
        if len(states) == group:
            block_of = lane_index((hid, width)) // TILE
            half = (start + step) // group - 1
            stride = group // 2
            while stride:
                upper = (block_of & stride) != 0
                mixed = list(states)
                for low_index in range(group):
                    if low_index & stride == 0:
                        first, second = states[low_index], states[low_index + stride]
                        mixed[low_index] = jnp.where(
                            upper, pltpu.roll(second, stride * TILE, 1), first
                        )
                        mixed[low_index + stride] = jnp.where(
                            upper, second, pltpu.roll(first, width - stride * TILE, 1)
                        )
                states = mixed
                stride //= 2
            for tile in range(tile_cols):
                tiles_ref[tile, :, half * 128 : (half + 1) * 128] = states[tile].astype(BF16)
            states = []
    delta = delta_ref[:, 2 * width : (rows + 2) * width]
    for row_off in range(3):
        part = lax.dot_general(
            taps_ref[:, row_off * width : (row_off + rows) * width],
            delta,
            (((1,), (1,)), ((), ())),
            preferred_element_type=F32,
        )
        place = slice(row_off * third, (row_off + 1) * third)
        if len(weight_refs) == 1:
            weight_refs[0][place] = part
        else:
            low, high = part[:, : gates // 2], part[:, gates // 2 :]
            weight_refs[0][place] = jnp.where(place_ref[0] == 0, low, high)
            weight_refs[1][place] = jnp.where(place_ref[0] == 0, high, low)


def spread_kernel(place_ref, delta_ref, wt_ref, grad_ref, *rest):
    row_refs, (left_ref, right_ref, side_ref) = rest[:-3], rest[-3:]
    hid = grad_ref.shape[0]
    width = left_ref.shape[1]
    rows = grad_ref.shape[1] // width
    channels = wt_ref.shape[0] // 9
    total = [None] * 3
    for col_off in range(3):
        for row_off in range(3):
            first = (row_off * 3 + col_off + 1) * channels - hid
            low = (2 - row_off) * width
            term = jnp.dot(
                wt_ref[first : first + hid],
                delta_ref[:, low : low + (rows + 2) * width],
                preferred_element_type=F32,
            )
            total[col_off] = term if row_off == 0 else total[col_off] + term
        side_ref[col_off] = total[col_off]
    lane = lane_index((hid, width))
    left = jnp.zeros((hid, width), F32)
    right = jnp.zeros((hid, width), F32)
    ends = []
    for row in range(rows + 2):
        lanes = slice(row * width, (row + 1) * width)
        before = side_ref[0, :, lanes]
        after = side_ref[2, :, lanes]
        slab = (
            side_ref[1, :, lanes]
            + jnp.where(lane == width - 1, 0.0, pltpu.roll(before, width - 1, 1))
            + jnp.where(lane == 0, 0.0, pltpu.roll(after, 1, 1))
        )
        if row in (0, rows + 1):
            corners = jnp.where(lane == 0, before[:, :1], 0.0)
            corners = jnp.where(lane == width - 1, after[:, width - 1 :], corners)
            ends.append((slab, corners))
        else:
            grad_ref[:, (row - 1) * width : row * width] = slab
            left = jnp.where(lane == row - 1, before[:, :1], left)
            right = jnp.where(lane == row - 1, after[:, width - 1 :], right)
    left_ref[...] = left.astype(BF16)
    right_ref[...] = right.astype(BF16)
    if len(row_refs) == 2:
        for index in range(2):
            row_refs[index][...] = jnp.where(
                place_ref[0] == 0, ends[1][index], ends[0][index]
            ).astype(BF16)
    else:
        for end in range(2):
            for index in range(2):
                row_refs[2 * end + index][...] = ends[end][index].astype(BF16)


def finish_kernel(
    place_ref,
    work_ref,
    hidden_new_ref,
    cell_back_ref,
    arrived_ref,
    grad_ref,
    up_ref,
    down_ref,
    up_left_ref,
    up_right_ref,
    down_left_ref,
    down_right_ref,
    left_ref,
    right_ref,
    hidden_next_ref,
    cell_grad_ref,
    cell_next_ref,
    hidden_grad_ref,
    wide_ref,
):
    hid = grad_ref.shape[0]
    width = up_ref.shape[1]
    rows = grad_ref.shape[1] // width
    lane = lane_index((hid, width))
    left = left_ref[...].astype(F32)
    right = right_ref[...].astype(F32)
    ends = {}
    for row, flag, refs in (
        (0, place_ref[2], (up_ref, up_left_ref, up_right_ref)),
        (rows - 1, place_ref[3], (down_ref, down_left_ref, down_right_ref)),
    ):
        slab, before, after = [ref[...].astype(F32) for ref in refs]
        slab = slab + jnp.where(lane == 0, before[:, width - 1 :], 0.0)
        slab = slab + jnp.where(lane == width - 1, after[:, :1], 0.0)
        ends[row] = jnp.where(flag == 1, slab, 0.0)
    for row in range(rows):
        lanes = slice(row * width, (row + 1) * width)
        slab = grad_ref[:, lanes]
        slab = slab + jnp.where(lane == 0, left[:, row : row + 1], 0.0)
        slab = slab + jnp.where(lane == width - 1, right[:, row : row + 1], 0.0)
        if row in ends:
            slab = slab + ends[row]
        hidden_grad_ref[pl.ds(row, hid, stride=rows), :] = slab
        cell_grad_ref[pl.ds(row, hid, stride=rows), :] = cell_back_ref[:, lanes]
        wide_ref[pl.ds(row, hid, stride=rows), :] = hidden_new_ref[:, lanes].astype(F32)
    hidden_next_ref[...] = wide_ref[...].reshape(hid, rows, width).astype(BF16)
    pieces = arrived_ref.shape[2]
    for index in range(cell_next_ref.shape[0]):
        for piece in range(cell_next_ref.shape[2] // pieces):
            cell_next_ref[index, :, piece * pieces : (piece + 1) * pieces] = arrived_ref[
                work_ref[index], piece * hid : (piece + 1) * hid
            ].astype(F32)


def split_bias(block, row):
    index = lax.broadcasted_iota(jnp.int32, block.shape, 0)
    rest = pltpu.roll(block - block.astype(BF16).astype(F32), 1, 0)
    return jnp.where(index == row + 1, rest, block)


def slots_kernel(place_ref, wet_ref, owner_ref, tiles_ref, out_ref):
    tile_cols, hid, cells = tiles_ref.shape
    slots, _, lanes = out_ref.shape
    out_ref[...] = jnp.zeros(out_ref.shape, BF16)
    for tile in range(tile_cols):
        index = place_ref[1] * tile_cols + tile

        @pl.when(wet_ref[0, index] > 0)
        def _():
            for piece in range(cells // lanes):
                out_ref[owner_ref[0, index], piece * hid : (piece + 1) * hid] = tiles_ref[
                    tile, :, piece * lanes : (piece + 1) * lanes
                ]


def pack_kernel(span, count, *refs):
    slots_ref, out_ref, token_ref, share_ref, semaphore = refs[count:]
    token_ref[...] = jnp.zeros(token_ref.shape, F32)
    slots, share, _ = share_ref.shape
    third = refs[0].shape[0] // 3
    total = refs[0][...]
    for ref in refs[1:count]:
        total = total + ref[...]
    total = jnp.concatenate([split_bias(total[:third], span), total[third:]], 0)
    for slot in range(slots):
        share_ref[slot] = total[slot * share : (slot + 1) * share].astype(BF16)
    state_rows = out_ref.shape[1] - share
    copy = pltpu.make_async_copy(share_ref, out_ref.at[:, pl.ds(state_rows, share)], semaphore)
    copy.start()
    copy.wait()


def sum_kernel(scaling, span, state_rows, place_ref, parts_ref, out_ref, token_ref):
    token_ref[...] = jnp.zeros(token_ref.shape, F32)
    total = parts_ref[0, state_rows:].astype(F32)
    for index in range(1, parts_ref.shape[0]):
        total = total + parts_ref[index, state_rows:].astype(F32)
    total = total * scaling
    share = total.shape[0]
    row = span % share
    index = lax.broadcasted_iota(jnp.int32, total.shape, 0)
    whole = jnp.where(index == row, total + pltpu.roll(total, share - 1, 0), total)
    total = jnp.where(place_ref[1] == span // share, split_bias(whole, row), total)
    for index in range(out_ref.shape[0]):
        out_ref[index] = total.astype(BF16)


def weights_kernel(span, place_ref, *refs):
    *parts, weight_ref, bias_ref = refs
    third = parts[0].shape[0] // 3
    half = parts[0].shape[1]
    for side in range(len(parts)):
        if len(parts) == 1:
            pick = parts[0][...]
        else:
            pick = jnp.where(place_ref[0] == side, parts[0][...], parts[1][...])
        pick = pick.astype(F32)
        lanes = slice(side * half, (side + 1) * half)
        for index in range(3):
            weight_ref[index * span : (index + 1) * span, lanes] = pick[
                index * third : index * third + span
            ]
        bias_ref[:, lanes] = pick[span : span + 1] + pick[span + 1 : span + 2]


def moved(values, lat_step, lon_step, lat_devices, lon_devices):
    pairs = []
    for lat in range(lat_devices):
        for lon in range(lon_devices):
            to_lat = lat + lat_step
            if lat_step and lat_devices == 2:
                to_lat = 1 - lat
            if 0 <= to_lat < lat_devices:
                to = to_lat * lon_devices + (lon + lon_step) % lon_devices
                pairs.append((lat * lon_devices + lon, to))
    return lax.ppermute(values, ("lat", "lon"), pairs)


def exchange(ends, corners, left, right, lat_devices, lon_devices):
    def go(values, lat_step, lon_step):
        return moved(values, lat_step, lon_step, lat_devices, lon_devices)

    from_left, from_right = go(right, 0, 1), go(left, 0, -1)
    if lat_devices == 2:
        row = go(ends[0], 1, 0)
        row_left, row_right = go(corners[0], 1, 1), go(corners[0], 1, -1)
        return (row, row, row_left, row_right, row_left, row_right, from_left, from_right)
    return (
        go(ends[1], 1, 0),
        go(ends[0], -1, 0),
        go(corners[1], 1, 1),
        go(corners[1], 1, -1),
        go(corners[0], -1, 1),
        go(corners[0], -1, -1),
        from_left,
        from_right,
    )


def body(forcing, hidden, cell, grad_hidden, grad_cell, wet_mask, tile_owner, w_gates, b_gates):
    lat_index = lax.axis_index("lat")
    lon_index = lax.axis_index("lon")
    lat_devices = lax.axis_size("lat")
    lon_devices = lax.axis_size("lon")
    inp, rows, width = forcing.shape
    hid = hidden.shape[0]
    channels = inp + hid
    gates = w_gates.shape[0]
    span = 3 * channels
    third = (span + 128) // 128 * 128
    cells = rows * width
    tile_cols = width // TILE
    capacity = tile_cols // 2
    place = jnp.stack(
        [
            lat_index,
            lon_index,
            (lat_index > 0).astype(jnp.int32),
            (lat_index < lat_devices - 1).astype(jnp.int32),
        ]
    ).astype(jnp.int32)

    def shaped(*shape, dtype=BF16):
        return jax.ShapeDtypeStruct(shape, dtype)

    end_count = 1 if lat_devices == 2 else 2
    wide, *ends = call(
        edges_kernel,
        (shaped(channels * rows, width, dtype=F32),) + (shaped(channels, width),) * end_count,
        (place, forcing, hidden),
        scalars=1,
        moved=4 * channels * cells,
        fetched=2,
    )
    flat, left, right = call(
        columns_kernel,
        (shaped(channels, cells),) + (shaped(channels, width),) * 2,
        (wide,),
        moved=6 * channels * cells,
    )
    if lat_devices == 2:
        up = down = moved(ends[0], 1, 0, lat_devices, lon_devices)
    else:
        up = moved(ends[1], 1, 0, lat_devices, lon_devices)
        down = moved(ends[0], -1, 0, lat_devices, lon_devices)
    left, right = call(
        lambda *refs: corners_kernel(rows, *refs),
        (shaped(channels, width),) * 2,
        (up, down, left, right),
        moved=8 * channels * width,
    )
    halo = (
        up,
        down,
        moved(right, 0, 1, lat_devices, lon_devices),
        moved(left, 0, -1, lat_devices, lon_devices),
    )
    w_turned = w_gates.T
    cell_flat, hcot_flat, ccot_flat, w_rows, bias = call(
        flatten_kernel,
        (shaped(hid, cells),) * 3
        + (shaped(gates, 3 * third), shaped(gates, width, dtype=F32)),
        (b_gates.reshape(1, gates), w_turned, cell, grad_hidden, grad_cell),
        scratch=[pltpu.VMEM((hid * rows, width), F32)],
        moved=12 * hid * cells,
        fetched=5,
    )
    halves = 2 if lat_devices == 2 else 1
    lanes = gates // halves
    hidden_new, cell_back, tiles, *weight_parts, delta = call(
        step_kernel,
        (
            shaped(hid, cells),
            shaped(hid, cells, dtype=F32),
            shaped(tile_cols, hid, TILE * TILE),
        )
        + (shaped(3 * third, lanes, dtype=F32),) * halves
        + (shaped(gates, (rows + 4) * width),),
        (place, wet_mask, tile_owner, flat, *halo)
        + (cell_flat, hcot_flat, ccot_flat, w_rows, bias),
        scalars=3,
        scratch=[pltpu.VMEM((third, (rows + 2) * width), BF16)],
        flops=4 * gates * 3 * span * cells,
        moved=16 * hid * cells,
    )
    swap = [(0, 1), (1, 0)]
    if halves == 2:
        weight_parts = (weight_parts[0], lax.ppermute(weight_parts[1], "lat", swap))
    else:
        weight_parts = (lax.psum(weight_parts[0], "lat"),)
    state_rows = hid * TILE * TILE // lanes
    share = 3 * third // lon_devices
    slots = call(
        slots_kernel,
        shaped(lon_devices, state_rows + share, lanes),
        (place, wet_mask, tile_owner, tiles),
        scalars=3,
        moved=4 * lon_devices * hid * TILE * TILE,
    )
    anywhere = pl.BlockSpec(memory_space=pl.ANY)
    count = len(weight_parts)
    outgoing, packed = pl.pallas_call(
        lambda *refs: pack_kernel(span, count, *refs),
        out_shape=(shaped(*slots.shape), shaped(8, 128, dtype=F32)),
        in_specs=[VMEM] * count + [anywhere],
        out_specs=(anywhere, VMEM),
        scratch_shapes=[
            pltpu.VMEM((lon_devices, share, lanes), BF16),
            pltpu.SemaphoreType.DMA(()),
        ],
        input_output_aliases={count: 0},
        compiler_params=pltpu.CompilerParams(vmem_limit_bytes=LIMIT),
        cost_estimate=pl.CostEstimate(
            flops=0, bytes_accessed=8 * gates * 3 * third, transcendentals=0
        ),
    )(*weight_parts, slots)
    incoming = lax.all_to_all(outgoing, "lon", 0, 0, tiled=True)
    grad_parts = call(
        spread_kernel,
        (shaped(hid, cells, dtype=F32),) + (shaped(hid, width),) * (2 * end_count + 2),
        (place, delta, w_turned),
        scalars=1,
        scratch=[pltpu.VMEM((3, hid, (rows + 2) * width), F32)],
        flops=2 * gates * 9 * hid * cells,
        moved=8 * gates * cells,
        after=(packed,),
    )
    grad_flat, grad_ends, grad_sides = grad_parts[0], grad_parts[1:-2], grad_parts[-2:]
    grad_halo = exchange(
        grad_ends[0::2], grad_ends[1::2], *grad_sides, lat_devices, lon_devices
    )
    scaling = 1.0 / math.sqrt(float(lat_devices * lon_devices * capacity * TILE * TILE))
    shares, shared = call(
        lambda *refs: sum_kernel(scaling, span, state_rows, *refs),
        (shaped(lon_devices, share, lanes), shaped(8, 128, dtype=F32)),
        (place, incoming),
        scalars=1,
        moved=2 * gates * 3 * third,
        after=grad_halo,
    )
    owned = (wet_mask > 0) & (tile_owner == lon_index)
    arrived = jnp.any(owned.reshape(lon_devices, tile_cols), 1)
    order = jnp.arange(lon_devices, dtype=jnp.int32)
    rank = jnp.sum((arrived[:, None] & (order[:, None] < order[None, :])).astype(jnp.int32), 0)
    placed = arrived[None, :] & (rank[None, :] == jnp.arange(capacity, dtype=jnp.int32)[:, None])
    work = jnp.sum(jnp.where(placed, order[None, :], 0), 1)
    finished = call(
        finish_kernel,
        (
            shaped(hid, rows, width),
            shaped(hid * rows, width, dtype=F32),
            shaped(capacity, hid, TILE * TILE, dtype=F32),
            shaped(hid * rows, width, dtype=F32),
        ),
        (place, work, hidden_new, cell_back, incoming, grad_flat, *grad_halo),
        scalars=2,
        scratch=[pltpu.VMEM((hid * rows, width), F32)],
        moved=32 * hid * cells,
        after=(shared,),
    )
    gathered = lax.all_to_all(shares, "lon", 0, 0, tiled=True).reshape(3 * third, lanes)
    gathered, finished = lax.optimization_barrier((gathered, finished))
    hidden_next, cell_grad, cell_next, hidden_grad = finished
    gathered = (gathered,)
    if halves == 2:
        gathered += (lax.ppermute(gathered[0], "lat", swap),)
    weight_grad, bias_grad = call(
        lambda *refs: weights_kernel(span, *refs),
        (shaped(3 * span, gates, dtype=F32), shaped(1, gates, dtype=F32)),
        (place, *gathered),
        scalars=1,
        moved=6 * gates * 3 * third,
    )
    return (
        hidden_next,
        cell_next,
        hidden_grad.reshape(hid, rows, width),
        cell_grad.reshape(hid, rows, width),
        weight_grad.T,
        bias_grad.reshape(gates),
    )


def solution(mesh):
    return jax.shard_map(
        body,
        mesh=mesh,
        in_specs=(
            P(None, "lat", "lon"),
            P(None, "lat", "lon"),
            P(None, "lat", "lon"),
            P(None, "lat", "lon"),
            P(None, "lat", "lon"),
            P("lat", None),
            P("lat", None),
            P(),
            P(),
        ),
        out_specs=(
            P(None, "lat", "lon"),
            P(("lat", "lon"), None, None),
            P(None, "lat", "lon"),
            P(None, "lat", "lon"),
            P(),
            P(),
        ),
        check_vma=False,
    )
```

```python
import math

import jax
import jax.numpy as jnp
from jax import lax
from jax.experimental import pallas as pl
from jax.experimental.pallas import tpu as pltpu
from jax.sharding import PartitionSpec as P

TILE = 16
F32 = jnp.float32
BF16 = jnp.bfloat16
LIMIT = 48 * 1024 * 1024
SMEM = pl.BlockSpec(memory_space=pltpu.SMEM)
VMEM = pl.BlockSpec(memory_space=pltpu.VMEM)


def call(kernel, outs, operands, scalars=0, scratch=(), flops=0, moved=0, after=(), fetched=0):
    count = len(operands)
    kept = count - fetched
    total = count + len(after)

    def run(*refs):
        if not fetched:
            kernel(*refs[:count], *refs[total:])
            return
        *rest, semaphores = refs[total:]
        buffers = rest[len(rest) - fetched :]
        copies = [
            pltpu.make_async_copy(source, target, semaphores.at[index])
            for index, (source, target) in enumerate(zip(refs[kept:count], buffers))
        ]
        for copy in copies:
            copy.start()
        waits = [copy.wait for copy in copies]
        kernel(waits, *refs[:kept], *buffers, *rest[: len(rest) - fetched])

    scratch = list(scratch)
    operands = list(operands)
    for index in range(kept, count):
        operands[index] = pltpu.with_memory_space_constraint(operands[index], pltpu.HBM)
    if fetched:
        scratch += [pltpu.VMEM(leaf.shape, leaf.dtype) for leaf in operands[kept:]]
        scratch.append(pltpu.SemaphoreType.DMA((fetched,)))

    return pl.pallas_call(
        run,
        out_shape=outs,
        in_specs=[SMEM] * scalars
        + [VMEM] * (kept - scalars)
        + [pl.BlockSpec(memory_space=pltpu.HBM)] * fetched
        + [VMEM] * len(after),
        out_specs=jax.tree.map(lambda _: VMEM, outs),
        scratch_shapes=scratch,
        compiler_params=pltpu.CompilerParams(vmem_limit_bytes=LIMIT),
        cost_estimate=pl.CostEstimate(flops=flops, bytes_accessed=moved, transcendentals=0),
    )(*operands, *after)


def lane_index(shape):
    return lax.broadcasted_iota(jnp.int32, shape, 1)


def sigmoid(values):
    return 0.5 * jnp.tanh(0.5 * values) + 0.5


def edges_kernel(waits, place_ref, forcing_ref, hidden_ref, wide_ref, *row_refs):
    inp, rows, width = forcing_ref.shape
    channels = inp + hidden_ref.shape[0]
    for wait in waits:
        wait()
    wide_ref[: inp * rows] = forcing_ref[...].astype(F32).reshape(inp * rows, width)
    wide_ref[inp * rows :] = hidden_ref[...].astype(F32).reshape((channels - inp) * rows, width)
    ends = [wide_ref[pl.ds(row, channels, stride=rows), :] for row in (0, rows - 1)]
    if len(row_refs) == 1:
        row_refs[0][...] = jnp.where(place_ref[0] == 0, ends[1], ends[0]).astype(BF16)
    else:
        for ref, end in zip(row_refs, ends):
            ref[...] = end.astype(BF16)


def columns_kernel(wide_ref, flat_ref, left_ref, right_ref):
    channels, width = left_ref.shape
    rows = wide_ref.shape[0] // channels
    lane = lane_index((channels, width))
    left = jnp.zeros((channels, width), F32)
    right = jnp.zeros((channels, width), F32)
    for row in range(rows):
        slab = wide_ref[pl.ds(row, channels, stride=rows), :]
        flat_ref[:, row * width : (row + 1) * width] = slab.astype(BF16)
        left = jnp.where(lane == row, slab[:, :1], left)
        right = jnp.where(lane == row, slab[:, width - 1 :], right)
    left_ref[...] = left.astype(BF16)
    right_ref[...] = right.astype(BF16)


def flatten_kernel(
    waits,
    b_ref,
    wt_ref,
    cell_ref,
    hcot_ref,
    ccot_ref,
    cell_out,
    hcot_out,
    ccot_out,
    w_ref,
    bias_ref,
    wide_ref,
):
    hid, rows, width = cell_ref.shape
    gates = wt_ref.shape[1]
    span = wt_ref.shape[0] // 3
    third = w_ref.shape[1] // 3
    waits[0]()
    bias_ref[...] = jnp.broadcast_to(b_ref[...], (bias_ref.shape[1], gates)).T
    waits[1]()
    blank = jnp.zeros((third - span, gates), F32)
    for index in range(3):
        block = wt_ref[index * span : (index + 1) * span].astype(F32)
        w_ref[:, index * third : (index + 1) * third] = (
            jnp.concatenate([block, blank], 0).T.astype(BF16)
        )
    for wait, source, target in zip(
        waits[2:], (cell_ref, hcot_ref, ccot_ref), (cell_out, hcot_out, ccot_out)
    ):
        wait()
        wide_ref[...] = source[...].astype(F32).reshape(hid * rows, width)
        for row in range(rows):
            target[:, row * width : (row + 1) * width] = wide_ref[
                pl.ds(row, hid, stride=rows), :
            ].astype(BF16)


def corners_kernel(rows, up_ref, down_ref, left_ref, right_ref, left_out, right_out):
    lane = lane_index(left_ref.shape)
    width = up_ref.shape[1]
    up = up_ref[...].astype(F32)
    down = down_ref[...].astype(F32)
    for column, source, target in ((0, left_ref, left_out), (width - 1, right_ref, right_out)):
        values = source[...].astype(F32)
        values = jnp.where(lane == rows, up[:, column : column + 1], values)
        values = jnp.where(lane == rows + 1, down[:, column : column + 1], values)
        target[...] = values.astype(BF16)


def step_kernel(
    place_ref,
    wet_ref,
    owner_ref,
    flat_ref,
    up_ref,
    down_ref,
    left_ref,
    right_ref,
    cell_ref,
    hcot_ref,
    ccot_ref,
    w_ref,
    b_ref,
    hidden_new_ref,
    cell_back_ref,
    cell_new_ref,
    *rest,
):
    weight_refs, (delta_ref, taps_ref) = rest[:-2], rest[-2:]
    channels = flat_ref.shape[0]
    hid = cell_ref.shape[0]
    gates = w_ref.shape[0]
    width = up_ref.shape[1]
    rows = flat_ref.shape[1] // width
    tile_cols = width // TILE
    span = 3 * channels
    first_tile = place_ref[1] * tile_cols
    lane = lane_index((channels, width))

    def put(row, slab, before, after):
        lanes = slice(row * width, (row + 1) * width)
        shifted = jnp.where(lane == 0, before, pltpu.roll(slab, 1, 1))
        taps_ref[0:channels, lanes] = shifted.astype(BF16)
        taps_ref[channels : 2 * channels, lanes] = slab.astype(BF16)
        shifted = jnp.where(lane == width - 1, after, pltpu.roll(slab, width - 1, 1))
        taps_ref[2 * channels : span, lanes] = shifted.astype(BF16)

    left = left_ref[...].astype(F32)
    right = right_ref[...].astype(F32)
    for end, flag, ref in ((0, place_ref[2], up_ref), (1, place_ref[3], down_ref)):
        corner = slice(rows + end, rows + end + 1)
        slab, before, after = [
            jnp.where(flag == 1, values, 0.0)
            for values in (ref[...].astype(F32), left[:, corner], right[:, corner])
        ]
        put(end * (rows + 1), slab, before, after)
    for row in range(rows):
        slab = flat_ref[:, row * width : (row + 1) * width].astype(F32)
        put(row + 1, slab, left[:, row : row + 1], right[:, row : row + 1])
    extra = taps_ref.shape[0] - span
    ones = lax.broadcasted_iota(jnp.int32, (extra, taps_ref.shape[1]), 0) == 0
    taps_ref[span:] = jnp.where(ones, 1.0, 0.0).astype(BF16)

    live = jnp.zeros((1, width), F32)
    live_lane = lane_index((1, width)) // TILE
    for tile in range(tile_cols):
        wet = (wet_ref[0, first_tile + tile] > 0).astype(F32)
        live = jnp.where(live_lane == tile, wet, live)
    step = 2 if rows % 2 == 0 else 1
    chunk = step * width
    live = jnp.concatenate([live] * step, 1)
    third = w_ref.shape[1] // 3
    blank = jnp.zeros((gates, 2 * width), BF16)
    delta_ref[:, : 2 * width] = blank
    delta_ref[:, (rows + 2) * width :] = blank
    bias = jnp.concatenate([b_ref[...]] * step, 1)
    for start in range(0, rows, step):
        lows = [(start + row_off) * width for row_off in range(3)]
        stacked = jnp.concatenate([taps_ref[:, low : low + chunk] for low in lows], 0)
        pre = bias + jnp.dot(w_ref[...], stacked, preferred_element_type=F32)
        gate_in = sigmoid(pre[:hid])
        gate_forget = sigmoid(pre[hid : 2 * hid])
        gate_out = sigmoid(pre[2 * hid : 3 * hid])
        candidate = jnp.tanh(pre[3 * hid :])
        lanes = slice(start * width, start * width + chunk)
        cell_in = cell_ref[:, lanes].astype(F32)
        cell_new = gate_forget * cell_in + gate_in * candidate
        squash = jnp.tanh(cell_new)
        hidden_new = live * gate_out * squash
        back_h = live * hcot_ref[:, lanes].astype(F32)
        back_c = live * ccot_ref[:, lanes].astype(F32) + back_h * gate_out * (1.0 - squash * squash)
        cell_back = back_c * gate_forget
        carried = back_c * gate_in
        terms = (
            carried * candidate * (1.0 - gate_in),
            cell_back * cell_in * (1.0 - gate_forget),
            back_h * squash * gate_out * (1.0 - gate_out),
            carried * (1.0 - candidate * candidate),
        )
        low = (start + 2) * width
        for index, term in enumerate(terms):
            delta_ref[index * hid : (index + 1) * hid, low : low + chunk] = term.astype(BF16)
        hidden_new_ref[:, lanes] = hidden_new.astype(BF16)
        cell_back_ref[:, lanes] = cell_back
        cell_new_ref[:, lanes] = cell_new
    delta = delta_ref[:, 2 * width : (rows + 2) * width]
    for row_off in range(3):
        part = lax.dot_general(
            taps_ref[:, row_off * width : (row_off + rows) * width],
            delta,
            (((1,), (1,)), ((), ())),
            preferred_element_type=F32,
        )
        place = slice(row_off * third, (row_off + 1) * third)
        if len(weight_refs) == 1:
            weight_refs[0][place] = part
        else:
            low, high = part[:, : gates // 2], part[:, gates // 2 :]
            weight_refs[0][place] = jnp.where(place_ref[0] == 0, low, high)
            weight_refs[1][place] = jnp.where(place_ref[0] == 0, high, low)


def spread_kernel(place_ref, delta_ref, wt_ref, grad_ref, *rest):
    row_refs, (left_ref, right_ref, side_ref) = rest[:-3], rest[-3:]
    hid = grad_ref.shape[0]
    width = left_ref.shape[1]
    rows = grad_ref.shape[1] // width
    channels = wt_ref.shape[0] // 9
    total = [None] * 3
    for col_off in range(3):
        for row_off in range(3):
            first = (row_off * 3 + col_off + 1) * channels - hid
            low = (2 - row_off) * width
            term = jnp.dot(
                wt_ref[first : first + hid],
                delta_ref[:, low : low + (rows + 2) * width],
                preferred_element_type=F32,
            )
            total[col_off] = term if row_off == 0 else total[col_off] + term
        side_ref[col_off] = total[col_off]
    lane = lane_index((hid, width))
    left = jnp.zeros((hid, width), F32)
    right = jnp.zeros((hid, width), F32)
    ends = []
    for row in range(rows + 2):
        lanes = slice(row * width, (row + 1) * width)
        before = side_ref[0, :, lanes]
        after = side_ref[2, :, lanes]
        slab = (
            side_ref[1, :, lanes]
            + jnp.where(lane == width - 1, 0.0, pltpu.roll(before, width - 1, 1))
            + jnp.where(lane == 0, 0.0, pltpu.roll(after, 1, 1))
        )
        if row in (0, rows + 1):
            corners = jnp.where(lane == 0, before[:, :1], 0.0)
            corners = jnp.where(lane == width - 1, after[:, width - 1 :], corners)
            ends.append((slab, corners))
        else:
            grad_ref[:, (row - 1) * width : row * width] = slab
            left = jnp.where(lane == row - 1, before[:, :1], left)
            right = jnp.where(lane == row - 1, after[:, width - 1 :], right)
    left_ref[...] = left.astype(BF16)
    right_ref[...] = right.astype(BF16)
    if len(row_refs) == 2:
        for index in range(2):
            row_refs[index][...] = jnp.where(
                place_ref[0] == 0, ends[1][index], ends[0][index]
            ).astype(BF16)
    else:
        for end in range(2):
            for index in range(2):
                row_refs[2 * end + index][...] = ends[end][index].astype(BF16)


def finish_kernel(
    place_ref,
    work_ref,
    hidden_new_ref,
    cell_back_ref,
    arrived_ref,
    grad_ref,
    up_ref,
    down_ref,
    up_left_ref,
    up_right_ref,
    down_left_ref,
    down_right_ref,
    left_ref,
    right_ref,
    hidden_next_ref,
    cell_grad_ref,
    cell_next_ref,
    hidden_grad_ref,
    wide_ref,
):
    hid = grad_ref.shape[0]
    width = up_ref.shape[1]
    rows = grad_ref.shape[1] // width
    lane = lane_index((hid, width))
    left = left_ref[...].astype(F32)
    right = right_ref[...].astype(F32)
    ends = {}
    for row, flag, refs in (
        (0, place_ref[2], (up_ref, up_left_ref, up_right_ref)),
        (rows - 1, place_ref[3], (down_ref, down_left_ref, down_right_ref)),
    ):
        slab, before, after = [ref[...].astype(F32) for ref in refs]
        slab = slab + jnp.where(lane == 0, before[:, width - 1 :], 0.0)
        slab = slab + jnp.where(lane == width - 1, after[:, :1], 0.0)
        ends[row] = jnp.where(flag == 1, slab, 0.0)
    for row in range(rows):
        lanes = slice(row * width, (row + 1) * width)
        slab = grad_ref[:, lanes]
        slab = slab + jnp.where(lane == 0, left[:, row : row + 1], 0.0)
        slab = slab + jnp.where(lane == width - 1, right[:, row : row + 1], 0.0)
        if row in ends:
            slab = slab + ends[row]
        hidden_grad_ref[pl.ds(row, hid, stride=rows), :] = slab
        cell_grad_ref[pl.ds(row, hid, stride=rows), :] = cell_back_ref[:, lanes]
        wide_ref[pl.ds(row, hid, stride=rows), :] = hidden_new_ref[:, lanes].astype(F32)
    hidden_next_ref[...] = wide_ref[...].reshape(hid, rows, width).astype(BF16)
    pieces = arrived_ref.shape[2]
    for index in range(cell_next_ref.shape[0]):
        for piece in range(cell_next_ref.shape[2] // pieces):
            cell_next_ref[index, :, piece * pieces : (piece + 1) * pieces] = arrived_ref[
                work_ref[index], piece * hid : (piece + 1) * hid
            ].astype(F32)


def split_bias(block, row):
    index = lax.broadcasted_iota(jnp.int32, block.shape, 0)
    rest = pltpu.roll(block - block.astype(BF16).astype(F32), 1, 0)
    return jnp.where(index == row + 1, rest, block)


def slots_kernel(
    place_ref, wet_ref, owner_ref, state_ref, out_ref, tiles_ref, slots_ref, semaphores
):
    tile_cols, hid, cells = tiles_ref.shape
    slots, state_rows, lanes = slots_ref.shape
    width = tile_cols * TILE
    rows = state_ref.shape[1] // width
    group = 128 // TILE
    block_of = lane_index((hid, width)) // TILE
    slots_ref[...] = jnp.zeros(slots_ref.shape, BF16)
    for half in range(rows // group):
        states = [
            state_ref[:, row * width : (row + 1) * width]
            for row in range(half * group, (half + 1) * group)
        ]
        stride = group // 2
        while stride:
            upper = (block_of & stride) != 0
            mixed = list(states)
            for low in range(group):
                if low & stride == 0:
                    first, second = states[low], states[low + stride]
                    mixed[low] = jnp.where(upper, pltpu.roll(second, stride * TILE, 1), first)
                    mixed[low + stride] = jnp.where(
                        upper, second, pltpu.roll(first, width - stride * TILE, 1)
                    )
            states = mixed
            stride //= 2
        for tile in range(tile_cols):
            tiles_ref[tile, :, half * 128 : (half + 1) * 128] = states[tile].astype(BF16)
    for tile in range(tile_cols):
        index = place_ref[1] * tile_cols + tile

        @pl.when(wet_ref[0, index] > 0)
        def _():
            for piece in range(cells // lanes):
                slots_ref[owner_ref[0, index], piece * hid : (piece + 1) * hid] = tiles_ref[
                    tile, :, piece * lanes : (piece + 1) * lanes
                ]

    count = semaphores.shape[0]
    some = slots // count
    copies = [
        pltpu.make_async_copy(
            slots_ref.at[pl.ds(index * some, some)],
            out_ref.at[pl.ds(index * some, some), pl.ds(0, state_rows)],
            semaphores.at[index],
        )
        for index in range(count)
    ]
    for copy in copies:
        copy.start()
    for copy in copies:
        copy.wait()


def pack_kernel(span, count, *refs):
    slots_ref, out_ref, token_ref, share_ref, semaphore = refs[count:]
    token_ref[...] = jnp.zeros(token_ref.shape, F32)
    slots, share, _ = share_ref.shape
    third = refs[0].shape[0] // 3
    total = refs[0][...]
    for ref in refs[1:count]:
        total = total + ref[...]
    total = jnp.concatenate([split_bias(total[:third], span), total[third:]], 0)
    for slot in range(slots):
        share_ref[slot] = total[slot * share : (slot + 1) * share].astype(BF16)
    state_rows = out_ref.shape[1] - share
    copy = pltpu.make_async_copy(share_ref, out_ref.at[:, pl.ds(state_rows, share)], semaphore)
    copy.start()
    copy.wait()


def sum_kernel(scaling, span, state_rows, place_ref, parts_ref, out_ref, token_ref):
    token_ref[...] = jnp.zeros(token_ref.shape, F32)
    total = parts_ref[0, state_rows:].astype(F32)
    for index in range(1, parts_ref.shape[0]):
        total = total + parts_ref[index, state_rows:].astype(F32)
    total = total * scaling
    share = total.shape[0]
    row = span % share
    index = lax.broadcasted_iota(jnp.int32, total.shape, 0)
    whole = jnp.where(index == row, total + pltpu.roll(total, share - 1, 0), total)
    total = jnp.where(place_ref[1] == span // share, split_bias(whole, row), total)
    for index in range(out_ref.shape[0]):
        out_ref[index] = total.astype(BF16)


def weights_kernel(span, place_ref, *refs):
    *parts, weight_ref, bias_ref = refs
    third = parts[0].shape[0] // 3
    half = parts[0].shape[1]
    for side in range(len(parts)):
        if len(parts) == 1:
            pick = parts[0][...]
        else:
            pick = jnp.where(place_ref[0] == side, parts[0][...], parts[1][...])
        pick = pick.astype(F32)
        lanes = slice(side * half, (side + 1) * half)
        for index in range(3):
            weight_ref[index * span : (index + 1) * span, lanes] = pick[
                index * third : index * third + span
            ]
        bias_ref[:, lanes] = pick[span : span + 1] + pick[span + 1 : span + 2]


def moved(values, lat_step, lon_step, lat_devices, lon_devices):
    pairs = []
    for lat in range(lat_devices):
        for lon in range(lon_devices):
            to_lat = lat + lat_step
            if lat_step and lat_devices == 2:
                to_lat = 1 - lat
            if 0 <= to_lat < lat_devices:
                to = to_lat * lon_devices + (lon + lon_step) % lon_devices
                pairs.append((lat * lon_devices + lon, to))
    return lax.ppermute(values, ("lat", "lon"), pairs)


def exchange(ends, corners, left, right, lat_devices, lon_devices):
    def go(values, lat_step, lon_step):
        return moved(values, lat_step, lon_step, lat_devices, lon_devices)

    from_left, from_right = go(right, 0, 1), go(left, 0, -1)
    if lat_devices == 2:
        row = go(ends[0], 1, 0)
        row_left, row_right = go(corners[0], 1, 1), go(corners[0], 1, -1)
        return (row, row, row_left, row_right, row_left, row_right, from_left, from_right)
    return (
        go(ends[1], 1, 0),
        go(ends[0], -1, 0),
        go(corners[1], 1, 1),
        go(corners[1], 1, -1),
        go(corners[0], -1, 1),
        go(corners[0], -1, -1),
        from_left,
        from_right,
    )


def body(forcing, hidden, cell, grad_hidden, grad_cell, wet_mask, tile_owner, w_gates, b_gates):
    lat_index = lax.axis_index("lat")
    lon_index = lax.axis_index("lon")
    lat_devices = lax.axis_size("lat")
    lon_devices = lax.axis_size("lon")
    inp, rows, width = forcing.shape
    hid = hidden.shape[0]
    channels = inp + hid
    gates = w_gates.shape[0]
    span = 3 * channels
    third = (span + 128) // 128 * 128
    cells = rows * width
    tile_cols = width // TILE
    capacity = tile_cols // 2
    place = jnp.stack(
        [
            lat_index,
            lon_index,
            (lat_index > 0).astype(jnp.int32),
            (lat_index < lat_devices - 1).astype(jnp.int32),
        ]
    ).astype(jnp.int32)

    def shaped(*shape, dtype=BF16):
        return jax.ShapeDtypeStruct(shape, dtype)

    end_count = 1 if lat_devices == 2 else 2
    wide, *ends = call(
        edges_kernel,
        (shaped(channels * rows, width, dtype=F32),) + (shaped(channels, width),) * end_count,
        (place, forcing, hidden),
        scalars=1,
        moved=4 * channels * cells,
        fetched=2,
    )
    flat, left, right = call(
        columns_kernel,
        (shaped(channels, cells),) + (shaped(channels, width),) * 2,
        (wide,),
        moved=6 * channels * cells,
    )
    if lat_devices == 2:
        up = down = moved(ends[0], 1, 0, lat_devices, lon_devices)
    else:
        up = moved(ends[1], 1, 0, lat_devices, lon_devices)
        down = moved(ends[0], -1, 0, lat_devices, lon_devices)
    left, right = call(
        lambda *refs: corners_kernel(rows, *refs),
        (shaped(channels, width),) * 2,
        (up, down, left, right),
        moved=8 * channels * width,
    )
    halo = (
        up,
        down,
        moved(right, 0, 1, lat_devices, lon_devices),
        moved(left, 0, -1, lat_devices, lon_devices),
    )
    w_turned = w_gates.T
    cell_flat, hcot_flat, ccot_flat, w_rows, bias = call(
        flatten_kernel,
        (shaped(hid, cells),) * 3
        + (shaped(gates, 3 * third), shaped(gates, width, dtype=F32)),
        (b_gates.reshape(1, gates), w_turned, cell, grad_hidden, grad_cell),
        scratch=[pltpu.VMEM((hid * rows, width), F32)],
        moved=12 * hid * cells,
        fetched=5,
    )
    halves = 2 if lat_devices == 2 else 1
    lanes = gates // halves
    hidden_new, cell_back, cell_new, *weight_parts, delta = call(
        step_kernel,
        (
            shaped(hid, cells),
            shaped(hid, cells, dtype=F32),
            shaped(hid, cells, dtype=F32),
        )
        + (shaped(3 * third, lanes, dtype=F32),) * halves
        + (shaped(gates, (rows + 4) * width),),
        (place, wet_mask, tile_owner, flat, *halo)
        + (cell_flat, hcot_flat, ccot_flat, w_rows, bias),
        scalars=3,
        scratch=[pltpu.VMEM((third, (rows + 2) * width), BF16)],
        flops=4 * gates * 3 * span * cells,
        moved=16 * hid * cells,
    )
    swap = [(0, 1), (1, 0)]
    if halves == 2:
        weight_parts = (weight_parts[0], lax.ppermute(weight_parts[1], "lat", swap))
    else:
        weight_parts = (lax.psum(weight_parts[0], "lat"),)
    state_rows = hid * TILE * TILE // lanes
    share = 3 * third // lon_devices
    anywhere = pl.BlockSpec(memory_space=pl.ANY)
    copies = 4 if lon_devices % 4 == 0 else 1
    slots = pl.pallas_call(
        slots_kernel,
        out_shape=shaped(lon_devices, state_rows + share, lanes),
        in_specs=[SMEM] * 3 + [VMEM],
        out_specs=anywhere,
        scratch_shapes=[
            pltpu.VMEM((tile_cols, hid, TILE * TILE), BF16),
            pltpu.VMEM((lon_devices, state_rows, lanes), BF16),
            pltpu.SemaphoreType.DMA((copies,)),
        ],
        compiler_params=pltpu.CompilerParams(vmem_limit_bytes=LIMIT),
        cost_estimate=pl.CostEstimate(
            flops=0, bytes_accessed=4 * lon_devices * hid * TILE * TILE, transcendentals=0
        ),
    )(place, wet_mask, tile_owner, cell_new)
    count = len(weight_parts)
    outgoing, packed = pl.pallas_call(
        lambda *refs: pack_kernel(span, count, *refs),
        out_shape=(shaped(*slots.shape), shaped(8, 128, dtype=F32)),
        in_specs=[VMEM] * count + [anywhere],
        out_specs=(anywhere, VMEM),
        scratch_shapes=[
            pltpu.VMEM((lon_devices, share, lanes), BF16),
            pltpu.SemaphoreType.DMA(()),
        ],
        input_output_aliases={count: 0},
        compiler_params=pltpu.CompilerParams(vmem_limit_bytes=LIMIT),
        cost_estimate=pl.CostEstimate(
            flops=0, bytes_accessed=8 * gates * 3 * third, transcendentals=0
        ),
    )(*weight_parts, slots)
    incoming = lax.all_to_all(outgoing, "lon", 0, 0, tiled=True)
    grad_parts = call(
        spread_kernel,
        (shaped(hid, cells, dtype=F32),) + (shaped(hid, width),) * (2 * end_count + 2),
        (place, delta, w_turned),
        scalars=1,
        scratch=[pltpu.VMEM((3, hid, (rows + 2) * width), F32)],
        flops=2 * gates * 9 * hid * cells,
        moved=8 * gates * cells,
        after=(packed,),
    )
    grad_flat, grad_ends, grad_sides = grad_parts[0], grad_parts[1:-2], grad_parts[-2:]
    grad_halo = exchange(
        grad_ends[0::2], grad_ends[1::2], *grad_sides, lat_devices, lon_devices
    )
    scaling = 1.0 / math.sqrt(float(lat_devices * lon_devices * capacity * TILE * TILE))
    shares, shared = call(
        lambda *refs: sum_kernel(scaling, span, state_rows, *refs),
        (shaped(lon_devices, share, lanes), shaped(8, 128, dtype=F32)),
        (place, incoming),
        scalars=1,
        moved=2 * gates * 3 * third,
        after=grad_halo,
    )
    owned = (wet_mask > 0) & (tile_owner == lon_index)
    arrived = jnp.any(owned.reshape(lon_devices, tile_cols), 1)
    order = jnp.arange(lon_devices, dtype=jnp.int32)
    rank = jnp.sum((arrived[:, None] & (order[:, None] < order[None, :])).astype(jnp.int32), 0)
    placed = arrived[None, :] & (rank[None, :] == jnp.arange(capacity, dtype=jnp.int32)[:, None])
    work = jnp.sum(jnp.where(placed, order[None, :], 0), 1)
    finished = call(
        finish_kernel,
        (
            shaped(hid, rows, width),
            shaped(hid * rows, width, dtype=F32),
            shaped(capacity, hid, TILE * TILE, dtype=F32),
            shaped(hid * rows, width, dtype=F32),
        ),
        (place, work, hidden_new, cell_back, incoming, grad_flat, *grad_halo),
        scalars=2,
        scratch=[pltpu.VMEM((hid * rows, width), F32)],
        moved=32 * hid * cells,
        after=(shared,),
    )
    gathered = lax.all_to_all(shares, "lon", 0, 0, tiled=True).reshape(3 * third, lanes)
    gathered, finished = lax.optimization_barrier((gathered, finished))
    hidden_next, cell_grad, cell_next, hidden_grad = finished
    gathered = (gathered,)
    if halves == 2:
        gathered += (lax.ppermute(gathered[0], "lat", swap),)
    weight_grad, bias_grad = call(
        lambda *refs: weights_kernel(span, *refs),
        (shaped(3 * span, gates, dtype=F32), shaped(1, gates, dtype=F32)),
        (place, *gathered),
        scalars=1,
        moved=6 * gates * 3 * third,
    )
    return (
        hidden_next,
        cell_next,
        hidden_grad.reshape(hid, rows, width),
        cell_grad.reshape(hid, rows, width),
        weight_grad.T,
        bias_grad.reshape(gates),
    )


def solution(mesh):
    return jax.shard_map(
        body,
        mesh=mesh,
        in_specs=(
            P(None, "lat", "lon"),
            P(None, "lat", "lon"),
            P(None, "lat", "lon"),
            P(None, "lat", "lon"),
            P(None, "lat", "lon"),
            P("lat", None),
            P("lat", None),
            P(),
            P(),
        ),
        out_specs=(
            P(None, "lat", "lon"),
            P(("lat", "lon"), None, None),
            P(None, "lat", "lon"),
            P(None, "lat", "lon"),
            P(),
            P(),
        ),
        check_vma=False,
    )
```

```python
import math

import jax
import jax.numpy as jnp
from jax import lax
from jax.experimental import pallas as pl
from jax.experimental.pallas import tpu as pltpu
from jax.sharding import PartitionSpec as P

TILE = 16
F32 = jnp.float32
BF16 = jnp.bfloat16
LIMIT = 48 * 1024 * 1024
SMEM = pl.BlockSpec(memory_space=pltpu.SMEM)
VMEM = pl.BlockSpec(memory_space=pltpu.VMEM)


def call(kernel, outs, operands, scalars=0, scratch=(), flops=0, moved=0, after=(), fetched=0):
    count = len(operands)
    kept = count - fetched
    total = count + len(after)

    def run(*refs):
        if not fetched:
            kernel(*refs[:count], *refs[total:])
            return
        *rest, semaphores = refs[total:]
        buffers = rest[len(rest) - fetched :]
        copies = [
            pltpu.make_async_copy(source, target, semaphores.at[index])
            for index, (source, target) in enumerate(zip(refs[kept:count], buffers))
        ]
        for copy in copies:
            copy.start()
        waits = [copy.wait for copy in copies]
        kernel(waits, *refs[:kept], *buffers, *rest[: len(rest) - fetched])

    scratch = list(scratch)
    operands = list(operands)
    for index in range(kept, count):
        operands[index] = pltpu.with_memory_space_constraint(operands[index], pltpu.HBM)
    if fetched:
        scratch += [pltpu.VMEM(leaf.shape, leaf.dtype) for leaf in operands[kept:]]
        scratch.append(pltpu.SemaphoreType.DMA((fetched,)))

    return pl.pallas_call(
        run,
        out_shape=outs,
        in_specs=[SMEM] * scalars
        + [VMEM] * (kept - scalars)
        + [pl.BlockSpec(memory_space=pltpu.HBM)] * fetched
        + [VMEM] * len(after),
        out_specs=jax.tree.map(lambda _: VMEM, outs),
        scratch_shapes=scratch,
        compiler_params=pltpu.CompilerParams(vmem_limit_bytes=LIMIT),
        cost_estimate=pl.CostEstimate(flops=flops, bytes_accessed=moved, transcendentals=0),
    )(*operands, *after)


def lane_index(shape):
    return lax.broadcasted_iota(jnp.int32, shape, 1)


def sigmoid(values):
    return 0.5 * jnp.tanh(0.5 * values) + 0.5


def edges_kernel(waits, place_ref, forcing_ref, hidden_ref, wide_ref, *row_refs):
    inp, rows, width = forcing_ref.shape
    channels = inp + hidden_ref.shape[0]
    for wait in waits:
        wait()
    wide_ref[: inp * rows] = forcing_ref[...].astype(F32).reshape(inp * rows, width)
    wide_ref[inp * rows :] = hidden_ref[...].astype(F32).reshape((channels - inp) * rows, width)
    ends = [wide_ref[pl.ds(row, channels, stride=rows), :] for row in (0, rows - 1)]
    if len(row_refs) == 1:
        row_refs[0][...] = jnp.where(place_ref[0] == 0, ends[1], ends[0]).astype(BF16)
    else:
        for ref, end in zip(row_refs, ends):
            ref[...] = end.astype(BF16)


def columns_kernel(wide_ref, flat_ref, left_ref, right_ref):
    channels, width = left_ref.shape
    rows = wide_ref.shape[0] // channels
    lane = lane_index((channels, width))
    left = jnp.zeros((channels, width), F32)
    right = jnp.zeros((channels, width), F32)
    for row in range(rows):
        slab = wide_ref[pl.ds(row, channels, stride=rows), :]
        flat_ref[:, row * width : (row + 1) * width] = slab.astype(BF16)
        left = jnp.where(lane == row, slab[:, :1], left)
        right = jnp.where(lane == row, slab[:, width - 1 :], right)
    left_ref[...] = left.astype(BF16)
    right_ref[...] = right.astype(BF16)


def flatten_kernel(
    waits,
    b_ref,
    wt_ref,
    cell_ref,
    hcot_ref,
    ccot_ref,
    cell_out,
    hcot_out,
    ccot_out,
    w_ref,
    bias_ref,
    wide_ref,
):
    hid, rows, width = cell_ref.shape
    gates = wt_ref.shape[1]
    span = wt_ref.shape[0] // 3
    third = w_ref.shape[1] // 3
    waits[0]()
    bias_ref[...] = jnp.broadcast_to(b_ref[...], (bias_ref.shape[1], gates)).T
    waits[1]()
    blank = jnp.zeros((third - span, gates), F32)
    for index in range(3):
        block = wt_ref[index * span : (index + 1) * span].astype(F32)
        w_ref[:, index * third : (index + 1) * third] = (
            jnp.concatenate([block, blank], 0).T.astype(BF16)
        )
    for wait, source, target in zip(
        waits[2:], (cell_ref, hcot_ref, ccot_ref), (cell_out, hcot_out, ccot_out)
    ):
        wait()
        wide_ref[...] = source[...].astype(F32).reshape(hid * rows, width)
        for row in range(rows):
            target[:, row * width : (row + 1) * width] = wide_ref[
                pl.ds(row, hid, stride=rows), :
            ].astype(BF16)


def corners_kernel(rows, up_ref, down_ref, left_ref, right_ref, left_out, right_out):
    lane = lane_index(left_ref.shape)
    width = up_ref.shape[1]
    up = up_ref[...].astype(F32)
    down = down_ref[...].astype(F32)
    for column, source, target in ((0, left_ref, left_out), (width - 1, right_ref, right_out)):
        values = source[...].astype(F32)
        values = jnp.where(lane == rows, up[:, column : column + 1], values)
        values = jnp.where(lane == rows + 1, down[:, column : column + 1], values)
        target[...] = values.astype(BF16)


def step_kernel(
    place_ref,
    wet_ref,
    owner_ref,
    flat_ref,
    up_ref,
    down_ref,
    left_ref,
    right_ref,
    cell_ref,
    hcot_ref,
    ccot_ref,
    w_ref,
    b_ref,
    hidden_new_ref,
    cell_back_ref,
    tiles_ref,
    *rest,
):
    weight_refs, (delta_ref, taps_ref) = rest[:-2], rest[-2:]
    channels = flat_ref.shape[0]
    hid = cell_ref.shape[0]
    gates = w_ref.shape[0]
    width = up_ref.shape[1]
    rows = flat_ref.shape[1] // width
    tile_cols = width // TILE
    span = 3 * channels
    first_tile = place_ref[1] * tile_cols
    lane = lane_index((channels, width))

    def put(row, slab, before, after):
        lanes = slice(row * width, (row + 1) * width)
        shifted = jnp.where(lane == 0, before, pltpu.roll(slab, 1, 1))
        taps_ref[0:channels, lanes] = shifted.astype(BF16)
        taps_ref[channels : 2 * channels, lanes] = slab.astype(BF16)
        shifted = jnp.where(lane == width - 1, after, pltpu.roll(slab, width - 1, 1))
        taps_ref[2 * channels : span, lanes] = shifted.astype(BF16)

    left = left_ref[...].astype(F32)
    right = right_ref[...].astype(F32)
    for end, flag, ref in ((0, place_ref[2], up_ref), (1, place_ref[3], down_ref)):
        corner = slice(rows + end, rows + end + 1)
        slab, before, after = [
            jnp.where(flag == 1, values, 0.0)
            for values in (ref[...].astype(F32), left[:, corner], right[:, corner])
        ]
        put(end * (rows + 1), slab, before, after)
    for row in range(rows):
        slab = flat_ref[:, row * width : (row + 1) * width].astype(F32)
        put(row + 1, slab, left[:, row : row + 1], right[:, row : row + 1])
    extra = taps_ref.shape[0] - span
    ones = lax.broadcasted_iota(jnp.int32, (extra, taps_ref.shape[1]), 0) == 0
    taps_ref[span:] = jnp.where(ones, 1.0, 0.0).astype(BF16)

    live = jnp.zeros((1, width), F32)
    live_lane = lane_index((1, width)) // TILE
    for tile in range(tile_cols):
        wet = (wet_ref[0, first_tile + tile] > 0).astype(F32)
        live = jnp.where(live_lane == tile, wet, live)
    step = 2 if rows % 2 == 0 else 1
    chunk = step * width
    live = jnp.concatenate([live] * step, 1)
    third = w_ref.shape[1] // 3
    blank = jnp.zeros((gates, 2 * width), BF16)
    delta_ref[:, : 2 * width] = blank
    delta_ref[:, (rows + 2) * width :] = blank
    bias = jnp.concatenate([b_ref[...]] * step, 1)
    group = 128 // TILE
    states = []
    for start in range(0, rows, step):
        lows = [(start + row_off) * width for row_off in range(3)]
        stacked = jnp.concatenate([taps_ref[:, low : low + chunk] for low in lows], 0)
        pre = bias + jnp.dot(w_ref[...], stacked, preferred_element_type=F32)
        gate_in = sigmoid(pre[:hid])
        gate_forget = sigmoid(pre[hid : 2 * hid])
        gate_out = sigmoid(pre[2 * hid : 3 * hid])
        candidate = jnp.tanh(pre[3 * hid :])
        lanes = slice(start * width, start * width + chunk)
        cell_in = cell_ref[:, lanes].astype(F32)
        cell_new = gate_forget * cell_in + gate_in * candidate
        squash = jnp.tanh(cell_new)
        hidden_new = live * gate_out * squash
        back_h = live * hcot_ref[:, lanes].astype(F32)
        back_c = live * ccot_ref[:, lanes].astype(F32) + back_h * gate_out * (1.0 - squash * squash)
        cell_back = back_c * gate_forget
        carried = back_c * gate_in
        terms = (
            carried * candidate * (1.0 - gate_in),
            cell_back * cell_in * (1.0 - gate_forget),
            back_h * squash * gate_out * (1.0 - gate_out),
            carried * (1.0 - candidate * candidate),
        )
        low = (start + 2) * width
        for index, term in enumerate(terms):
            delta_ref[index * hid : (index + 1) * hid, low : low + chunk] = term.astype(BF16)
        hidden_new_ref[:, lanes] = hidden_new.astype(BF16)
        cell_back_ref[:, lanes] = cell_back
        for part in range(step):
            piece = slice(part * width, (part + 1) * width)
            states.append(cell_new[:, piece])
        if len(states) == group:
            block_of = lane_index((hid, width)) // TILE
            half = (start + step) // group - 1
            stride = group // 2
            while stride:
                upper = (block_of & stride) != 0
                mixed = list(states)
                for low_index in range(group):
                    if low_index & stride == 0:
                        first, second = states[low_index], states[low_index + stride]
                        mixed[low_index] = jnp.where(
                            upper, pltpu.roll(second, stride * TILE, 1), first
                        )
                        mixed[low_index + stride] = jnp.where(
                            upper, second, pltpu.roll(first, width - stride * TILE, 1)
                        )
                states = mixed
                stride //= 2
            for tile in range(tile_cols):
                tiles_ref[tile, :, half * 128 : (half + 1) * 128] = states[tile].astype(BF16)
            states = []
    delta = delta_ref[:, 2 * width : (rows + 2) * width]
    for row_off in range(3):
        part = lax.dot_general(
            taps_ref[:, row_off * width : (row_off + rows) * width],
            delta,
            (((1,), (1,)), ((), ())),
            preferred_element_type=F32,
        )
        place = slice(row_off * third, (row_off + 1) * third)
        if len(weight_refs) == 1:
            weight_refs[0][place] = part
        else:
            low, high = part[:, : gates // 2], part[:, gates // 2 :]
            weight_refs[0][place] = jnp.where(place_ref[0] == 0, low, high)
            weight_refs[1][place] = jnp.where(place_ref[0] == 0, high, low)


def spread_kernel(place_ref, delta_ref, wt_ref, grad_ref, *rest):
    row_refs, (left_ref, right_ref, side_ref) = rest[:-3], rest[-3:]
    hid = grad_ref.shape[0]
    width = left_ref.shape[1]
    rows = grad_ref.shape[1] // width
    channels = wt_ref.shape[0] // 9
    total = [None] * 3
    for col_off in range(3):
        for row_off in range(3):
            first = (row_off * 3 + col_off + 1) * channels - hid
            low = (2 - row_off) * width
            term = jnp.dot(
                wt_ref[first : first + hid],
                delta_ref[:, low : low + (rows + 2) * width],
                preferred_element_type=F32,
            )
            total[col_off] = term if row_off == 0 else total[col_off] + term
        side_ref[col_off] = total[col_off]
    lane = lane_index((hid, width))
    left = jnp.zeros((hid, width), F32)
    right = jnp.zeros((hid, width), F32)
    ends = []
    for row in range(rows + 2):
        lanes = slice(row * width, (row + 1) * width)
        before = side_ref[0, :, lanes]
        after = side_ref[2, :, lanes]
        slab = (
            side_ref[1, :, lanes]
            + jnp.where(lane == width - 1, 0.0, pltpu.roll(before, width - 1, 1))
            + jnp.where(lane == 0, 0.0, pltpu.roll(after, 1, 1))
        )
        if row in (0, rows + 1):
            corners = jnp.where(lane == 0, before[:, :1], 0.0)
            corners = jnp.where(lane == width - 1, after[:, width - 1 :], corners)
            ends.append((slab, corners))
        else:
            grad_ref[:, (row - 1) * width : row * width] = slab
            left = jnp.where(lane == row - 1, before[:, :1], left)
            right = jnp.where(lane == row - 1, after[:, width - 1 :], right)
    left_ref[...] = left.astype(BF16)
    right_ref[...] = right.astype(BF16)
    if len(row_refs) == 2:
        for index in range(2):
            row_refs[index][...] = jnp.where(
                place_ref[0] == 0, ends[1][index], ends[0][index]
            ).astype(BF16)
    else:
        for end in range(2):
            for index in range(2):
                row_refs[2 * end + index][...] = ends[end][index].astype(BF16)


def finish_kernel(
    place_ref,
    work_ref,
    hidden_new_ref,
    cell_back_ref,
    arrived_ref,
    grad_ref,
    up_ref,
    down_ref,
    up_left_ref,
    up_right_ref,
    down_left_ref,
    down_right_ref,
    left_ref,
    right_ref,
    hidden_next_ref,
    cell_grad_ref,
    cell_next_ref,
    hidden_grad_ref,
    wide_ref,
):
    hid = grad_ref.shape[0]
    width = up_ref.shape[1]
    rows = grad_ref.shape[1] // width
    lane = lane_index((hid, width))
    left = left_ref[...].astype(F32)
    right = right_ref[...].astype(F32)
    ends = {}
    for row, flag, refs in (
        (0, place_ref[2], (up_ref, up_left_ref, up_right_ref)),
        (rows - 1, place_ref[3], (down_ref, down_left_ref, down_right_ref)),
    ):
        slab, before, after = [ref[...].astype(F32) for ref in refs]
        slab = slab + jnp.where(lane == 0, before[:, width - 1 :], 0.0)
        slab = slab + jnp.where(lane == width - 1, after[:, :1], 0.0)
        ends[row] = jnp.where(flag == 1, slab, 0.0)
    for row in range(rows):
        lanes = slice(row * width, (row + 1) * width)
        slab = grad_ref[:, lanes]
        slab = slab + jnp.where(lane == 0, left[:, row : row + 1], 0.0)
        slab = slab + jnp.where(lane == width - 1, right[:, row : row + 1], 0.0)
        if row in ends:
            slab = slab + ends[row]
        hidden_grad_ref[pl.ds(row, hid, stride=rows), :] = slab
        cell_grad_ref[pl.ds(row, hid, stride=rows), :] = cell_back_ref[:, lanes]
        wide_ref[pl.ds(row, hid, stride=rows), :] = hidden_new_ref[:, lanes].astype(F32)
    hidden_next_ref[...] = wide_ref[...].reshape(hid, rows, width).astype(BF16)
    pieces = arrived_ref.shape[2]
    for index in range(cell_next_ref.shape[0]):
        for piece in range(cell_next_ref.shape[2] // pieces):
            cell_next_ref[index, :, piece * pieces : (piece + 1) * pieces] = arrived_ref[
                work_ref[index], piece * hid : (piece + 1) * hid
            ].astype(F32)


def split_bias(block, row):
    index = lax.broadcasted_iota(jnp.int32, block.shape, 0)
    rest = pltpu.roll(block - block.astype(BF16).astype(F32), 1, 0)
    return jnp.where(index == row + 1, rest, block)


def slots_kernel(place_ref, wet_ref, owner_ref, tiles_ref, out_ref, slots_ref, semaphores):
    tile_cols, hid, cells = tiles_ref.shape
    slots, state_rows, lanes = slots_ref.shape
    slots_ref[...] = jnp.zeros(slots_ref.shape, BF16)
    for tile in range(tile_cols):
        index = place_ref[1] * tile_cols + tile

        @pl.when(wet_ref[0, index] > 0)
        def _():
            for piece in range(cells // lanes):
                slots_ref[owner_ref[0, index], piece * hid : (piece + 1) * hid] = tiles_ref[
                    tile, :, piece * lanes : (piece + 1) * lanes
                ]

    count = semaphores.shape[0]
    some = slots // count
    copies = [
        pltpu.make_async_copy(
            slots_ref.at[pl.ds(index * some, some)],
            out_ref.at[pl.ds(index * some, some), pl.ds(0, state_rows)],
            semaphores.at[index],
        )
        for index in range(count)
    ]
    for copy in copies:
        copy.start()
    for copy in copies:
        copy.wait()


def pack_kernel(span, count, *refs):
    slots_ref, out_ref, token_ref, share_ref, semaphore = refs[count:]
    token_ref[...] = jnp.zeros(token_ref.shape, F32)
    slots, share, _ = share_ref.shape
    third = refs[0].shape[0] // 3
    total = refs[0][...]
    for ref in refs[1:count]:
        total = total + ref[...]
    total = jnp.concatenate([split_bias(total[:third], span), total[third:]], 0)
    for slot in range(slots):
        share_ref[slot] = total[slot * share : (slot + 1) * share].astype(BF16)
    state_rows = out_ref.shape[1] - share
    copy = pltpu.make_async_copy(share_ref, out_ref.at[:, pl.ds(state_rows, share)], semaphore)
    copy.start()
    copy.wait()


def sum_kernel(scaling, span, state_rows, place_ref, parts_ref, out_ref, token_ref):
    token_ref[...] = jnp.zeros(token_ref.shape, F32)
    total = parts_ref[0, state_rows:].astype(F32)
    for index in range(1, parts_ref.shape[0]):
        total = total + parts_ref[index, state_rows:].astype(F32)
    total = total * scaling
    share = total.shape[0]
    row = span % share
    index = lax.broadcasted_iota(jnp.int32, total.shape, 0)
    whole = jnp.where(index == row, total + pltpu.roll(total, share - 1, 0), total)
    total = jnp.where(place_ref[1] == span // share, split_bias(whole, row), total)
    for index in range(out_ref.shape[0]):
        out_ref[index] = total.astype(BF16)


def weights_kernel(span, place_ref, *refs):
    *parts, weight_ref, bias_ref = refs
    third = parts[0].shape[0] // 3
    half = parts[0].shape[1]
    for side in range(len(parts)):
        if len(parts) == 1:
            pick = parts[0][...]
        else:
            pick = jnp.where(place_ref[0] == side, parts[0][...], parts[1][...])
        pick = pick.astype(F32)
        lanes = slice(side * half, (side + 1) * half)
        for index in range(3):
            weight_ref[index * span : (index + 1) * span, lanes] = pick[
                index * third : index * third + span
            ]
        bias_ref[:, lanes] = pick[span : span + 1] + pick[span + 1 : span + 2]


def moved(values, lat_step, lon_step, lat_devices, lon_devices):
    pairs = []
    for lat in range(lat_devices):
        for lon in range(lon_devices):
            to_lat = lat + lat_step
            if lat_step and lat_devices == 2:
                to_lat = 1 - lat
            if 0 <= to_lat < lat_devices:
                to = to_lat * lon_devices + (lon + lon_step) % lon_devices
                pairs.append((lat * lon_devices + lon, to))
    return lax.ppermute(values, ("lat", "lon"), pairs)


def exchange(ends, corners, left, right, lat_devices, lon_devices):
    def go(values, lat_step, lon_step):
        return moved(values, lat_step, lon_step, lat_devices, lon_devices)

    from_left, from_right = go(right, 0, 1), go(left, 0, -1)
    if lat_devices == 2:
        row = go(ends[0], 1, 0)
        row_left, row_right = go(corners[0], 1, 1), go(corners[0], 1, -1)
        return (row, row, row_left, row_right, row_left, row_right, from_left, from_right)
    return (
        go(ends[1], 1, 0),
        go(ends[0], -1, 0),
        go(corners[1], 1, 1),
        go(corners[1], 1, -1),
        go(corners[0], -1, 1),
        go(corners[0], -1, -1),
        from_left,
        from_right,
    )


def body(forcing, hidden, cell, grad_hidden, grad_cell, wet_mask, tile_owner, w_gates, b_gates):
    lat_index = lax.axis_index("lat")
    lon_index = lax.axis_index("lon")
    lat_devices = lax.axis_size("lat")
    lon_devices = lax.axis_size("lon")
    inp, rows, width = forcing.shape
    hid = hidden.shape[0]
    channels = inp + hid
    gates = w_gates.shape[0]
    span = 3 * channels
    third = (span + 128) // 128 * 128
    cells = rows * width
    tile_cols = width // TILE
    capacity = tile_cols // 2
    place = jnp.stack(
        [
            lat_index,
            lon_index,
            (lat_index > 0).astype(jnp.int32),
            (lat_index < lat_devices - 1).astype(jnp.int32),
        ]
    ).astype(jnp.int32)

    def shaped(*shape, dtype=BF16):
        return jax.ShapeDtypeStruct(shape, dtype)

    end_count = 1 if lat_devices == 2 else 2
    wide, *ends = call(
        edges_kernel,
        (shaped(channels * rows, width, dtype=F32),) + (shaped(channels, width),) * end_count,
        (place, forcing, hidden),
        scalars=1,
        moved=4 * channels * cells,
        fetched=2,
    )
    flat, left, right = call(
        columns_kernel,
        (shaped(channels, cells),) + (shaped(channels, width),) * 2,
        (wide,),
        moved=6 * channels * cells,
    )
    if lat_devices == 2:
        up = down = moved(ends[0], 1, 0, lat_devices, lon_devices)
    else:
        up = moved(ends[1], 1, 0, lat_devices, lon_devices)
        down = moved(ends[0], -1, 0, lat_devices, lon_devices)
    left, right = call(
        lambda *refs: corners_kernel(rows, *refs),
        (shaped(channels, width),) * 2,
        (up, down, left, right),
        moved=8 * channels * width,
    )
    halo = (
        up,
        down,
        moved(right, 0, 1, lat_devices, lon_devices),
        moved(left, 0, -1, lat_devices, lon_devices),
    )
    w_turned = w_gates.T
    cell_flat, hcot_flat, ccot_flat, w_rows, bias = call(
        flatten_kernel,
        (shaped(hid, cells),) * 3
        + (shaped(gates, 3 * third), shaped(gates, width, dtype=F32)),
        (b_gates.reshape(1, gates), w_turned, cell, grad_hidden, grad_cell),
        scratch=[pltpu.VMEM((hid * rows, width), F32)],
        moved=12 * hid * cells,
        fetched=5,
    )
    halves = 2 if lat_devices == 2 else 1
    lanes = gates // halves
    hidden_new, cell_back, tiles, *weight_parts, delta = call(
        step_kernel,
        (
            shaped(hid, cells),
            shaped(hid, cells, dtype=F32),
            shaped(tile_cols, hid, TILE * TILE),
        )
        + (shaped(3 * third, lanes, dtype=F32),) * halves
        + (shaped(gates, (rows + 4) * width),),
        (place, wet_mask, tile_owner, flat, *halo)
        + (cell_flat, hcot_flat, ccot_flat, w_rows, bias),
        scalars=3,
        scratch=[pltpu.VMEM((third, (rows + 2) * width), BF16)],
        flops=4 * gates * 3 * span * cells,
        moved=16 * hid * cells,
    )
    swap = [(0, 1), (1, 0)]
    if halves == 2:
        weight_parts = (weight_parts[0], lax.ppermute(weight_parts[1], "lat", swap))
    else:
        weight_parts = (lax.psum(weight_parts[0], "lat"),)
    state_rows = hid * TILE * TILE // lanes
    share = 3 * third // lon_devices
    anywhere = pl.BlockSpec(memory_space=pl.ANY)
    copies = 4 if lon_devices % 4 == 0 else 1
    slots = pl.pallas_call(
        slots_kernel,
        out_shape=shaped(lon_devices, state_rows + share, lanes),
        in_specs=[SMEM] * 3 + [VMEM],
        out_specs=anywhere,
        scratch_shapes=[
            pltpu.VMEM((lon_devices, state_rows, lanes), BF16),
            pltpu.SemaphoreType.DMA((copies,)),
        ],
        compiler_params=pltpu.CompilerParams(vmem_limit_bytes=LIMIT),
        cost_estimate=pl.CostEstimate(
            flops=0, bytes_accessed=4 * lon_devices * hid * TILE * TILE, transcendentals=0
        ),
    )(place, wet_mask, tile_owner, tiles)
    count = len(weight_parts)
    outgoing, packed = pl.pallas_call(
        lambda *refs: pack_kernel(span, count, *refs),
        out_shape=(shaped(*slots.shape), shaped(8, 128, dtype=F32)),
        in_specs=[VMEM] * count + [anywhere],
        out_specs=(anywhere, VMEM),
        scratch_shapes=[
            pltpu.VMEM((lon_devices, share, lanes), BF16),
            pltpu.SemaphoreType.DMA(()),
        ],
        input_output_aliases={count: 0},
        compiler_params=pltpu.CompilerParams(vmem_limit_bytes=LIMIT),
        cost_estimate=pl.CostEstimate(
            flops=0, bytes_accessed=8 * gates * 3 * third, transcendentals=0
        ),
    )(*weight_parts, slots)
    incoming = lax.all_to_all(outgoing, "lon", 0, 0, tiled=True)
    grad_parts = call(
        spread_kernel,
        (shaped(hid, cells, dtype=F32),) + (shaped(hid, width),) * (2 * end_count + 2),
        (place, delta, w_turned),
        scalars=1,
        scratch=[pltpu.VMEM((3, hid, (rows + 2) * width), F32)],
        flops=2 * gates * 9 * hid * cells,
        moved=8 * gates * cells,
        after=(packed,),
    )
    grad_flat, grad_ends, grad_sides = grad_parts[0], grad_parts[1:-2], grad_parts[-2:]
    grad_halo = exchange(
        grad_ends[0::2], grad_ends[1::2], *grad_sides, lat_devices, lon_devices
    )
    scaling = 1.0 / math.sqrt(float(lat_devices * lon_devices * capacity * TILE * TILE))
    shares, shared = call(
        lambda *refs: sum_kernel(scaling, span, state_rows, *refs),
        (shaped(lon_devices, share, lanes), shaped(8, 128, dtype=F32)),
        (place, incoming),
        scalars=1,
        moved=2 * gates * 3 * third,
        after=grad_halo,
    )
    owned = (wet_mask > 0) & (tile_owner == lon_index)
    arrived = jnp.any(owned.reshape(lon_devices, tile_cols), 1)
    order = jnp.arange(lon_devices, dtype=jnp.int32)
    rank = jnp.sum((arrived[:, None] & (order[:, None] < order[None, :])).astype(jnp.int32), 0)
    placed = arrived[None, :] & (rank[None, :] == jnp.arange(capacity, dtype=jnp.int32)[:, None])
    work = jnp.sum(jnp.where(placed, order[None, :], 0), 1)
    finished = call(
        finish_kernel,
        (
            shaped(hid, rows, width),
            shaped(hid * rows, width, dtype=F32),
            shaped(capacity, hid, TILE * TILE, dtype=F32),
            shaped(hid * rows, width, dtype=F32),
        ),
        (place, work, hidden_new, cell_back, incoming, grad_flat, *grad_halo),
        scalars=2,
        scratch=[pltpu.VMEM((hid * rows, width), F32)],
        moved=32 * hid * cells,
        after=(shared,),
    )
    gathered = lax.all_to_all(shares, "lon", 0, 0, tiled=True).reshape(3 * third, lanes)
    gathered, finished = lax.optimization_barrier((gathered, finished))
    hidden_next, cell_grad, cell_next, hidden_grad = finished
    gathered = (gathered,)
    if halves == 2:
        gathered += (lax.ppermute(gathered[0], "lat", swap),)
    weight_grad, bias_grad = call(
        lambda *refs: weights_kernel(span, *refs),
        (shaped(3 * span, gates, dtype=F32), shaped(1, gates, dtype=F32)),
        (place, *gathered),
        scalars=1,
        moved=6 * gates * 3 * third,
    )
    return (
        hidden_next,
        cell_next,
        hidden_grad.reshape(hid, rows, width),
        cell_grad.reshape(hid, rows, width),
        weight_grad.T,
        bias_grad.reshape(gates),
    )


def solution(mesh):
    return jax.shard_map(
        body,
        mesh=mesh,
        in_specs=(
            P(None, "lat", "lon"),
            P(None, "lat", "lon"),
            P(None, "lat", "lon"),
            P(None, "lat", "lon"),
            P(None, "lat", "lon"),
            P("lat", None),
            P("lat", None),
            P(),
            P(),
        ),
        out_specs=(
            P(None, "lat", "lon"),
            P(("lat", "lon"), None, None),
            P(None, "lat", "lon"),
            P(None, "lat", "lon"),
            P(),
            P(),
        ),
        check_vma=False,
    )
```

```python
import math

import jax
import jax.numpy as jnp
from jax import lax
from jax.experimental import pallas as pl
from jax.experimental.pallas import tpu as pltpu
from jax.sharding import PartitionSpec as P

TILE = 16
F32 = jnp.float32
BF16 = jnp.bfloat16
LIMIT = 24 * 1024 * 1024
SMEM = pl.BlockSpec(memory_space=pltpu.SMEM)
VMEM = pl.BlockSpec(memory_space=pltpu.VMEM)


def call(kernel, outs, operands, scalars=0, scratch=(), flops=0, moved=0, after=(), fetched=0):
    count = len(operands)
    kept = count - fetched
    total = count + len(after)

    def run(*refs):
        if not fetched:
            kernel(*refs[:count], *refs[total:])
            return
        *rest, semaphores = refs[total:]
        buffers = rest[len(rest) - fetched :]
        copies = [
            pltpu.make_async_copy(source, target, semaphores.at[index])
            for index, (source, target) in enumerate(zip(refs[kept:count], buffers))
        ]
        for copy in copies:
            copy.start()
        waits = [copy.wait for copy in copies]
        kernel(waits, *refs[:kept], *buffers, *rest[: len(rest) - fetched])

    scratch = list(scratch)
    operands = list(operands)
    for index in range(kept, count):
        operands[index] = pltpu.with_memory_space_constraint(operands[index], pltpu.HBM)
    if fetched:
        scratch += [pltpu.VMEM(leaf.shape, leaf.dtype) for leaf in operands[kept:]]
        scratch.append(pltpu.SemaphoreType.DMA((fetched,)))

    return pl.pallas_call(
        run,
        out_shape=outs,
        in_specs=[SMEM] * scalars
        + [VMEM] * (kept - scalars)
        + [pl.BlockSpec(memory_space=pltpu.HBM)] * fetched
        + [VMEM] * len(after),
        out_specs=jax.tree.map(lambda _: VMEM, outs),
        scratch_shapes=scratch,
        compiler_params=pltpu.CompilerParams(vmem_limit_bytes=LIMIT),
        cost_estimate=pl.CostEstimate(flops=flops, bytes_accessed=moved, transcendentals=0),
    )(*operands, *after)


def lane_index(shape):
    return lax.broadcasted_iota(jnp.int32, shape, 1)


def sigmoid(values):
    return 0.5 * jnp.tanh(0.5 * values) + 0.5


def edges_kernel(waits, place_ref, forcing_ref, hidden_ref, wide_ref, *row_refs):
    inp, rows, width = forcing_ref.shape
    channels = inp + hidden_ref.shape[0]
    for wait in waits:
        wait()
    wide_ref[: inp * rows] = forcing_ref[...].astype(F32).reshape(inp * rows, width)
    wide_ref[inp * rows :] = hidden_ref[...].astype(F32).reshape((channels - inp) * rows, width)
    ends = [wide_ref[pl.ds(row, channels, stride=rows), :] for row in (0, rows - 1)]
    if len(row_refs) == 1:
        row_refs[0][...] = jnp.where(place_ref[0] == 0, ends[1], ends[0]).astype(BF16)
    else:
        for ref, end in zip(row_refs, ends):
            ref[...] = end.astype(BF16)


def columns_kernel(wide_ref, flat_ref, left_ref, right_ref):
    channels, width = left_ref.shape
    rows = wide_ref.shape[0] // channels
    lane = lane_index((channels, width))
    left = jnp.zeros((channels, width), F32)
    right = jnp.zeros((channels, width), F32)
    for row in range(rows):
        slab = wide_ref[pl.ds(row, channels, stride=rows), :]
        flat_ref[:, row * width : (row + 1) * width] = slab.astype(BF16)
        left = jnp.where(lane == row, slab[:, :1], left)
        right = jnp.where(lane == row, slab[:, width - 1 :], right)
    left_ref[...] = left.astype(BF16)
    right_ref[...] = right.astype(BF16)


def flatten_kernel(
    waits,
    b_ref,
    wt_ref,
    cell_ref,
    hcot_ref,
    ccot_ref,
    cell_out,
    hcot_out,
    ccot_out,
    w_ref,
    bias_ref,
    wide_ref,
):
    hid, rows, width = cell_ref.shape
    gates = wt_ref.shape[1]
    span = wt_ref.shape[0] // 3
    third = w_ref.shape[1] // 3
    waits[0]()
    bias_ref[...] = jnp.broadcast_to(b_ref[...], (bias_ref.shape[1], gates)).T
    waits[1]()
    blank = jnp.zeros((third - span, gates), F32)
    for index in range(3):
        block = wt_ref[index * span : (index + 1) * span].astype(F32)
        w_ref[:, index * third : (index + 1) * third] = (
            jnp.concatenate([block, blank], 0).T.astype(BF16)
        )
    for wait, source, target in zip(
        waits[2:], (cell_ref, hcot_ref, ccot_ref), (cell_out, hcot_out, ccot_out)
    ):
        wait()
        wide_ref[...] = source[...].astype(F32).reshape(hid * rows, width)
        for row in range(rows):
            target[:, row * width : (row + 1) * width] = wide_ref[
                pl.ds(row, hid, stride=rows), :
            ].astype(BF16)


def corners_kernel(rows, up_ref, down_ref, left_ref, right_ref, left_out, right_out):
    lane = lane_index(left_ref.shape)
    width = up_ref.shape[1]
    up = up_ref[...].astype(F32)
    down = down_ref[...].astype(F32)
    for column, source, target in ((0, left_ref, left_out), (width - 1, right_ref, right_out)):
        values = source[...].astype(F32)
        values = jnp.where(lane == rows, up[:, column : column + 1], values)
        values = jnp.where(lane == rows + 1, down[:, column : column + 1], values)
        target[...] = values.astype(BF16)


def step_kernel(
    place_ref,
    wet_ref,
    owner_ref,
    flat_ref,
    up_ref,
    down_ref,
    left_ref,
    right_ref,
    cell_ref,
    hcot_ref,
    ccot_ref,
    w_ref,
    b_ref,
    hidden_new_ref,
    cell_back_ref,
    tiles_ref,
    *rest,
):
    weight_refs, (delta_ref, taps_ref) = rest[:-2], rest[-2:]
    channels = flat_ref.shape[0]
    hid = cell_ref.shape[0]
    gates = w_ref.shape[0]
    width = up_ref.shape[1]
    rows = flat_ref.shape[1] // width
    tile_cols = width // TILE
    span = 3 * channels
    first_tile = place_ref[1] * tile_cols
    lane = lane_index((channels, width))

    def put(row, slab, before, after):
        lanes = slice(row * width, (row + 1) * width)
        shifted = jnp.where(lane == 0, before, pltpu.roll(slab, 1, 1))
        taps_ref[0:channels, lanes] = shifted.astype(BF16)
        taps_ref[channels : 2 * channels, lanes] = slab.astype(BF16)
        shifted = jnp.where(lane == width - 1, after, pltpu.roll(slab, width - 1, 1))
        taps_ref[2 * channels : span, lanes] = shifted.astype(BF16)

    left = left_ref[...].astype(F32)
    right = right_ref[...].astype(F32)
    for end, flag, ref in ((0, place_ref[2], up_ref), (1, place_ref[3], down_ref)):
        corner = slice(rows + end, rows + end + 1)
        slab, before, after = [
            jnp.where(flag == 1, values, 0.0)
            for values in (ref[...].astype(F32), left[:, corner], right[:, corner])
        ]
        put(end * (rows + 1), slab, before, after)
    for row in range(rows):
        slab = flat_ref[:, row * width : (row + 1) * width].astype(F32)
        put(row + 1, slab, left[:, row : row + 1], right[:, row : row + 1])
    extra = taps_ref.shape[0] - span
    ones = lax.broadcasted_iota(jnp.int32, (extra, taps_ref.shape[1]), 0) == 0
    taps_ref[span:] = jnp.where(ones, 1.0, 0.0).astype(BF16)

    live = jnp.zeros((1, width), F32)
    live_lane = lane_index((1, width)) // TILE
    for tile in range(tile_cols):
        wet = (wet_ref[0, first_tile + tile] > 0).astype(F32)
        live = jnp.where(live_lane == tile, wet, live)
    step = 2 if rows % 2 == 0 else 1
    chunk = step * width
    live = jnp.concatenate([live] * step, 1)
    third = w_ref.shape[1] // 3
    blank = jnp.zeros((gates, 2 * width), BF16)
    delta_ref[:, : 2 * width] = blank
    delta_ref[:, (rows + 2) * width :] = blank
    bias = jnp.concatenate([b_ref[...]] * step, 1)
    group = 128 // TILE
    states = []
    for start in range(0, rows, step):
        lows = [(start + row_off) * width for row_off in range(3)]
        stacked = jnp.concatenate([taps_ref[:, low : low + chunk] for low in lows], 0)
        pre = bias + jnp.dot(w_ref[...], stacked, preferred_element_type=F32)
        gate_in = sigmoid(pre[:hid])
        gate_forget = sigmoid(pre[hid : 2 * hid])
        gate_out = sigmoid(pre[2 * hid : 3 * hid])
        candidate = jnp.tanh(pre[3 * hid :])
        lanes = slice(start * width, start * width + chunk)
        cell_in = cell_ref[:, lanes].astype(F32)
        cell_new = gate_forget * cell_in + gate_in * candidate
        squash = jnp.tanh(cell_new)
        hidden_new = live * gate_out * squash
        back_h = live * hcot_ref[:, lanes].astype(F32)
        back_c = live * ccot_ref[:, lanes].astype(F32) + back_h * gate_out * (1.0 - squash * squash)
        cell_back = back_c * gate_forget
        carried = back_c * gate_in
        terms = (
            carried * candidate * (1.0 - gate_in),
            cell_back * cell_in * (1.0 - gate_forget),
            back_h * squash * gate_out * (1.0 - gate_out),
            carried * (1.0 - candidate * candidate),
        )
        low = (start + 2) * width
        for index, term in enumerate(terms):
            delta_ref[index * hid : (index + 1) * hid, low : low + chunk] = term.astype(BF16)
        hidden_new_ref[:, lanes] = hidden_new.astype(BF16)
        cell_back_ref[:, lanes] = cell_back
        for part in range(step):
            piece = slice(part * width, (part + 1) * width)
            states.append(cell_new[:, piece])
        if len(states) == group:
            block_of = lane_index((hid, width)) // TILE
            half = (start + step) // group - 1
            stride = group // 2
            while stride:
                upper = (block_of & stride) != 0
                mixed = list(states)
                for low_index in range(group):
                    if low_index & stride == 0:
                        first, second = states[low_index], states[low_index + stride]
                        mixed[low_index] = jnp.where(
                            upper, pltpu.roll(second, stride * TILE, 1), first
                        )
                        mixed[low_index + stride] = jnp.where(
                            upper, second, pltpu.roll(first, width - stride * TILE, 1)
                        )
                states = mixed
                stride //= 2
            for tile in range(tile_cols):
                tiles_ref[tile, :, half * 128 : (half + 1) * 128] = states[tile].astype(BF16)
            states = []
    delta = delta_ref[:, 2 * width : (rows + 2) * width]
    for row_off in range(3):
        part = lax.dot_general(
            taps_ref[:, row_off * width : (row_off + rows) * width],
            delta,
            (((1,), (1,)), ((), ())),
            preferred_element_type=F32,
        )
        place = slice(row_off * third, (row_off + 1) * third)
        if len(weight_refs) == 1:
            weight_refs[0][place] = part
        else:
            low, high = part[:, : gates // 2], part[:, gates // 2 :]
            weight_refs[0][place] = jnp.where(place_ref[0] == 0, low, high)
            weight_refs[1][place] = jnp.where(place_ref[0] == 0, high, low)


def spread_kernel(place_ref, delta_ref, wt_ref, grad_ref, *rest):
    row_refs, (left_ref, right_ref, side_ref) = rest[:-3], rest[-3:]
    hid = grad_ref.shape[0]
    width = left_ref.shape[1]
    rows = grad_ref.shape[1] // width
    channels = wt_ref.shape[0] // 9
    total = [None] * 3
    for col_off in range(3):
        for row_off in range(3):
            first = (row_off * 3 + col_off + 1) * channels - hid
            low = (2 - row_off) * width
            term = jnp.dot(
                wt_ref[first : first + hid],
                delta_ref[:, low : low + (rows + 2) * width],
                preferred_element_type=F32,
            )
            total[col_off] = term if row_off == 0 else total[col_off] + term
        side_ref[col_off] = total[col_off]
    lane = lane_index((hid, width))
    left = jnp.zeros((hid, width), F32)
    right = jnp.zeros((hid, width), F32)
    ends = []
    for row in range(rows + 2):
        lanes = slice(row * width, (row + 1) * width)
        before = side_ref[0, :, lanes]
        after = side_ref[2, :, lanes]
        slab = (
            side_ref[1, :, lanes]
            + jnp.where(lane == width - 1, 0.0, pltpu.roll(before, width - 1, 1))
            + jnp.where(lane == 0, 0.0, pltpu.roll(after, 1, 1))
        )
        if row in (0, rows + 1):
            corners = jnp.where(lane == 0, before[:, :1], 0.0)
            corners = jnp.where(lane == width - 1, after[:, width - 1 :], corners)
            ends.append((slab, corners))
        else:
            grad_ref[:, (row - 1) * width : row * width] = slab
            left = jnp.where(lane == row - 1, before[:, :1], left)
            right = jnp.where(lane == row - 1, after[:, width - 1 :], right)
    left_ref[...] = left.astype(BF16)
    right_ref[...] = right.astype(BF16)
    if len(row_refs) == 2:
        for index in range(2):
            row_refs[index][...] = jnp.where(
                place_ref[0] == 0, ends[1][index], ends[0][index]
            ).astype(BF16)
    else:
        for end in range(2):
            for index in range(2):
                row_refs[2 * end + index][...] = ends[end][index].astype(BF16)


def finish_kernel(
    place_ref,
    work_ref,
    hidden_new_ref,
    cell_back_ref,
    arrived_ref,
    grad_ref,
    up_ref,
    down_ref,
    up_left_ref,
    up_right_ref,
    down_left_ref,
    down_right_ref,
    left_ref,
    right_ref,
    hidden_next_ref,
    cell_grad_ref,
    cell_next_ref,
    hidden_grad_ref,
    wide_ref,
):
    hid = grad_ref.shape[0]
    width = up_ref.shape[1]
    rows = grad_ref.shape[1] // width
    lane = lane_index((hid, width))
    left = left_ref[...].astype(F32)
    right = right_ref[...].astype(F32)
    ends = {}
    for row, flag, refs in (
        (0, place_ref[2], (up_ref, up_left_ref, up_right_ref)),
        (rows - 1, place_ref[3], (down_ref, down_left_ref, down_right_ref)),
    ):
        slab, before, after = [ref[...].astype(F32) for ref in refs]
        slab = slab + jnp.where(lane == 0, before[:, width - 1 :], 0.0)
        slab = slab + jnp.where(lane == width - 1, after[:, :1], 0.0)
        ends[row] = jnp.where(flag == 1, slab, 0.0)
    for row in range(rows):
        lanes = slice(row * width, (row + 1) * width)
        slab = grad_ref[:, lanes]
        slab = slab + jnp.where(lane == 0, left[:, row : row + 1], 0.0)
        slab = slab + jnp.where(lane == width - 1, right[:, row : row + 1], 0.0)
        if row in ends:
            slab = slab + ends[row]
        hidden_grad_ref[pl.ds(row, hid, stride=rows), :] = slab
        cell_grad_ref[pl.ds(row, hid, stride=rows), :] = cell_back_ref[:, lanes]
        wide_ref[pl.ds(row, hid, stride=rows), :] = hidden_new_ref[:, lanes].astype(F32)
    hidden_next_ref[...] = wide_ref[...].reshape(hid, rows, width).astype(BF16)
    pieces = arrived_ref.shape[2]
    for index in range(cell_next_ref.shape[0]):
        for piece in range(cell_next_ref.shape[2] // pieces):
            cell_next_ref[index, :, piece * pieces : (piece + 1) * pieces] = arrived_ref[
                work_ref[index], piece * hid : (piece + 1) * hid
            ].astype(F32)


def split_bias(block, row):
    index = lax.broadcasted_iota(jnp.int32, block.shape, 0)
    rest = pltpu.roll(block - block.astype(BF16).astype(F32), 1, 0)
    return jnp.where(index == row + 1, rest, block)


def slots_kernel(place_ref, wet_ref, owner_ref, tiles_ref, out_ref):
    tile_cols, hid, cells = tiles_ref.shape
    slots, _, lanes = out_ref.shape
    out_ref[...] = jnp.zeros(out_ref.shape, BF16)
    for tile in range(tile_cols):
        index = place_ref[1] * tile_cols + tile

        @pl.when(wet_ref[0, index] > 0)
        def _():
            for piece in range(cells // lanes):
                out_ref[owner_ref[0, index], piece * hid : (piece + 1) * hid] = tiles_ref[
                    tile, :, piece * lanes : (piece + 1) * lanes
                ]


def pack_kernel(span, count, *refs):
    slots_ref, out_ref, token_ref, share_ref, semaphore = refs[count:]
    token_ref[...] = jnp.zeros(token_ref.shape, F32)
    slots, share, _ = share_ref.shape
    third = refs[0].shape[0] // 3
    total = refs[0][...]
    for ref in refs[1:count]:
        total = total + ref[...]
    total = jnp.concatenate([split_bias(total[:third], span), total[third:]], 0)
    for slot in range(slots):
        share_ref[slot] = total[slot * share : (slot + 1) * share].astype(BF16)
    state_rows = out_ref.shape[1] - share
    copy = pltpu.make_async_copy(share_ref, out_ref.at[:, pl.ds(state_rows, share)], semaphore)
    copy.start()
    copy.wait()


def sum_kernel(scaling, span, state_rows, place_ref, parts_ref, out_ref, token_ref):
    token_ref[...] = jnp.zeros(token_ref.shape, F32)
    total = parts_ref[0, state_rows:].astype(F32)
    for index in range(1, parts_ref.shape[0]):
        total = total + parts_ref[index, state_rows:].astype(F32)
    total = total * scaling
    share = total.shape[0]
    row = span % share
    index = lax.broadcasted_iota(jnp.int32, total.shape, 0)
    whole = jnp.where(index == row, total + pltpu.roll(total, share - 1, 0), total)
    total = jnp.where(place_ref[1] == span // share, split_bias(whole, row), total)
    for index in range(out_ref.shape[0]):
        out_ref[index] = total.astype(BF16)


def weights_kernel(span, place_ref, *refs):
    *parts, weight_ref, bias_ref = refs
    third = parts[0].shape[0] // 3
    half = parts[0].shape[1]
    for side in range(len(parts)):
        if len(parts) == 1:
            pick = parts[0][...]
        else:
            pick = jnp.where(place_ref[0] == side, parts[0][...], parts[1][...])
        pick = pick.astype(F32)
        lanes = slice(side * half, (side + 1) * half)
        for index in range(3):
            weight_ref[index * span : (index + 1) * span, lanes] = pick[
                index * third : index * third + span
            ]
        bias_ref[:, lanes] = pick[span : span + 1] + pick[span + 1 : span + 2]


def moved(values, lat_step, lon_step, lat_devices, lon_devices):
    pairs = []
    for lat in range(lat_devices):
        for lon in range(lon_devices):
            to_lat = lat + lat_step
            if lat_step and lat_devices == 2:
                to_lat = 1 - lat
            if 0 <= to_lat < lat_devices:
                to = to_lat * lon_devices + (lon + lon_step) % lon_devices
                pairs.append((lat * lon_devices + lon, to))
    return lax.ppermute(values, ("lat", "lon"), pairs)


def exchange(ends, corners, left, right, lat_devices, lon_devices):
    def go(values, lat_step, lon_step):
        return moved(values, lat_step, lon_step, lat_devices, lon_devices)

    from_left, from_right = go(right, 0, 1), go(left, 0, -1)
    if lat_devices == 2:
        row = go(ends[0], 1, 0)
        row_left, row_right = go(corners[0], 1, 1), go(corners[0], 1, -1)
        return (row, row, row_left, row_right, row_left, row_right, from_left, from_right)
    return (
        go(ends[1], 1, 0),
        go(ends[0], -1, 0),
        go(corners[1], 1, 1),
        go(corners[1], 1, -1),
        go(corners[0], -1, 1),
        go(corners[0], -1, -1),
        from_left,
        from_right,
    )


def body(forcing, hidden, cell, grad_hidden, grad_cell, wet_mask, tile_owner, w_gates, b_gates):
    lat_index = lax.axis_index("lat")
    lon_index = lax.axis_index("lon")
    lat_devices = lax.axis_size("lat")
    lon_devices = lax.axis_size("lon")
    inp, rows, width = forcing.shape
    hid = hidden.shape[0]
    channels = inp + hid
    gates = w_gates.shape[0]
    span = 3 * channels
    third = (span + 128) // 128 * 128
    cells = rows * width
    tile_cols = width // TILE
    capacity = tile_cols // 2
    place = jnp.stack(
        [
            lat_index,
            lon_index,
            (lat_index > 0).astype(jnp.int32),
            (lat_index < lat_devices - 1).astype(jnp.int32),
        ]
    ).astype(jnp.int32)

    def shaped(*shape, dtype=BF16):
        return jax.ShapeDtypeStruct(shape, dtype)

    end_count = 1 if lat_devices == 2 else 2
    wide, *ends = call(
        edges_kernel,
        (shaped(channels * rows, width, dtype=F32),) + (shaped(channels, width),) * end_count,
        (place, forcing, hidden),
        scalars=1,
        moved=4 * channels * cells,
        fetched=2,
    )
    flat, left, right = call(
        columns_kernel,
        (shaped(channels, cells),) + (shaped(channels, width),) * 2,
        (wide,),
        moved=6 * channels * cells,
    )
    if lat_devices == 2:
        up = down = moved(ends[0], 1, 0, lat_devices, lon_devices)
    else:
        up = moved(ends[1], 1, 0, lat_devices, lon_devices)
        down = moved(ends[0], -1, 0, lat_devices, lon_devices)
    left, right = call(
        lambda *refs: corners_kernel(rows, *refs),
        (shaped(channels, width),) * 2,
        (up, down, left, right),
        moved=8 * channels * width,
    )
    halo = (
        up,
        down,
        moved(right, 0, 1, lat_devices, lon_devices),
        moved(left, 0, -1, lat_devices, lon_devices),
    )
    w_turned = w_gates.T
    cell_flat, hcot_flat, ccot_flat, w_rows, bias = call(
        flatten_kernel,
        (shaped(hid, cells),) * 3
        + (shaped(gates, 3 * third), shaped(gates, width, dtype=F32)),
        (b_gates.reshape(1, gates), w_turned, cell, grad_hidden, grad_cell),
        scratch=[pltpu.VMEM((hid * rows, width), F32)],
        moved=12 * hid * cells,
        fetched=5,
    )
    halves = 2 if lat_devices == 2 else 1
    lanes = gates // halves
    hidden_new, cell_back, tiles, *weight_parts, delta = call(
        step_kernel,
        (
            shaped(hid, cells),
            shaped(hid, cells, dtype=F32),
            shaped(tile_cols, hid, TILE * TILE),
        )
        + (shaped(3 * third, lanes, dtype=F32),) * halves
        + (shaped(gates, (rows + 4) * width),),
        (place, wet_mask, tile_owner, flat, *halo)
        + (cell_flat, hcot_flat, ccot_flat, w_rows, bias),
        scalars=3,
        scratch=[pltpu.VMEM((third, (rows + 2) * width), BF16)],
        flops=4 * gates * 3 * span * cells,
        moved=16 * hid * cells,
    )
    swap = [(0, 1), (1, 0)]
    if halves == 2:
        weight_parts = (weight_parts[0], lax.ppermute(weight_parts[1], "lat", swap))
    else:
        weight_parts = (lax.psum(weight_parts[0], "lat"),)
    state_rows = hid * TILE * TILE // lanes
    share = 3 * third // lon_devices
    slots = call(
        slots_kernel,
        shaped(lon_devices, state_rows + share, lanes),
        (place, wet_mask, tile_owner, tiles),
        scalars=3,
        moved=4 * lon_devices * hid * TILE * TILE,
    )
    anywhere = pl.BlockSpec(memory_space=pl.ANY)
    count = len(weight_parts)
    outgoing, packed = pl.pallas_call(
        lambda *refs: pack_kernel(span, count, *refs),
        out_shape=(shaped(*slots.shape), shaped(8, 128, dtype=F32)),
        in_specs=[VMEM] * count + [anywhere],
        out_specs=(anywhere, VMEM),
        scratch_shapes=[
            pltpu.VMEM((lon_devices, share, lanes), BF16),
            pltpu.SemaphoreType.DMA(()),
        ],
        input_output_aliases={count: 0},
        compiler_params=pltpu.CompilerParams(vmem_limit_bytes=LIMIT),
        cost_estimate=pl.CostEstimate(
            flops=0, bytes_accessed=8 * gates * 3 * third, transcendentals=0
        ),
    )(*weight_parts, slots)
    incoming = lax.all_to_all(outgoing, "lon", 0, 0, tiled=True)
    grad_parts = call(
        spread_kernel,
        (shaped(hid, cells, dtype=F32),) + (shaped(hid, width),) * (2 * end_count + 2),
        (place, delta, w_turned),
        scalars=1,
        scratch=[pltpu.VMEM((3, hid, (rows + 2) * width), F32)],
        flops=2 * gates * 9 * hid * cells,
        moved=8 * gates * cells,
        after=(packed,),
    )
    grad_flat, grad_ends, grad_sides = grad_parts[0], grad_parts[1:-2], grad_parts[-2:]
    grad_halo = exchange(
        grad_ends[0::2], grad_ends[1::2], *grad_sides, lat_devices, lon_devices
    )
    scaling = 1.0 / math.sqrt(float(lat_devices * lon_devices * capacity * TILE * TILE))
    shares, shared = call(
        lambda *refs: sum_kernel(scaling, span, state_rows, *refs),
        (shaped(lon_devices, share, lanes), shaped(8, 128, dtype=F32)),
        (place, incoming),
        scalars=1,
        moved=2 * gates * 3 * third,
        after=grad_halo,
    )
    owned = (wet_mask > 0) & (tile_owner == lon_index)
    arrived = jnp.any(owned.reshape(lon_devices, tile_cols), 1)
    order = jnp.arange(lon_devices, dtype=jnp.int32)
    rank = jnp.sum((arrived[:, None] & (order[:, None] < order[None, :])).astype(jnp.int32), 0)
    placed = arrived[None, :] & (rank[None, :] == jnp.arange(capacity, dtype=jnp.int32)[:, None])
    work = jnp.sum(jnp.where(placed, order[None, :], 0), 1)
    finished = call(
        finish_kernel,
        (
            shaped(hid, rows, width),
            shaped(hid * rows, width, dtype=F32),
            shaped(capacity, hid, TILE * TILE, dtype=F32),
            shaped(hid * rows, width, dtype=F32),
        ),
        (place, work, hidden_new, cell_back, incoming, grad_flat, *grad_halo),
        scalars=2,
        scratch=[pltpu.VMEM((hid * rows, width), F32)],
        moved=32 * hid * cells,
        after=(shared,),
    )
    gathered = lax.all_to_all(shares, "lon", 0, 0, tiled=True).reshape(3 * third, lanes)
    gathered, finished = lax.optimization_barrier((gathered, finished))
    hidden_next, cell_grad, cell_next, hidden_grad = finished
    gathered = (gathered,)
    if halves == 2:
        gathered += (lax.ppermute(gathered[0], "lat", swap),)
    weight_grad, bias_grad = call(
        lambda *refs: weights_kernel(span, *refs),
        (shaped(3 * span, gates, dtype=F32), shaped(1, gates, dtype=F32)),
        (place, *gathered),
        scalars=1,
        moved=6 * gates * 3 * third,
    )
    return (
        hidden_next,
        cell_next,
        hidden_grad.reshape(hid, rows, width),
        cell_grad.reshape(hid, rows, width),
        weight_grad.T,
        bias_grad.reshape(gates),
    )


def solution(mesh):
    return jax.shard_map(
        body,
        mesh=mesh,
        in_specs=(
            P(None, "lat", "lon"),
            P(None, "lat", "lon"),
            P(None, "lat", "lon"),
            P(None, "lat", "lon"),
            P(None, "lat", "lon"),
            P("lat", None),
            P("lat", None),
            P(),
            P(),
        ),
        out_specs=(
            P(None, "lat", "lon"),
            P(("lat", "lon"), None, None),
            P(None, "lat", "lon"),
            P(None, "lat", "lon"),
            P(),
            P(),
        ),
        check_vma=False,
    )
```

```python
import math

import jax
import jax.numpy as jnp
from jax import lax
from jax.experimental import pallas as pl
from jax.experimental.pallas import tpu as pltpu
from jax.sharding import PartitionSpec as P

TILE = 16
F32 = jnp.float32
BF16 = jnp.bfloat16
LIMIT = 48 * 1024 * 1024
SMEM = pl.BlockSpec(memory_space=pltpu.SMEM)
VMEM = pl.BlockSpec(memory_space=pltpu.VMEM)


def call(kernel, outs, operands, scalars=0, scratch=(), flops=0, moved=0, after=(), fetched=0):
    count = len(operands)
    kept = count - fetched
    total = count + len(after)

    def run(*refs):
        if not fetched:
            kernel(*refs[:count], *refs[total:])
            return
        *rest, semaphores = refs[total:]
        buffers = rest[len(rest) - fetched :]
        copies = [
            pltpu.make_async_copy(source, target, semaphores.at[index])
            for index, (source, target) in enumerate(zip(refs[kept:count], buffers))
        ]
        for copy in copies:
            copy.start()
        waits = [copy.wait for copy in copies]
        kernel(waits, *refs[:kept], *buffers, *rest[: len(rest) - fetched])

    scratch = list(scratch)
    operands = list(operands)
    for index in range(kept, count):
        operands[index] = pltpu.with_memory_space_constraint(operands[index], pltpu.HBM)
    if fetched:
        scratch += [pltpu.VMEM(leaf.shape, leaf.dtype) for leaf in operands[kept:]]
        scratch.append(pltpu.SemaphoreType.DMA((fetched,)))

    return pl.pallas_call(
        run,
        out_shape=outs,
        in_specs=[SMEM] * scalars
        + [VMEM] * (kept - scalars)
        + [pl.BlockSpec(memory_space=pltpu.HBM)] * fetched
        + [VMEM] * len(after),
        out_specs=jax.tree.map(lambda _: VMEM, outs),
        scratch_shapes=scratch,
        compiler_params=pltpu.CompilerParams(vmem_limit_bytes=LIMIT),
        cost_estimate=pl.CostEstimate(flops=flops, bytes_accessed=moved, transcendentals=0),
    )(*operands, *after)


def lane_index(shape):
    return lax.broadcasted_iota(jnp.int32, shape, 1)


def sigmoid(values):
    return 0.5 * jnp.tanh(0.5 * values) + 0.5


def edges_kernel(waits, place_ref, forcing_ref, hidden_ref, wide_ref, *row_refs):
    inp, rows, width = forcing_ref.shape
    channels = inp + hidden_ref.shape[0]
    for wait in waits:
        wait()
    wide_ref[: inp * rows] = forcing_ref[...].astype(F32).reshape(inp * rows, width)
    wide_ref[inp * rows :] = hidden_ref[...].astype(F32).reshape((channels - inp) * rows, width)
    ends = [wide_ref[pl.ds(row, channels, stride=rows), :] for row in (0, rows - 1)]
    if len(row_refs) == 1:
        row_refs[0][...] = jnp.where(place_ref[0] == 0, ends[1], ends[0]).astype(BF16)
    else:
        for ref, end in zip(row_refs, ends):
            ref[...] = end.astype(BF16)


def columns_kernel(wide_ref, flat_ref, left_ref, right_ref):
    channels, width = left_ref.shape
    rows = wide_ref.shape[0] // channels
    lane = lane_index((channels, width))
    left = jnp.zeros((channels, width), F32)
    right = jnp.zeros((channels, width), F32)
    for row in range(rows):
        slab = wide_ref[pl.ds(row, channels, stride=rows), :]
        flat_ref[:, row * width : (row + 1) * width] = slab.astype(BF16)
        left = jnp.where(lane == row, slab[:, :1], left)
        right = jnp.where(lane == row, slab[:, width - 1 :], right)
    left_ref[...] = left.astype(BF16)
    right_ref[...] = right.astype(BF16)


def flatten_kernel(
    waits,
    b_ref,
    wt_ref,
    cell_ref,
    hcot_ref,
    ccot_ref,
    cell_out,
    hcot_out,
    ccot_out,
    w_ref,
    bias_ref,
    wide_ref,
):
    hid, rows, width = cell_ref.shape
    gates = wt_ref.shape[1]
    span = wt_ref.shape[0] // 3
    third = w_ref.shape[1] // 3
    waits[0]()
    bias_ref[...] = jnp.broadcast_to(b_ref[...], (bias_ref.shape[1], gates)).T
    waits[1]()
    blank = jnp.zeros((third - span, gates), F32)
    for index in range(3):
        block = wt_ref[index * span : (index + 1) * span].astype(F32)
        w_ref[:, index * third : (index + 1) * third] = (
            jnp.concatenate([block, blank], 0).T.astype(BF16)
        )
    for wait, source, target in zip(
        waits[2:], (cell_ref, hcot_ref, ccot_ref), (cell_out, hcot_out, ccot_out)
    ):
        wait()
        wide_ref[...] = source[...].astype(F32).reshape(hid * rows, width)
        for row in range(rows):
            target[:, row * width : (row + 1) * width] = wide_ref[
                pl.ds(row, hid, stride=rows), :
            ].astype(BF16)


def corners_kernel(rows, up_ref, down_ref, left_ref, right_ref, left_out, right_out):
    lane = lane_index(left_ref.shape)
    width = up_ref.shape[1]
    up = up_ref[...].astype(F32)
    down = down_ref[...].astype(F32)
    for column, source, target in ((0, left_ref, left_out), (width - 1, right_ref, right_out)):
        values = source[...].astype(F32)
        values = jnp.where(lane == rows, up[:, column : column + 1], values)
        values = jnp.where(lane == rows + 1, down[:, column : column + 1], values)
        target[...] = values.astype(BF16)


def step_kernel(
    place_ref,
    wet_ref,
    owner_ref,
    flat_ref,
    up_ref,
    down_ref,
    left_ref,
    right_ref,
    cell_ref,
    hcot_ref,
    ccot_ref,
    w_ref,
    b_ref,
    hidden_new_ref,
    cell_back_ref,
    tiles_ref,
    *rest,
):
    weight_refs, (delta_ref, taps_ref) = rest[:-2], rest[-2:]
    channels = flat_ref.shape[0]
    hid = cell_ref.shape[0]
    gates = w_ref.shape[0]
    width = up_ref.shape[1]
    rows = flat_ref.shape[1] // width
    tile_cols = width // TILE
    span = 3 * channels
    first_tile = place_ref[1] * tile_cols
    lane = lane_index((channels, width))

    def put(row, slab, before, after):
        lanes = slice(row * width, (row + 1) * width)
        shifted = jnp.where(lane == 0, before, pltpu.roll(slab, 1, 1))
        taps_ref[0:channels, lanes] = shifted.astype(BF16)
        taps_ref[channels : 2 * channels, lanes] = slab.astype(BF16)
        shifted = jnp.where(lane == width - 1, after, pltpu.roll(slab, width - 1, 1))
        taps_ref[2 * channels : span, lanes] = shifted.astype(BF16)

    left = left_ref[...].astype(F32)
    right = right_ref[...].astype(F32)
    for end, flag, ref in ((0, place_ref[2], up_ref), (1, place_ref[3], down_ref)):
        corner = slice(rows + end, rows + end + 1)
        slab, before, after = [
            jnp.where(flag == 1, values, 0.0)
            for values in (ref[...].astype(F32), left[:, corner], right[:, corner])
        ]
        put(end * (rows + 1), slab, before, after)
    for row in range(rows):
        slab = flat_ref[:, row * width : (row + 1) * width].astype(F32)
        put(row + 1, slab, left[:, row : row + 1], right[:, row : row + 1])
    extra = taps_ref.shape[0] - span
    ones = lax.broadcasted_iota(jnp.int32, (extra, taps_ref.shape[1]), 0) == 0
    taps_ref[span:] = jnp.where(ones, 1.0, 0.0).astype(BF16)

    live = jnp.zeros((1, width), F32)
    live_lane = lane_index((1, width)) // TILE
    for tile in range(tile_cols):
        wet = (wet_ref[0, first_tile + tile] > 0).astype(F32)
        live = jnp.where(live_lane == tile, wet, live)
    step = 2 if rows % 2 == 0 else 1
    chunk = step * width
    live = jnp.concatenate([live] * step, 1)
    third = w_ref.shape[1] // 3
    blank = jnp.zeros((gates, 2 * width), BF16)
    delta_ref[:, : 2 * width] = blank
    delta_ref[:, (rows + 2) * width :] = blank
    bias = jnp.concatenate([b_ref[...]] * step, 1)
    group = 128 // TILE
    states = []
    for start in range(0, rows, step):
        lows = [(start + row_off) * width for row_off in range(3)]
        stacked = jnp.concatenate([taps_ref[:, low : low + chunk] for low in lows], 0)
        pre = bias + jnp.dot(w_ref[...], stacked, preferred_element_type=F32)
        gate_in = sigmoid(pre[:hid])
        gate_forget = sigmoid(pre[hid : 2 * hid])
        gate_out = sigmoid(pre[2 * hid : 3 * hid])
        candidate = jnp.tanh(pre[3 * hid :])
        lanes = slice(start * width, start * width + chunk)
        cell_in = cell_ref[:, lanes].astype(F32)
        cell_new = gate_forget * cell_in + gate_in * candidate
        squash = jnp.tanh(cell_new)
        hidden_new = live * gate_out * squash
        back_h = live * hcot_ref[:, lanes].astype(F32)
        back_c = live * ccot_ref[:, lanes].astype(F32) + back_h * gate_out * (1.0 - squash * squash)
        cell_back = back_c * gate_forget
        carried = back_c * gate_in
        terms = (
            carried * candidate * (1.0 - gate_in),
            cell_back * cell_in * (1.0 - gate_forget),
            back_h * squash * gate_out * (1.0 - gate_out),
            carried * (1.0 - candidate * candidate),
        )
        low = (start + 2) * width
        for index, term in enumerate(terms):
            delta_ref[index * hid : (index + 1) * hid, low : low + chunk] = term.astype(BF16)
        hidden_new_ref[:, lanes] = hidden_new.astype(BF16)
        cell_back_ref[:, lanes] = cell_back
        for part in range(step):
            piece = slice(part * width, (part + 1) * width)
            states.append(cell_new[:, piece])
        if len(states) == group:
            block_of = lane_index((hid, width)) // TILE
            half = (start + step) // group - 1
            stride = group // 2
            while stride:
                upper = (block_of & stride) != 0
                mixed = list(states)
                for low_index in range(group):
                    if low_index & stride == 0:
                        first, second = states[low_index], states[low_index + stride]
                        mixed[low_index] = jnp.where(
                            upper, pltpu.roll(second, stride * TILE, 1), first
                        )
                        mixed[low_index + stride] = jnp.where(
                            upper, second, pltpu.roll(first, width - stride * TILE, 1)
                        )
                states = mixed
                stride //= 2
            for tile in range(tile_cols):
                tiles_ref[tile, :, half * 128 : (half + 1) * 128] = states[tile].astype(BF16)
            states = []
    delta = delta_ref[:, 2 * width : (rows + 2) * width]
    for row_off in range(3):
        part = lax.dot_general(
            taps_ref[:, row_off * width : (row_off + rows) * width],
            delta,
            (((1,), (1,)), ((), ())),
            preferred_element_type=F32,
        )
        place = slice(row_off * third, (row_off + 1) * third)
        if len(weight_refs) == 1:
            weight_refs[0][place] = part
        else:
            low, high = part[:, : gates // 2], part[:, gates // 2 :]
            weight_refs[0][place] = jnp.where(place_ref[0] == 0, low, high)
            weight_refs[1][place] = jnp.where(place_ref[0] == 0, high, low)


def spread_kernel(place_ref, delta_ref, wt_ref, grad_ref, *rest):
    row_refs, (left_ref, right_ref, side_ref) = rest[:-3], rest[-3:]
    hid = grad_ref.shape[0]
    width = left_ref.shape[1]
    rows = grad_ref.shape[1] // width
    channels = wt_ref.shape[0] // 9
    total = [None] * 3
    for col_off in range(3):
        for row_off in range(3):
            first = (row_off * 3 + col_off + 1) * channels - hid
            low = (2 - row_off) * width
            term = jnp.dot(
                wt_ref[first : first + hid],
                delta_ref[:, low : low + (rows + 2) * width],
                preferred_element_type=F32,
            )
            total[col_off] = term if row_off == 0 else total[col_off] + term
        side_ref[col_off] = total[col_off]
    lane = lane_index((hid, width))
    left = jnp.zeros((hid, width), F32)
    right = jnp.zeros((hid, width), F32)
    ends = []
    for row in range(rows + 2):
        lanes = slice(row * width, (row + 1) * width)
        before = side_ref[0, :, lanes]
        after = side_ref[2, :, lanes]
        slab = (
            side_ref[1, :, lanes]
            + jnp.where(lane == width - 1, 0.0, pltpu.roll(before, width - 1, 1))
            + jnp.where(lane == 0, 0.0, pltpu.roll(after, 1, 1))
        )
        if row in (0, rows + 1):
            corners = jnp.where(lane == 0, before[:, :1], 0.0)
            corners = jnp.where(lane == width - 1, after[:, width - 1 :], corners)
            ends.append((slab, corners))
        else:
            grad_ref[:, (row - 1) * width : row * width] = slab
            left = jnp.where(lane == row - 1, before[:, :1], left)
            right = jnp.where(lane == row - 1, after[:, width - 1 :], right)
    left_ref[...] = left.astype(BF16)
    right_ref[...] = right.astype(BF16)
    if len(row_refs) == 2:
        for index in range(2):
            row_refs[index][...] = jnp.where(
                place_ref[0] == 0, ends[1][index], ends[0][index]
            ).astype(BF16)
    else:
        for end in range(2):
            for index in range(2):
                row_refs[2 * end + index][...] = ends[end][index].astype(BF16)


def finish_kernel(
    place_ref,
    work_ref,
    hidden_new_ref,
    cell_back_ref,
    arrived_ref,
    grad_ref,
    up_ref,
    down_ref,
    up_left_ref,
    up_right_ref,
    down_left_ref,
    down_right_ref,
    left_ref,
    right_ref,
    hidden_next_ref,
    cell_grad_ref,
    cell_next_ref,
    hidden_grad_ref,
    wide_ref,
):
    hid = grad_ref.shape[0]
    width = up_ref.shape[1]
    rows = grad_ref.shape[1] // width
    lane = lane_index((hid, width))
    left = left_ref[...].astype(F32)
    right = right_ref[...].astype(F32)
    ends = {}
    for row, flag, refs in (
        (0, place_ref[2], (up_ref, up_left_ref, up_right_ref)),
        (rows - 1, place_ref[3], (down_ref, down_left_ref, down_right_ref)),
    ):
        slab, before, after = [ref[...].astype(F32) for ref in refs]
        slab = slab + jnp.where(lane == 0, before[:, width - 1 :], 0.0)
        slab = slab + jnp.where(lane == width - 1, after[:, :1], 0.0)
        ends[row] = jnp.where(flag == 1, slab, 0.0)
    for row in range(rows):
        lanes = slice(row * width, (row + 1) * width)
        slab = grad_ref[:, lanes]
        slab = slab + jnp.where(lane == 0, left[:, row : row + 1], 0.0)
        slab = slab + jnp.where(lane == width - 1, right[:, row : row + 1], 0.0)
        if row in ends:
            slab = slab + ends[row]
        hidden_grad_ref[pl.ds(row, hid, stride=rows), :] = slab
        cell_grad_ref[pl.ds(row, hid, stride=rows), :] = cell_back_ref[:, lanes]
        wide_ref[pl.ds(row, hid, stride=rows), :] = hidden_new_ref[:, lanes].astype(F32)
    hidden_next_ref[...] = wide_ref[...].reshape(hid, rows, width).astype(BF16)
    pieces = arrived_ref.shape[2]
    for index in range(cell_next_ref.shape[0]):
        for piece in range(cell_next_ref.shape[2] // pieces):
            cell_next_ref[index, :, piece * pieces : (piece + 1) * pieces] = arrived_ref[
                work_ref[index], piece * hid : (piece + 1) * hid
            ].astype(F32)


def split_bias(block, row):
    index = lax.broadcasted_iota(jnp.int32, block.shape, 0)
    rest = pltpu.roll(block - block.astype(BF16).astype(F32), 1, 0)
    return jnp.where(index == row + 1, rest, block)


def slots_kernel(place_ref, wet_ref, owner_ref, tiles_ref, out_ref):
    tile_cols, hid, cells = tiles_ref.shape
    slots, _, lanes = out_ref.shape
    out_ref[...] = jnp.zeros(out_ref.shape, BF16)
    for tile in range(tile_cols):
        index = place_ref[1] * tile_cols + tile

        @pl.when(wet_ref[0, index] > 0)
        def _():
            for piece in range(cells // lanes):
                out_ref[owner_ref[0, index], piece * hid : (piece + 1) * hid] = tiles_ref[
                    tile, :, piece * lanes : (piece + 1) * lanes
                ]


def pack_kernel(span, count, *refs):
    slots_ref, out_ref, token_ref, share_ref, semaphore = refs[count:]
    token_ref[...] = jnp.zeros(token_ref.shape, F32)
    slots, share, _ = share_ref.shape
    third = refs[0].shape[0] // 3
    total = refs[0][...]
    for ref in refs[1:count]:
        total = total + ref[...]
    total = jnp.concatenate([split_bias(total[:third], span), total[third:]], 0)
    for slot in range(slots):
        share_ref[slot] = total[slot * share : (slot + 1) * share].astype(BF16)
    state_rows = out_ref.shape[1] - share
    copy = pltpu.make_async_copy(share_ref, out_ref.at[:, pl.ds(state_rows, share)], semaphore)
    copy.start()
    copy.wait()


def sum_kernel(scaling, span, state_rows, place_ref, parts_ref, out_ref, token_ref):
    token_ref[...] = jnp.zeros(token_ref.shape, F32)
    total = parts_ref[0, state_rows:].astype(F32)
    for index in range(1, parts_ref.shape[0]):
        total = total + parts_ref[index, state_rows:].astype(F32)
    total = total * scaling
    share = total.shape[0]
    row = span % share
    index = lax.broadcasted_iota(jnp.int32, total.shape, 0)
    whole = jnp.where(index == row, total + pltpu.roll(total, share - 1, 0), total)
    total = jnp.where(place_ref[1] == span // share, split_bias(whole, row), total)
    for index in range(out_ref.shape[0]):
        out_ref[index] = total.astype(BF16)


def weights_kernel(span, place_ref, *refs):
    *parts, weight_ref, bias_ref = refs
    third = parts[0].shape[0] // 3
    half = parts[0].shape[1]
    for side in range(len(parts)):
        if len(parts) == 1:
            pick = parts[0][...]
        else:
            pick = jnp.where(place_ref[0] == side, parts[0][...], parts[1][...])
        pick = pick.astype(F32)
        lanes = slice(side * half, (side + 1) * half)
        for index in range(3):
            weight_ref[index * span : (index + 1) * span, lanes] = pick[
                index * third : index * third + span
            ]
        bias_ref[:, lanes] = pick[span : span + 1] + pick[span + 1 : span + 2]


def moved(values, lat_step, lon_step, lat_devices, lon_devices):
    pairs = []
    for lat in range(lat_devices):
        for lon in range(lon_devices):
            to_lat = lat + lat_step
            if lat_step and lat_devices == 2:
                to_lat = 1 - lat
            if 0 <= to_lat < lat_devices:
                to = to_lat * lon_devices + (lon + lon_step) % lon_devices
                pairs.append((lat * lon_devices + lon, to))
    return lax.ppermute(values, ("lat", "lon"), pairs)


def exchange(ends, corners, left, right, lat_devices, lon_devices):
    def go(values, lat_step, lon_step):
        return moved(values, lat_step, lon_step, lat_devices, lon_devices)

    from_left, from_right = go(right, 0, 1), go(left, 0, -1)
    if lat_devices == 2:
        row = go(ends[0], 1, 0)
        row_left, row_right = go(corners[0], 1, 1), go(corners[0], 1, -1)
        return (row, row, row_left, row_right, row_left, row_right, from_left, from_right)
    return (
        go(ends[1], 1, 0),
        go(ends[0], -1, 0),
        go(corners[1], 1, 1),
        go(corners[1], 1, -1),
        go(corners[0], -1, 1),
        go(corners[0], -1, -1),
        from_left,
        from_right,
    )


def body(forcing, hidden, cell, grad_hidden, grad_cell, wet_mask, tile_owner, w_gates, b_gates):
    lat_index = lax.axis_index("lat")
    lon_index = lax.axis_index("lon")
    lat_devices = lax.axis_size("lat")
    lon_devices = lax.axis_size("lon")
    inp, rows, width = forcing.shape
    hid = hidden.shape[0]
    channels = inp + hid
    gates = w_gates.shape[0]
    span = 3 * channels
    third = (span + 128) // 128 * 128
    cells = rows * width
    tile_cols = width // TILE
    capacity = tile_cols // 2
    place = jnp.stack(
        [
            lat_index,
            lon_index,
            (lat_index > 0).astype(jnp.int32),
            (lat_index < lat_devices - 1).astype(jnp.int32),
        ]
    ).astype(jnp.int32)

    def shaped(*shape, dtype=BF16):
        return jax.ShapeDtypeStruct(shape, dtype)

    end_count = 1 if lat_devices == 2 else 2
    wide, *ends = call(
        edges_kernel,
        (shaped(channels * rows, width, dtype=F32),) + (shaped(channels, width),) * end_count,
        (place, forcing, hidden),
        scalars=1,
        moved=4 * channels * cells,
        fetched=2,
    )
    flat, left, right = call(
        columns_kernel,
        (shaped(channels, cells),) + (shaped(channels, width),) * 2,
        (wide,),
        moved=6 * channels * cells,
    )
    if lat_devices == 2:
        up = down = moved(ends[0], 1, 0, lat_devices, lon_devices)
    else:
        up = moved(ends[1], 1, 0, lat_devices, lon_devices)
        down = moved(ends[0], -1, 0, lat_devices, lon_devices)
    left, right = call(
        lambda *refs: corners_kernel(rows, *refs),
        (shaped(channels, width),) * 2,
        (up, down, left, right),
        moved=8 * channels * width,
    )
    halo = (
        up,
        down,
        moved(right, 0, 1, lat_devices, lon_devices),
        moved(left, 0, -1, lat_devices, lon_devices),
    )
    w_turned = w_gates.T
    cell_flat, hcot_flat, ccot_flat, w_rows, bias = call(
        flatten_kernel,
        (shaped(hid, cells),) * 3
        + (shaped(gates, 3 * third), shaped(gates, width, dtype=F32)),
        (b_gates.reshape(1, gates), w_turned, cell, grad_hidden, grad_cell),
        scratch=[pltpu.VMEM((hid * rows, width), F32)],
        moved=12 * hid * cells,
        fetched=5,
    )
    halves = 2 if lat_devices == 2 else 1
    lanes = gates // halves
    hidden_new, cell_back, tiles, *weight_parts, delta = call(
        step_kernel,
        (
            shaped(hid, cells),
            shaped(hid, cells, dtype=F32),
            shaped(tile_cols, hid, TILE * TILE),
        )
        + (shaped(3 * third, lanes, dtype=F32),) * halves
        + (shaped(gates, (rows + 4) * width),),
        (place, wet_mask, tile_owner, flat, *halo)
        + (cell_flat, hcot_flat, ccot_flat, w_rows, bias),
        scalars=3,
        scratch=[pltpu.VMEM((third, (rows + 2) * width), BF16)],
        flops=4 * gates * 3 * span * cells,
        moved=16 * hid * cells,
    )
    swap = [(0, 1), (1, 0)]
    if halves == 2:
        weight_parts = (weight_parts[0], lax.ppermute(weight_parts[1], "lat", swap))
    else:
        weight_parts = (lax.psum(weight_parts[0], "lat"),)
    state_rows = hid * TILE * TILE // lanes
    share = 3 * third // lon_devices
    slots = call(
        slots_kernel,
        shaped(lon_devices, state_rows + share, lanes),
        (place, wet_mask, tile_owner, tiles),
        scalars=3,
        moved=4 * lon_devices * hid * TILE * TILE,
    )
    anywhere = pl.BlockSpec(memory_space=pl.ANY)
    count = len(weight_parts)
    outgoing, packed = pl.pallas_call(
        lambda *refs: pack_kernel(span, count, *refs),
        out_shape=(shaped(*slots.shape), shaped(8, 128, dtype=F32)),
        in_specs=[VMEM] * count + [anywhere],
        out_specs=(anywhere, VMEM),
        scratch_shapes=[
            pltpu.VMEM((lon_devices, share, lanes), BF16),
            pltpu.SemaphoreType.DMA(()),
        ],
        input_output_aliases={count: 0},
        compiler_params=pltpu.CompilerParams(vmem_limit_bytes=LIMIT),
        cost_estimate=pl.CostEstimate(
            flops=0, bytes_accessed=8 * gates * 3 * third, transcendentals=0
        ),
    )(*weight_parts, slots)
    incoming = lax.all_to_all(outgoing, "lon", 0, 0, tiled=True)
    grad_parts = call(
        spread_kernel,
        (shaped(hid, cells, dtype=F32),) + (shaped(hid, width),) * (2 * end_count + 2),
        (place, delta, w_turned),
        scalars=1,
        scratch=[pltpu.VMEM((3, hid, (rows + 2) * width), F32)],
        flops=2 * gates * 9 * hid * cells,
        moved=8 * gates * cells,
        after=(packed,),
    )
    grad_flat, grad_ends, grad_sides = grad_parts[0], grad_parts[1:-2], grad_parts[-2:]
    grad_halo = exchange(
        grad_ends[0::2], grad_ends[1::2], *grad_sides, lat_devices, lon_devices
    )
    scaling = 1.0 / math.sqrt(float(lat_devices * lon_devices * capacity * TILE * TILE))
    shares, shared = call(
        lambda *refs: sum_kernel(scaling, span, state_rows, *refs),
        (shaped(lon_devices, share, lanes), shaped(8, 128, dtype=F32)),
        (place, incoming),
        scalars=1,
        moved=2 * gates * 3 * third,
        after=grad_halo[:-2],
    )
    owned = (wet_mask > 0) & (tile_owner == lon_index)
    arrived = jnp.any(owned.reshape(lon_devices, tile_cols), 1)
    order = jnp.arange(lon_devices, dtype=jnp.int32)
    rank = jnp.sum((arrived[:, None] & (order[:, None] < order[None, :])).astype(jnp.int32), 0)
    placed = arrived[None, :] & (rank[None, :] == jnp.arange(capacity, dtype=jnp.int32)[:, None])
    work = jnp.sum(jnp.where(placed, order[None, :], 0), 1)
    finished = call(
        finish_kernel,
        (
            shaped(hid, rows, width),
            shaped(hid * rows, width, dtype=F32),
            shaped(capacity, hid, TILE * TILE, dtype=F32),
            shaped(hid * rows, width, dtype=F32),
        ),
        (place, work, hidden_new, cell_back, incoming, grad_flat, *grad_halo),
        scalars=2,
        scratch=[pltpu.VMEM((hid * rows, width), F32)],
        moved=32 * hid * cells,
        after=(shared,),
    )
    gathered = lax.all_to_all(shares, "lon", 0, 0, tiled=True).reshape(3 * third, lanes)
    gathered, finished = lax.optimization_barrier((gathered, finished))
    hidden_next, cell_grad, cell_next, hidden_grad = finished
    gathered = (gathered,)
    if halves == 2:
        gathered += (lax.ppermute(gathered[0], "lat", swap),)
    weight_grad, bias_grad = call(
        lambda *refs: weights_kernel(span, *refs),
        (shaped(3 * span, gates, dtype=F32), shaped(1, gates, dtype=F32)),
        (place, *gathered),
        scalars=1,
        moved=6 * gates * 3 * third,
    )
    return (
        hidden_next,
        cell_next,
        hidden_grad.reshape(hid, rows, width),
        cell_grad.reshape(hid, rows, width),
        weight_grad.T,
        bias_grad.reshape(gates),
    )


def solution(mesh):
    return jax.shard_map(
        body,
        mesh=mesh,
        in_specs=(
            P(None, "lat", "lon"),
            P(None, "lat", "lon"),
            P(None, "lat", "lon"),
            P(None, "lat", "lon"),
            P(None, "lat", "lon"),
            P("lat", None),
            P("lat", None),
            P(),
            P(),
        ),
        out_specs=(
            P(None, "lat", "lon"),
            P(("lat", "lon"), None, None),
            P(None, "lat", "lon"),
            P(None, "lat", "lon"),
            P(),
            P(),
        ),
        check_vma=False,
    )
```
